32 devices in a mesh: seq: 16 (over z, x, core), dp: 2 (over y).
Axes of the slice: x: 2, y: 2, z: 4, core: 2. Of those that a mesh axis runs over, the one named last changes fastest.
Arguments:
- queries: bfloat16 [2, 2048, 4096], P('dp', 'seq'), may hold values from -4.5 to 4.5
- context: bfloat16 [2, 2048, 1024], P('dp', 'seq'), may hold values from -4.5 to 4.5
- segment_start: int32 [2, 2048], P('dp', 'seq'), may hold values from 0 to 2047, as said below
- memory: bfloat16 [2, 16, 64, 1024], P('dp', 'seq'), may hold values from -4.5 to 4.5
- image_offset: int32 [2, 16], P('dp', 'seq'), may hold values from 0 to 128, as said below
- cross_gate: float32 [32], replicated, may hold values from -1.5 to 1.5
- out_grad: bfloat16 [2, 2048, 4096], P('dp', 'seq'), may hold values from -6 to 6
Outputs:
- query_grad: bfloat16 [2, 2048, 4096], P('dp', 'seq')
- context_grad: bfloat16 [2, 2048, 1024], P('dp', 'seq')
- memory_grad: bfloat16 [2, 16, 64, 1024], P('dp', 'seq')
- gate_grad: float32 [32], replicated
The draws below stay inside these ranges and needn't reach their ends.
Inputs may be any that keep to these rules, and one draw needn't show every extreme that they name: `segment_start`: position of the first token of each token's segment: non-decreasing, equal to the position itself at a segment's first token; positions 0 and 2047 begin segments. `image_offset`: in each aligned block of 4 shards exactly one shard owns an image (offset below 128); every token that reads an image reads one owned at most 7 shards before its own, and that distance is reached in every draw.
All inputs are finite; a program needn't handle non-finite values.
Results may differ from the reference program's by a relative error of at most 0.012.
The reference program's roundings to bfloat16 on the way (of `narrow_weights`, `self_out`, `cross_narrow`, `grad_cross`, `grad_scores` and `grad_self`) count: a program that leaves them out, or rounds other values in their place, can miss the bound.
Values may be sent and summed in bfloat16 or wider, within the bound.
No kernel may reach another device: no remote copies, remote signals or barrier semaphores. Data moves between devices by JAX's collectives and lax.ppermute only.
A program may use at most 128 MiB of HBM per device.

```python
import math
import jax
import jax.numpy as jnp
from jax import lax

HEADS = 32
KV_HEADS = 4
HEAD_DIM = 128
TOK_DEV = 128
IMG_TOK = 64
GAP = 4
WINDOW = 64
SHARDS = 16
SEQ = 2048
DOCS = 2


def base_law(key, shape):
    values = jnp.clip(jax.random.normal(key, shape, jnp.float32), -4.5, 4.5)
    return values


def draw_queries(key, part):
    values = base_law(jax.random.fold_in(key, 1), (DOCS, SEQ, HEADS * HEAD_DIM))
    return values.astype(jnp.bfloat16)


def draw_context(key, part):
    values = base_law(jax.random.fold_in(key, 2), (DOCS, SEQ, 2 * KV_HEADS * HEAD_DIM))
    return values.astype(jnp.bfloat16)


def draw_memory(key, part):
    values = base_law(jax.random.fold_in(key, 3), (DOCS, SHARDS, IMG_TOK, 2 * KV_HEADS * HEAD_DIM))
    return values.astype(jnp.bfloat16)


def draw_image_offset(key, part):
    blocks = SHARDS // GAP
    middle = SHARDS // 2 // GAP
    block_ids = jnp.arange(blocks, dtype=jnp.int32)
    slot = jax.random.randint(jax.random.fold_in(key, 21), (DOCS, blocks), 0, GAP)
    last_slot = (block_ids == 1) | (block_ids == middle - 1)
    first_slot = (block_ids == 0) | (block_ids == middle)
    slot = jnp.where(first_slot[None, :], 0, jnp.where(last_slot[None, :], GAP - 1, slot))
    first = jax.random.randint(jax.random.fold_in(key, 22), (DOCS, blocks), 0, TOK_DEV)
    later_first = jax.random.randint(jax.random.fold_in(key, 23), (DOCS, blocks), 1, TOK_DEV)
    first = jnp.where(((block_ids == 1) | (block_ids == middle))[None, :], later_first, first)
    shard_ids = jnp.arange(SHARDS, dtype=jnp.int32)
    block_of = shard_ids // GAP
    within = shard_ids % GAP
    owns = slot[:, block_of] == within[None, :]
    return jnp.where(owns, first[:, block_of], TOK_DEV).astype(jnp.int32)


def draw_segment_start(key, part):
    positions = jnp.arange(SEQ, dtype=jnp.int32)
    starts_here = jax.random.randint(jax.random.fold_in(key, 31), (DOCS, SEQ), 0, 160) == 0
    starts_here = starts_here | (positions == 0)[None, :] | (positions == SEQ - 1)[None, :]
    return lax.cummax(jnp.where(starts_here, positions[None, :], 0), axis=1).astype(jnp.int32)


def steps_of(stream_key, extent, pieces, low, top_value):
    def one(dim, blocks):
        heights = jax.random.uniform(jax.random.fold_in(jax.random.fold_in(stream_key, 6), dim), (blocks,), jnp.float32, low / len(pieces), top_value / len(pieces))
        return jnp.repeat(jnp.exp(heights), extent[dim] // blocks).reshape((-1,) + (1,) * (len(extent) - dim - 1))

    loudness = one(*pieces[0])
    for cut in pieces[1:]:
        loudness = loudness * one(*cut)
    return loudness


def noise(own_key, extent, scale, most, shards=(), held_as=jnp.bfloat16):
    gain = steps_of(own_key, extent, shards, -0.22, 0.18) if shards else 1.0
    drawn = jax.random.normal(own_key, extent, jnp.float32) * scale * gain
    return jnp.minimum(jnp.maximum(drawn, -most), most).astype(held_as)


def setup_inputs(seed: int = 0) -> dict:
    splits = jax.random.split(jax.random.key(seed), 8)
    return {
        "queries": draw_queries(jax.random.fold_in(splits[7], 71), 0),
        "context": draw_context(jax.random.fold_in(splits[7], 71), 0),
        "segment_start": draw_segment_start(jax.random.fold_in(splits[7], 71), 0),
        "memory": draw_memory(jax.random.fold_in(splits[7], 71), 0),
        "image_offset": draw_image_offset(jax.random.fold_in(splits[7], 71), 0),
        "cross_gate": jnp.clip(jax.random.uniform(splits[5], (HEADS,), jnp.float32, -1.5, 1.5), -1.5, 1.5),
        "out_grad": noise(splits[6], (DOCS, SEQ, HEADS * HEAD_DIM), 1.0, 6.0, ((0, 2), (1, 16))),
    }


def rounded(values):
    return lax.optimization_barrier(values.astype(jnp.bfloat16)).astype(jnp.float32)

def masked_softmax(scores, allowed):
    scores = jnp.where(allowed, scores, -1e+30)
    row_top = lax.optimization_barrier(jnp.max(scores, axis=-1, keepdims=True))
    powers = jnp.exp(scores - row_top)
    return powers / lax.optimization_barrier(jnp.sum(powers, axis=-1, keepdims=True))

def attend(query_heads, key_part, value_part, allowed):
    score_scale = 1.0 / math.sqrt(HEAD_DIM)
    scores = jnp.einsum('tgrd,kgd->grtk', query_heads, key_part) * score_scale
    weights = masked_softmax(scores, allowed[None, None])
    narrow_weights = rounded(weights)
    mixed = jnp.einsum('grtk,kgd->tgrd', narrow_weights, value_part)
    return (weights, narrow_weights, mixed)

def attend_back(grad_mixed, query_heads, key_part, value_part, weights, narrow_weights):
    score_scale = 1.0 / math.sqrt(HEAD_DIM)
    grad_weights = jnp.einsum('tgrd,kgd->grtk', grad_mixed, value_part)
    row_delta = lax.optimization_barrier(jnp.sum(weights * grad_weights, axis=-1, keepdims=True))
    grad_scores = rounded(weights * (grad_weights - row_delta))
    grad_queries = jnp.einsum('grtk,kgd->tgrd', grad_scores, key_part) * score_scale
    grad_keys = jnp.einsum('grtk,tgrd->kgd', grad_scores, query_heads) * score_scale
    grad_values = jnp.einsum('grtk,tgrd->kgd', narrow_weights, grad_mixed)
    return (grad_queries, grad_keys, grad_values)

def split_pair(joined):
    key_width = KV_HEADS * HEAD_DIM
    key_part = joined[:, :key_width].reshape(-1, KV_HEADS, HEAD_DIM)
    value_part = joined[:, key_width:].reshape(-1, KV_HEADS, HEAD_DIM)
    return (key_part, value_part)

def self_mask(shard_index, tok_rows, segment_row):
    query_pos = shard_index * tok_rows + jnp.arange(tok_rows, dtype=jnp.int32)
    key_pos = shard_index * tok_rows - WINDOW + jnp.arange(WINDOW + tok_rows, dtype=jnp.int32)
    return (key_pos[None, :] <= query_pos[:, None]) & (key_pos[None, :] >= query_pos[:, None] - WINDOW) & (key_pos[None, :] >= segment_row[:, None])

def cross_mask(tok_rows, offset, is_owner, has_prev):
    local = jnp.arange(tok_rows, dtype=jnp.int32)
    use_own = is_owner & (local >= offset)
    use_prev = jnp.logical_not(use_own) & has_prev
    columns = jnp.arange(2 * IMG_TOK, dtype=jnp.int32)
    allowed = jnp.where(columns[None, :] < IMG_TOK, use_prev[:, None], use_own[:, None])
    return (allowed, (use_own | use_prev).astype(jnp.float32))

def shard_pass(query_rows, joined_keys, joined_memory, allowed, cross_allowed, has_image, cross_gate, grad_rows):
    tok_rows = query_rows.shape[0]
    key_rows = joined_keys.shape[0]
    repeat = HEADS // KV_HEADS
    query_heads = query_rows.astype(jnp.float32).reshape(tok_rows, KV_HEADS, repeat, HEAD_DIM)
    key_part, value_part = split_pair(joined_keys.astype(jnp.float32))
    weights, narrow_weights, mixed = attend(query_heads, key_part, value_part, allowed)
    self_out = rounded(mixed)
    memory_keys, memory_values = split_pair(joined_memory.astype(jnp.float32))
    cross_weights, cross_narrow, cross_mixed = attend(self_out, memory_keys, memory_values, cross_allowed)
    image_mask = has_image[:, None, None, None]
    cross_mixed = cross_mixed * image_mask
    gate_tanh = jnp.tanh(cross_gate).reshape(1, KV_HEADS, repeat, 1)
    grad_out = grad_rows.astype(jnp.float32).reshape(tok_rows, KV_HEADS, repeat, HEAD_DIM)
    gate_part = lax.optimization_barrier(jnp.sum(grad_out * cross_mixed, axis=(0, 3))).reshape(HEADS)
    grad_cross = rounded(grad_out * gate_tanh * image_mask)
    cross_query_grad, memory_key_grad, memory_value_grad = attend_back(grad_cross, self_out, memory_keys, memory_values, cross_weights, cross_narrow)
    grad_self = rounded(grad_out + cross_query_grad)
    query_grad, key_grad, value_grad = attend_back(grad_self, query_heads, key_part, value_part, weights, narrow_weights)
    context_part = jnp.concatenate([key_grad.reshape(key_rows, -1), value_grad.reshape(key_rows, -1)], axis=1)
    memory_part = jnp.concatenate([memory_key_grad.reshape(2 * IMG_TOK, -1), memory_value_grad.reshape(2 * IMG_TOK, -1)], axis=1)
    return (query_grad.reshape(tok_rows, -1).astype(jnp.bfloat16), context_part, memory_part, gate_part)

def reference(queries, context, segment_start, memory, image_offset, cross_gate, out_grad):
    doc_count = queries.shape[0]
    tok_rows = TOK_DEV
    flat_count = doc_count * SHARDS
    shard_ids = jnp.arange(SHARDS, dtype=jnp.int32)
    context_blocks = context.reshape(doc_count, SHARDS, tok_rows, -1)
    tail_rows = context_blocks[:, :, tok_rows - WINDOW:]
    earlier = jnp.concatenate([jnp.zeros_like(tail_rows[:, :1]), tail_rows[:, :-1]], axis=1)
    joined_keys = jnp.concatenate([earlier, context_blocks], axis=2).reshape(flat_count, WINDOW + tok_rows, -1)
    is_owner = image_offset < tok_rows
    owner_index = jnp.where(is_owner, shard_ids[None, :], -1).astype(jnp.int32)
    latest = lax.cummax(owner_index, axis=1)
    previous = jnp.concatenate([jnp.full((doc_count, 1), -1, jnp.int32), latest[:, :-1]], axis=1)
    has_prev = previous >= 0
    picked = jax.vmap(lambda images, index: images[index])(memory, jnp.maximum(previous, 0).astype(jnp.int32))
    joined_memory = jnp.concatenate([picked, memory], axis=2).reshape(flat_count, 2 * IMG_TOK, -1)

    def one_shard(item):
        query_rows, key_rows, memory_rows, segment_row, shard_index, offset, owner_flag, prev_flag, grad_rows = item
        allowed = self_mask(shard_index, tok_rows, segment_row)
        cross_allowed, has_image = cross_mask(tok_rows, offset, owner_flag, prev_flag)
        return shard_pass(query_rows, key_rows, memory_rows, allowed, cross_allowed, has_image, cross_gate, grad_rows)
    items = (queries.reshape(flat_count, tok_rows, -1), joined_keys, joined_memory, segment_start.reshape(flat_count, tok_rows), jnp.tile(shard_ids, doc_count), image_offset.reshape(flat_count), is_owner.reshape(flat_count), has_prev.reshape(flat_count), out_grad.reshape(flat_count, tok_rows, -1))
    query_grad, context_part, memory_part, gate_part = lax.map(one_shard, items)
    query_grad = query_grad.reshape(doc_count, SHARDS * tok_rows, -1)
    context_part = context_part.reshape(doc_count, SHARDS, WINDOW + tok_rows, -1)
    returned = jnp.pad(context_part[:, 1:, :WINDOW], ((0, 0), (0, 1), (tok_rows - WINDOW, 0), (0, 0)))
    context_grad = (context_part[:, :, WINDOW:] + returned).astype(jnp.bfloat16).reshape(doc_count, SHARDS * tok_rows, -1)
    memory_part = memory_part.reshape(doc_count, SHARDS, 2 * IMG_TOK, -1)
    carried = memory_part[:, :, :IMG_TOK]
    target = jnp.where(has_prev, previous, SHARDS).astype(jnp.int32)
    flat_target = (jnp.arange(doc_count, dtype=jnp.int32)[:, None] * (SHARDS + 1) + target).reshape(-1).astype(jnp.int32)
    summed = jax.ops.segment_sum(carried.reshape(flat_count, IMG_TOK, -1), flat_target, num_segments=doc_count * (SHARDS + 1))
    summed = summed.reshape(doc_count, SHARDS + 1, IMG_TOK, -1)[:, :SHARDS]
    memory_grad = jnp.where(is_owner[:, :, None, None], memory_part[:, :, IMG_TOK:] + summed, 0.0).astype(jnp.bfloat16)
    gate_tanh = jnp.tanh(cross_gate)
    gate_grad = (1.0 - gate_tanh * gate_tanh) * lax.optimization_barrier(jnp.sum(gate_part, axis=0))
    return (query_grad, context_grad, memory_grad, gate_grad)
```

```python
import functools
import math

import jax
import jax.numpy as jnp
from jax import lax
from jax.experimental import pallas as pl
from jax.experimental.pallas import tpu as pltpu
from jax.sharding import PartitionSpec as P

HEAD_DIM = 128
WINDOW = 64
GAP = 4
LANES = 128
SCALE = 1.0 / math.sqrt(HEAD_DIM)

VMEM = pl.BlockSpec(memory_space=pltpu.VMEM)
SMEM = pl.BlockSpec(memory_space=pltpu.SMEM)
PARAMS = pltpu.CompilerParams(vmem_limit_bytes=40 * 1024 * 1024)

NN = (((1,), (0,)), ((), ()))
NT = (((1,), (1,)), ((), ()))
TN = (((0,), (0,)), ((), ()))


def dot(a, b, dims):
    return lax.dot_general(a, b, dims, preferred_element_type=jnp.float32)


def stack(ref, first, rows, group, repeat):
    return jnp.concatenate(
        [
            ref[first : first + rows, (group * repeat + h) * HEAD_DIM : (group * repeat + h + 1) * HEAD_DIM]
            for h in range(repeat)
        ],
        axis=0,
    )


def part(ref, index):
    return ref[:, index * HEAD_DIM : (index + 1) * HEAD_DIM]


def softmax_rows(scores):
    top = jnp.max(scores, axis=0, keepdims=True)
    powers = jnp.exp(scores - top)
    return powers * (1.0 / jnp.sum(powers, axis=0, keepdims=True))


def self_mask(segment_ref, block, base):
    segment = segment_ref[0:1, block * WINDOW : (block + 1) * WINDOW]
    segment = jnp.concatenate([segment] * (LANES // WINDOW), axis=1)
    shape = (2 * WINDOW, LANES)
    key = lax.broadcasted_iota(jnp.int32, shape, 0)
    query = lax.broadcasted_iota(jnp.int32, shape, 1) % WINDOW
    key_pos = key + (base + (block - 1) * WINDOW)
    return (key >= query) & (key <= query + WINDOW) & (key_pos >= segment)


def self_weights(query_rows, keys, allowed):
    scores = dot(keys, query_rows, NT) * SCALE
    allowed = jnp.concatenate([allowed] * (scores.shape[1] // LANES), axis=1)
    return softmax_rows(jnp.where(allowed, scores, -1e30))


def joined(context_ref, halo_ref, block, index):
    own = context_ref[:, index * HEAD_DIM : (index + 1) * HEAD_DIM]
    if block == 0:
        return jnp.concatenate([part(halo_ref, index), own[:WINDOW]], axis=0)
    return own[(block - 1) * WINDOW : (block + 1) * WINDOW]


def chip_kernel(own_off, pair_off, own_ref, pair_ref, out_ref, *, tok_rows):
    is_owner = own_off[0, 0] < tok_rows
    has = is_owner | (pair_off[0, 0] < tok_rows)
    width = own_ref.shape[1]

    @pl.when(is_owner)
    def _():
        out_ref[:, :width] = own_ref[...]

    @pl.when(jnp.logical_not(is_owner))
    def _():
        out_ref[:, :width] = pair_ref[...]

    flag = jnp.where(has, 1.0, 0.0).astype(jnp.float32)
    out_ref[:, width:] = jnp.full((own_ref.shape[0], LANES), flag, jnp.float32).astype(jnp.bfloat16)


def self_kernel(query_ref, context_ref, halo_ref, segment_ref, out_ref, *, groups, repeat):
    tok_rows = query_ref.shape[0]
    base = lax.axis_index("seq") * tok_rows
    half = repeat * WINDOW
    for block in range(tok_rows // WINDOW):
        allowed = self_mask(segment_ref, block, base)
        for g in range(groups):
            rows = stack(query_ref, block * WINDOW, WINDOW, g, repeat)
            weights = self_weights(rows, joined(context_ref, halo_ref, block, g), allowed)
            values = joined(context_ref, halo_ref, block, groups + g)
            mixed = dot(values, weights.astype(jnp.bfloat16), TN)
            out_ref[g, :, block * half : (block + 1) * half] = mixed.astype(jnp.bfloat16)


def cross_kernel(
    own_off, pair_off, gate_ref, self_ref, grad_ref, own_ref, pair_ref, x_ref, z_ref, d_ref,
    grad_self_ref, to_pair_ref, to_x_ref, to_z_ref, to_d_ref, own_terms_ref, gate_out_ref, prev, *, groups, repeat
):
    tok_rows, width = grad_ref.shape[0], own_ref.shape[1]
    img = own_ref.shape[0]
    shard = lax.axis_index("seq")
    in_chip, in_block = shard % 2, shard % GAP
    off = own_off[0, 0]
    is_owner = off < tok_rows
    pair_owner = pair_off[0, 0] < tok_rows
    chip_owner = is_owner | pair_owner
    z_owner = jnp.max(z_ref[0:16, width:].astype(jnp.float32)) > 0.5
    from_pair = (in_chip == 1) & pair_owner
    from_x = (in_block >= 2) & jnp.logical_not(chip_owner)
    before = jnp.logical_not(from_pair | from_x) & (shard >= GAP)
    from_z = before & z_owner
    from_d = before & jnp.logical_not(z_owner)
    has_prev = from_pair | from_x | before

    @pl.when(from_pair)
    def _():
        prev[...] = pair_ref[...]

    @pl.when(from_x)
    def _():
        prev[...] = x_ref[:, :width]

    @pl.when(from_z)
    def _():
        prev[...] = z_ref[:, :width]

    @pl.when(jnp.logical_not(from_pair | from_x | from_z))
    def _():
        prev[...] = d_ref[:, :width]

    half = repeat * WINDOW
    rows = tok_rows * repeat
    lane = lax.broadcasted_iota(jnp.int32, (1, rows), 1)
    lane_tok = (lane // half) * WINDOW + lane % WINDOW
    own_from = jnp.where(is_owner, off, tok_rows)
    has_from = jnp.where(has_prev, 0, own_from)
    use_own = lane_tok >= own_from
    has_lane = lane_tok >= has_from
    row_tok = lax.broadcasted_iota(jnp.int32, (WINDOW, HEAD_DIM), 0)

    carried_key, carried_value = [], []
    for g in range(groups):
        keys = jnp.concatenate([part(prev, g), part(own_ref, g)], axis=0)
        values = jnp.concatenate([part(prev, groups + g), part(own_ref, groups + g)], axis=0)
        out_t = self_ref[g]
        scores = dot(keys, out_t, NN)
        weights = softmax_rows(jnp.where(use_own, scores[img:], scores[:img]) * SCALE)
        narrow = weights.astype(jnp.bfloat16)
        grad_rows, cross_rows = [], []
        for block in range(tok_rows // WINDOW):
            has_rows = row_tok + block * WINDOW >= has_from
            for h in range(repeat):
                head = g * repeat + h
                tile = grad_ref[
                    block * WINDOW : (block + 1) * WINDOW, head * HEAD_DIM : (head + 1) * HEAD_DIM
                ]
                grad_rows.append(tile)
                factor = jnp.where(has_rows, gate_ref[head], 0.0)
                cross_rows.append((tile.astype(jnp.float32) * factor).astype(jnp.bfloat16))
        grad_rows = jnp.concatenate(grad_rows, axis=0)
        cross_rows = jnp.concatenate(cross_rows, axis=0)
        plain = dot(values, grad_rows, NT)
        plain = jnp.where(use_own, plain[img:], plain[:img])
        gate_row = jnp.sum(narrow.astype(jnp.float32) * plain, axis=0, keepdims=True)
        gate_row = jnp.where(has_lane, gate_row, 0.0)
        gate_out_ref[g : g + 1, :] = gate_row[:, :half] + gate_row[:, half:]
        grad_weights = dot(values, cross_rows, NT)
        grad_weights = jnp.where(use_own, grad_weights[img:], grad_weights[:img])
        delta = jnp.sum(weights * grad_weights, axis=0, keepdims=True)
        grad_scores = weights * (grad_weights - delta)
        scores_j = jnp.concatenate(
            [jnp.where(use_own, 0.0, grad_scores), jnp.where(use_own, grad_scores, 0.0)], axis=0
        ).astype(jnp.bfloat16)
        narrow_j = jnp.concatenate(
            [jnp.where(use_own, 0.0, weights), jnp.where(use_own, weights, 0.0)], axis=0
        ).astype(jnp.bfloat16)
        grad_key = dot(scores_j, out_t, NT) * SCALE
        grad_value = dot(narrow_j, cross_rows, NN)
        grad_query = dot(scores_j, keys, TN) * SCALE
        grad_self_ref[g] = (grad_rows.astype(jnp.float32) + grad_query).astype(jnp.bfloat16)
        own_terms_ref[:, g * HEAD_DIM : (g + 1) * HEAD_DIM] = grad_key[img:]
        own_terms_ref[:, (groups + g) * HEAD_DIM : (groups + g + 1) * HEAD_DIM] = grad_value[img:]
        carried_key.append(grad_key[:img])
        carried_value.append(grad_value[:img])
    carried = jnp.concatenate(carried_key + carried_value, axis=1)
    for ref, here in ((to_pair_ref, from_pair), (to_x_ref, from_x), (to_z_ref, from_z), (to_d_ref, from_d)):
        ref[...] = (carried * jnp.where(here, 1.0, 0.0)).astype(ref.dtype)


def self_back_block(query_ref, context_ref, halo_ref, segment_ref, grad_ref, block, base, groups, repeat, put):
    half = repeat * WINDOW
    allowed = self_mask(segment_ref, block, base)
    for g in range(groups):
        rows = stack(query_ref, block * WINDOW, WINDOW, g, repeat)
        keys = joined(context_ref, halo_ref, block, g)
        values = joined(context_ref, halo_ref, block, groups + g)
        weights = self_weights(rows, keys, allowed)
        grads = grad_ref[g, block * half : (block + 1) * half, :]
        grad_weights = dot(values, grads, NT)
        delta = jnp.sum(weights * grad_weights, axis=0, keepdims=True)
        grad_scores = (weights * (grad_weights - delta)).astype(jnp.bfloat16)
        grad_query = (dot(grad_scores, keys, TN) * SCALE).astype(jnp.bfloat16)
        grad_key = dot(grad_scores, rows, NN) * SCALE
        grad_value = dot(weights.astype(jnp.bfloat16), grads, NN)
        put(g, grad_query, grad_key, grad_value)


def self_back_kernel(
    query_ref, context_ref, halo_ref, segment_ref, grad_ref, query_grad_ref, halo_out_ref, terms_ref, *, groups, repeat
):
    tok_rows = query_ref.shape[0]
    base = lax.axis_index("seq") * tok_rows
    blocks = tok_rows // WINDOW

    for block in range(blocks):

        def put(g, grad_query, grad_key, grad_value):
            for h in range(repeat):
                head = g * repeat + h
                query_grad_ref[
                    block * WINDOW : (block + 1) * WINDOW, head * HEAD_DIM : (head + 1) * HEAD_DIM
                ] = grad_query[h * WINDOW : (h + 1) * WINDOW]
            for index, grad in ((g, grad_key), (groups + g, grad_value)):
                cols = slice(index * HEAD_DIM, (index + 1) * HEAD_DIM)
                if block == 0:
                    halo_out_ref[:, cols] = grad[:WINDOW].astype(halo_out_ref.dtype)
                else:
                    before = slice((block - 1) * WINDOW, block * WINDOW)
                    terms_ref[before, cols] = terms_ref[before, cols] + grad[:WINDOW]
                terms_ref[block * WINDOW : (block + 1) * WINDOW, cols] = grad[WINDOW:]

        self_back_block(
            query_ref, context_ref, halo_ref, segment_ref, grad_ref, block, base, groups, repeat, put
        )


def chip_sum_kernel(to_pair_ref, x_ref, z_ref, d_ref, out_ref):
    f32 = jnp.float32
    out_ref[...] = (
        to_pair_ref[...].astype(f32) + x_ref[...].astype(f32) + z_ref[...].astype(f32) + d_ref[...].astype(f32)
    )


def finish_kernel(own_off, own_ref, mine_ref, pair_ref, terms_ref, halo_ref, memory_ref, context_ref, *, tok_rows):
    keep = jnp.where(own_off[0, 0] < tok_rows, 1.0, 0.0)
    memory_ref[...] = ((own_ref[...] + mine_ref[...] + pair_ref[...]) * keep).astype(memory_ref.dtype)
    size = lax.axis_size("seq")
    more = jnp.where(lax.axis_index("seq") < size - 1, 1.0, 0.0)
    first = tok_rows - WINDOW
    context_ref[:first] = terms_ref[:first].astype(context_ref.dtype)
    context_ref[first:] = (terms_ref[first:] + halo_ref[...].astype(jnp.float32) * more).astype(context_ref.dtype)


def struct(shape, dtype):
    return jax.ShapeDtypeStruct(shape, dtype)


def total(values, seq, dp):
    if seq % 16 or seq & (seq - 1) or dp != 2:
        return lax.psum(values, ("seq", "dp"))

    def swapped(value, seq_bits, dp_bits):
        pairs = [
            (s * dp + d, (s ^ seq_bits) * dp + (d ^ dp_bits)) for s in range(seq) for d in range(dp)
        ]
        return lax.ppermute(value, ("seq", "dp"), pairs)

    values = values + swapped(values, 1, 0)
    values = values + swapped(values, 2, 0) + swapped(values, 4, 0) + swapped(values, 6, 0)
    step = 8
    values = values + swapped(values, step, 0) + swapped(values, 0, 1) + swapped(values, step, 1)
    step = 16
    while step < seq:
        values = values + swapped(values, step, 0)
        step *= 2
    return values


def on_device(queries, context, segment_start, memory, image_offset, cross_gate, out_grad):
    tok_rows, model = queries.shape[1:]
    width = context.shape[2]
    groups = width // 2 // HEAD_DIM
    heads = cross_gate.shape[0]
    repeat = heads // groups
    img = memory.shape[2]
    seq, dp = lax.axis_size("seq"), lax.axis_size("dp")
    f32, bf16 = jnp.float32, jnp.bfloat16

    def send(value, where):
        return lax.ppermute(value, "seq", [(i, where(i)) for i in range(seq)])

    q, ctx, grad, own = queries[0], context[0], out_grad[0], memory[0, 0]
    pair_off = send(image_offset, lambda i: i ^ 1)
    pair = send(own, lambda i: i ^ 1)
    halo = send(ctx[tok_rows - WINDOW :], lambda i: (i + 1) % seq)
    gate_tanh = jnp.tanh(cross_gate)

    chip = pl.pallas_call(
        functools.partial(chip_kernel, tok_rows=tok_rows),
        out_shape=struct((img, width + LANES), bf16),
        in_specs=[SMEM, SMEM, VMEM, VMEM],
        out_specs=VMEM,
        compiler_params=PARAMS,
        name="chip_image",
    )(image_offset, pair_off, own, pair)
    by_x = send(chip, lambda i: i ^ 2)
    by_z = send(chip, lambda i: (i + GAP) % seq)
    by_d = send(chip, lambda i: ((i ^ 2) + GAP) % seq)

    self_out = pl.pallas_call(
        functools.partial(self_kernel, groups=groups, repeat=repeat),
        out_shape=struct((groups, HEAD_DIM, repeat * tok_rows), bf16),
        in_specs=[VMEM] * 4,
        out_specs=VMEM,
        compiler_params=PARAMS,
        cost_estimate=pl.CostEstimate(flops=2 * 10**9, bytes_accessed=3 * 10**6, transcendentals=10**6),
        name="self_forward",
    )(q, ctx, halo, segment_start)

    grad_self, to_pair, to_x, to_z, to_d, own_terms, gate_part = pl.pallas_call(
        functools.partial(cross_kernel, groups=groups, repeat=repeat),
        out_shape=[struct((groups, repeat * tok_rows, HEAD_DIM), bf16)]
        + [struct((img, width), bf16)] * 4
        + [struct((img, width), f32), struct((groups, repeat * WINDOW), f32)],
        in_specs=[SMEM] * 3 + [VMEM] * 7,
        out_specs=[VMEM] * 7,
        scratch_shapes=[pltpu.VMEM((img, width), bf16)],
        compiler_params=PARAMS,
        cost_estimate=pl.CostEstimate(flops=4 * 10**9, bytes_accessed=5 * 10**6, transcendentals=10**6),
        name="cross",
    )(image_offset, pair_off, gate_tanh, self_out, grad, own, pair, by_x, by_z, by_d)
    back_x = send(to_x, lambda i: i ^ 2)
    back_z = send(to_z, lambda i: (i - GAP) % seq)
    back_d = send(to_d, lambda i: (i - GAP) % seq ^ 2)
    gate_sum = total(gate_part, seq, dp)
    gate_sum = jnp.sum(gate_sum.reshape(heads, WINDOW), axis=1)
    gate_grad = (1.0 - gate_tanh * gate_tanh) * gate_sum

    query_grad, halo_terms, terms = pl.pallas_call(
        functools.partial(self_back_kernel, groups=groups, repeat=repeat),
        out_shape=[struct((tok_rows, model), bf16), struct((WINDOW, width), bf16), struct((tok_rows, width), f32)],
        in_specs=[VMEM] * 5,
        out_specs=[VMEM] * 3,
        compiler_params=PARAMS,
        cost_estimate=pl.CostEstimate(flops=4 * 10**9, bytes_accessed=5 * 10**6, transcendentals=10**6),
        name="self_backward",
    )(q, ctx, halo, segment_start, grad_self)
    halo_back = send(halo_terms, lambda i: (i - 1) % seq)

    mine = pl.pallas_call(
        chip_sum_kernel,
        out_shape=struct((img, width), f32),
        in_specs=[VMEM] * 4,
        out_specs=VMEM,
        compiler_params=PARAMS,
        name="chip_sum",
    )(to_pair, back_x, back_z, back_d)
    other = send(mine, lambda i: i ^ 1)
    memory_grad, context_grad = pl.pallas_call(
        functools.partial(finish_kernel, tok_rows=tok_rows),
        out_shape=[struct((img, width), bf16), struct((tok_rows, width), bf16)],
        in_specs=[SMEM] + [VMEM] * 5,
        out_specs=[VMEM] * 2,
        compiler_params=PARAMS,
        name="finish",
    )(image_offset, own_terms, mine, other, terms, halo_back)
    return (query_grad[None], context_grad[None], memory_grad[None, None], gate_grad)


def solution(mesh):
    placed = (
        P("dp", "seq", None),
        P("dp", "seq", None),
        P("dp", "seq"),
        P("dp", "seq", None, None),
        P("dp", "seq"),
        P(),
        P("dp", "seq", None),
    )
    return jax.shard_map(
        on_device,
        mesh=mesh,
        in_specs=placed,
        out_specs=(P("dp", "seq", None), P("dp", "seq", None), P("dp", "seq", None, None), P()),
        check_vma=False,
    )
```

```python
import functools
import math

import jax
import jax.numpy as jnp
from jax import lax
from jax.experimental import pallas as pl
from jax.experimental.pallas import tpu as pltpu
from jax.sharding import PartitionSpec as P

HEAD_DIM = 128
WINDOW = 64
GAP = 4
LANES = 128
SCALE = 1.0 / math.sqrt(HEAD_DIM)

VMEM = pl.BlockSpec(memory_space=pltpu.VMEM)
ANY = pl.BlockSpec(memory_space=pl.ANY)
SMEM = pl.BlockSpec(memory_space=pltpu.SMEM)

NN = (((1,), (0,)), ((), ()))
NT = (((1,), (1,)), ((), ()))
TN = (((0,), (0,)), ((), ()))


def dot(a, b, dims):
    return lax.dot_general(a, b, dims, preferred_element_type=jnp.float32)


def stack(ref, first, rows, group, repeat):
    return jnp.concatenate(
        [
            ref[first : first + rows, (group * repeat + h) * HEAD_DIM : (group * repeat + h + 1) * HEAD_DIM]
            for h in range(repeat)
        ],
        axis=0,
    )


def part(ref, index):
    return ref[:, index * HEAD_DIM : (index + 1) * HEAD_DIM]


def softmax_rows(scores):
    top = jnp.max(scores, axis=0, keepdims=True)
    powers = jnp.exp(scores - top)
    return powers * (1.0 / jnp.sum(powers, axis=0, keepdims=True))


def self_mask(segment_ref, block, base):
    segment = segment_ref[0:1, block * WINDOW : (block + 1) * WINDOW]
    segment = jnp.concatenate([segment] * (LANES // WINDOW), axis=1)
    shape = (2 * WINDOW, LANES)
    key = lax.broadcasted_iota(jnp.int32, shape, 0)
    query = lax.broadcasted_iota(jnp.int32, shape, 1) % WINDOW
    key_pos = key + (base + (block - 1) * WINDOW)
    return (key >= query) & (key <= query + WINDOW) & (key_pos >= segment)


def self_weights(query_rows, keys, allowed):
    scores = dot(keys, query_rows, NT) * SCALE
    allowed = jnp.concatenate([allowed] * (scores.shape[1] // LANES), axis=1)
    return softmax_rows(jnp.where(allowed, scores, -1e30))


def joined(context_ref, halo_ref, block, index):
    own = context_ref[:, index * HEAD_DIM : (index + 1) * HEAD_DIM]
    if block == 0:
        return jnp.concatenate([part(halo_ref, index), own[:WINDOW]], axis=0)
    return own[(block - 1) * WINDOW : (block + 1) * WINDOW]


def odd_core():
    return flag(lax.axis_index("seq") % 2 == 1)


def flag(cond):
    return jnp.where(cond, 1, 0)


def choose(here, mine_ref, other_ref, out_ref, width=None):
    here = jnp.broadcast_to(here, out_ref.shape) > 0
    width = width or mine_ref.shape[1]
    mine, other = mine_ref[:, :width].astype(jnp.float32), other_ref[:, :width].astype(jnp.float32)
    out_ref[...] = jnp.where(here, mine, other).astype(out_ref.dtype)


def owner(off_ref, row, tok_rows):
    return flag(off_ref[row : row + 1, 0:1] < tok_rows)


def chip_kernel(
    off_ref, pair_off_ref, mine_ref, other_ref, tail_ref, out_ref, marked_ref, half_ref, tail_out, owner_ref, *, tok_rows
):
    off, pair_off = off_ref[0, 0], pair_off_ref[0, 0]
    width = mine_ref.shape[1]
    tail_out[...] = tail_ref[...]
    choose(flag(off < tok_rows), mine_ref, other_ref, out_ref)
    marked_ref[:, :width] = out_ref[...]
    owns = jnp.where((off < tok_rows) | (pair_off < tok_rows), 1.0, 0.0)
    marked_ref[:, width:] = jnp.full((mine_ref.shape[0], LANES), owns, jnp.float32).astype(marked_ref.dtype)
    choose(odd_core(), out_ref.at[:, width // 2 :], out_ref.at[:, : width // 2], half_ref)
    row = lax.broadcasted_iota(jnp.int32, owner_ref.shape, 0)
    owner_ref[...] = jnp.where(row == 0, off, pair_off)


def join_kernel(z_ref, x_ref, _, __, out_ref):
    out_ref[:, : z_ref.shape[1]] = z_ref[...]
    out_ref[:, z_ref.shape[1] :] = x_ref[...]


def near_kernel(chip_ref, other_ref, _, out_ref, *, step):
    choose(flag(lax.axis_index("seq") % 2 == (1 if step > 0 else 0)), chip_ref, other_ref, out_ref)


def self_kernel(query_ref, context_ref, halo_ref, segment_ref, _, out_ref, weights_ref, *, block, groups, repeat):
    tok_rows = query_ref.shape[0]
    base = lax.axis_index("seq") * tok_rows
    allowed = self_mask(segment_ref, block, base)
    for g in range(groups):
        rows = stack(query_ref, block * WINDOW, WINDOW, g, repeat)
        weights = self_weights(rows, joined(context_ref, halo_ref, block, g), allowed)
        weights_ref[g] = weights
        values = joined(context_ref, halo_ref, block, groups + g)
        out_ref[g] = dot(values, weights.astype(jnp.bfloat16), TN).astype(jnp.bfloat16)


def split(values):
    high = values.astype(jnp.bfloat16)
    rest = values - high.astype(jnp.float32)
    middle = rest.astype(jnp.bfloat16)
    low = (rest - middle.astype(jnp.float32)).astype(jnp.bfloat16)
    return jnp.concatenate([high, middle, low, jnp.zeros_like(low)], axis=0)


def unsplit(parts):
    parts = parts.astype(jnp.float32)
    rows = parts.shape[0] // 4
    return parts[:rows] + (parts[rows : 2 * rows] + parts[2 * rows : 3 * rows])


def cross_kernel(
    off_ref, gate_ref, self_0_ref, self_1_ref, grad_ref, own_ref, chip_ref, mine_ref, pair_ref,
    grad_self_ref, to_pair_ref, in_chip_ref, own_terms_ref, mask_ref, prev, *, groups, repeat
):
    tok_rows, width = grad_ref.shape[0], own_ref.shape[1]
    img = own_ref.shape[0]
    shard = lax.axis_index("seq")
    off = off_ref[0:1, 0:1]
    is_owner, pair_owner = owner(off_ref, 0, tok_rows), owner(off_ref, 1, tok_rows)
    upper, odd = flag(shard % GAP >= 2), flag(shard % 2 == 1)
    from_chip = odd * pair_owner
    from_x = upper * (1 - (is_owner | pair_owner))
    from_z = flag(shard >= GAP) * (1 - (from_chip | from_x))
    has_prev = from_chip | from_x | from_z
    marked = width + LANES
    by_mine = flag(mine_ref[0:1, width : width + 1].astype(jnp.float32) > 0.5)
    choose(by_mine, mine_ref, pair_ref, prev, width)
    for first in (0, 1):
        cols = prev.at[:, first * width // 2 : (first + 1) * width // 2]
        mine = from_x * flag(odd == first)
        choose(mine, mine_ref.at[:, marked:], cols, cols)
        choose(from_x - mine, pair_ref.at[:, marked:], cols, cols)
    choose(from_chip, chip_ref, prev, prev)

    half = repeat * WINDOW
    rows = tok_rows * repeat
    lane = lax.broadcasted_iota(jnp.int32, (1, rows), 1)
    lane_tok = (lane // half) * WINDOW + lane % WINDOW
    own_from = jnp.minimum(off, tok_rows)
    has_from = own_from * (1 - has_prev)
    from_chip, from_x, from_z = (here.astype(jnp.float32) for here in (from_chip, from_x, from_z))
    use_own = lane_tok >= own_from
    has_lane = lane_tok >= has_from
    row_tok = lax.broadcasted_iota(jnp.int32, (WINDOW, HEAD_DIM), 0)

    gate_rows = []
    for g in range(groups):
        keys = jnp.concatenate([part(prev, g), part(own_ref, g)], axis=0)
        values = jnp.concatenate([part(prev, groups + g), part(own_ref, groups + g)], axis=0)
        out_t = jnp.concatenate([self_0_ref[g], self_1_ref[g]], axis=1)
        scores = dot(keys, out_t, NN)
        weights = softmax_rows(jnp.where(use_own, scores[img:], scores[:img]) * SCALE)
        narrow = weights.astype(jnp.bfloat16)
        grad_rows, cross_rows = [], []
        for block in range(tok_rows // WINDOW):
            has_rows = row_tok + block * WINDOW >= has_from
            for h in range(repeat):
                head = g * repeat + h
                tile = grad_ref[
                    block * WINDOW : (block + 1) * WINDOW, head * HEAD_DIM : (head + 1) * HEAD_DIM
                ]
                grad_rows.append(tile)
                factor = jnp.where(has_rows, gate_ref[head : head + 1, :], 0.0)
                cross_rows.append((tile.astype(jnp.float32) * factor).astype(jnp.bfloat16))
        grad_rows = jnp.concatenate(grad_rows, axis=0)
        cross_rows = jnp.concatenate(cross_rows, axis=0)
        plain = dot(values, grad_rows, NT)
        plain = jnp.where(use_own, plain[img:], plain[:img])
        gate_row = jnp.sum(narrow.astype(jnp.float32) * plain, axis=0, keepdims=True)
        gate_row = jnp.where(has_lane, gate_row, 0.0)
        gate_row = gate_row[:, :half] + gate_row[:, half:]
        gate_rows.extend(gate_row[:, i * LANES : (i + 1) * LANES] for i in range(half // LANES))
        grad_weights = dot(values, cross_rows, NT)
        grad_weights = jnp.where(use_own, grad_weights[img:], grad_weights[:img])
        delta = jnp.sum(weights * grad_weights, axis=0, keepdims=True)
        grad_scores = weights * (grad_weights - delta)
        scores_j = jnp.concatenate(
            [jnp.where(use_own, 0.0, grad_scores), jnp.where(use_own, grad_scores, 0.0)], axis=0
        ).astype(jnp.bfloat16)
        narrow_j = jnp.concatenate(
            [jnp.where(use_own, 0.0, weights), jnp.where(use_own, weights, 0.0)], axis=0
        ).astype(jnp.bfloat16)
        grad_key = dot(scores_j, out_t, NT) * SCALE
        grad_value = dot(narrow_j, cross_rows, NN)
        grad_query = dot(scores_j, keys, TN) * SCALE
        grad_self_ref[g] = (grad_rows.astype(jnp.float32) + grad_query).astype(jnp.bfloat16)
        for index, terms in ((g, grad_key), (groups + g, grad_value)):
            cols = slice(index * HEAD_DIM, (index + 1) * HEAD_DIM)
            own_terms_ref[:, cols] = terms[img:]
            to_pair_ref[:, cols] = terms[:img] * (from_x + from_z)
            in_chip_ref[:, cols] = terms[:img] * from_chip
    gate = jnp.concatenate(gate_rows, axis=0)
    to_pair_ref[:, width:] = jnp.concatenate([gate] * (img // gate.shape[0]), axis=0)
    row = lax.broadcasted_iota(jnp.int32, mask_ref.shape, 0)
    mask_ref[...] = jnp.where(row == 0, by_mine.astype(jnp.float32) * (1.0 - from_x), from_x)


def outside_kernel(mine_ref, pair_ref, mask_ref, to_z_ref, to_x_ref, gate_ref):
    width = mine_ref.shape[1] - LANES
    total = mine_ref[...] + pair_ref[...]
    gate = total[: gate_ref.shape[0], width:]
    terms = total[:, :width]
    to_z_ref[:, :width] = (terms * mask_ref[0:1, 0:1]).astype(to_z_ref.dtype)
    to_z_ref[:, width:] = split(gate)
    odd = jnp.broadcast_to(odd_core(), (terms.shape[0], width // 2)) > 0
    half = jnp.where(odd, terms[:, width // 2 :], terms[:, : width // 2])
    to_x_ref[:, : width // 2] = (half * mask_ref[1:2, 0:1]).astype(to_x_ref.dtype)
    to_x_ref[:, width // 2 :] = split(gate)
    gate_ref[...] = gate


def chip_sum_kernel(mine_ref, x_ref, z_ref, gate_ref, halo_ref, _, out_ref, gate_out, halo_out):
    halo_out[...] = halo_ref[...]
    width = mine_ref.shape[1]
    odd = odd_core().astype(jnp.float32)
    half = width // 2
    from_x = x_ref[:, :half].astype(jnp.float32)
    out_ref[:, :half] = mine_ref[:, :half] + (from_x * (1.0 - odd) + z_ref[:, :half].astype(jnp.float32))
    out_ref[:, half:width] = mine_ref[:, half:] + (from_x * odd + z_ref[:, half:width].astype(jnp.float32))
    gate_out[...] = gate_ref[...] + unsplit(x_ref[:, half:])
    gate = unsplit(z_ref[:, width:])
    out_ref[:, width:] = jnp.concatenate([gate] * (mine_ref.shape[0] // gate.shape[0]), axis=0)


def self_back_kernel(
    query_ref, context_ref, halo_ref, weights_ref, grad_ref, _,
    query_grad_ref, key_low_ref, key_high_ref, rows_out, sems, *, block, groups, repeat
):
    copies = []
    half = repeat * WINDOW
    for g in range(groups):
        rows = stack(query_ref, block * WINDOW, WINDOW, g, repeat)
        keys = joined(context_ref, halo_ref, block, g)
        values = joined(context_ref, halo_ref, block, groups + g)
        weights = weights_ref[g]
        grads = grad_ref[g, block * half : (block + 1) * half, :]
        grad_weights = dot(values, grads, NT)
        delta = jnp.sum(weights * grad_weights, axis=0, keepdims=True)
        grad_scores = (weights * (grad_weights - delta)).astype(jnp.bfloat16)
        grad_query = (dot(grad_scores, keys, TN) * SCALE).astype(jnp.bfloat16)
        for h in range(repeat):
            head = g * repeat + h
            rows_out[:, head * HEAD_DIM : (head + 1) * HEAD_DIM] = grad_query[h * WINDOW : (h + 1) * WINDOW]
        cols = slice(g * repeat * HEAD_DIM, (g + 1) * repeat * HEAD_DIM)
        copies.append(
            pltpu.make_async_copy(
                rows_out.at[:, cols], query_grad_ref.at[block * WINDOW : (block + 1) * WINDOW, cols], sems.at[g]
            )
        )
        copies[-1].start()
        grad_key = dot(grad_scores, rows, NN) * SCALE
        grad_value = dot(weights.astype(jnp.bfloat16), grads, NN)
        for index, terms in ((g, grad_key), (groups + g, grad_value)):
            cols = slice(index * HEAD_DIM, (index + 1) * HEAD_DIM)
            key_low_ref[:, cols] = terms[:WINDOW].astype(key_low_ref.dtype)
            key_high_ref[:, cols] = terms[WINDOW:]
    for copy in copies:
        copy.wait()


def gate_kernel(chip_ref, mine_ref, pair_ref, out_ref):
    width = mine_ref.shape[1] - LANES
    rows = out_ref.shape[0]
    out_ref[...] = chip_ref[...] + (mine_ref[:rows, width:] + pair_ref[:rows, width:])


def add_kernel(one_ref, other_ref, out_ref):
    out_ref[...] = one_ref[...] + other_ref[...]


def gate_grad_kernel(one_ref, other_ref, gate_ref, out_ref):
    rows, heads = one_ref.shape[0], out_ref.shape[1]
    total = one_ref[...] + other_ref[...]
    lane = lax.broadcasted_iota(jnp.int32, total.shape, 1)
    first = jnp.sum(jnp.where(lane < WINDOW, total, 0.0), axis=1, keepdims=True)
    second = jnp.sum(jnp.where(lane < WINDOW, 0.0, total), axis=1, keepdims=True)
    row = lax.broadcasted_iota(jnp.int32, (rows, heads), 0)
    head = lax.broadcasted_iota(jnp.int32, (rows, heads), 1)
    sums = jnp.where(head == 2 * row, first, 0.0) + jnp.where(head == 2 * row + 1, second, 0.0)
    sums = jnp.sum(sums, axis=0, keepdims=True)
    tanh = gate_ref[:, :heads]
    same = lax.broadcasted_iota(jnp.int32, tanh.shape, 0) == lax.broadcasted_iota(jnp.int32, tanh.shape, 1)
    tanh = jnp.sum(jnp.where(same, tanh, 0.0), axis=0, keepdims=True)
    out_ref[...] = (1.0 - tanh * tanh) * sums


def finish_kernel(
    off_ref, own_ref, mine_ref, pair_ref, low_ref, also_ref, high_ref, halo_ref, _,
    memory_ref, context_ref, *, tok_rows
):
    width = own_ref.shape[1]
    keep = flag(off_ref[0:1, 0:1] < tok_rows).astype(jnp.float32)
    total = own_ref[...] + (mine_ref[:, :width] + pair_ref[:, :width])
    memory_ref[...] = (total * keep).astype(memory_ref.dtype)
    more = jnp.where(lax.axis_index("seq") < lax.axis_size("seq") - 1, 1.0, 0.0)
    first = tok_rows - WINDOW
    context_ref[:first] = (low_ref[...] + also_ref[...]).astype(context_ref.dtype)
    context_ref[first:] = (high_ref[...] + halo_ref[...].astype(jnp.float32) * more).astype(context_ref.dtype)


def struct(shape, dtype):
    return jax.ShapeDtypeStruct(shape, dtype)


def call(
    name, kernel, out_shape, in_specs, scratch=(), out_specs=None, aliases=None, flops=10**6, moved=10**6
):
    return pl.pallas_call(
        kernel,
        out_shape=out_shape,
        in_specs=in_specs,
        out_specs=[VMEM] * len(out_shape) if out_specs is None else out_specs,
        scratch_shapes=scratch,
        input_output_aliases=aliases or {},
        compiler_params=pltpu.CompilerParams(vmem_limit_bytes=40 * 2**20),
        cost_estimate=pl.CostEstimate(flops=flops, bytes_accessed=moved, transcendentals=0),
        name=name,
    )


def on_device(queries, context, segment_start, memory, image_offset, cross_gate, out_grad):
    tok_rows, model = queries.shape[1:]
    width = context.shape[2]
    groups = width // 2 // HEAD_DIM
    heads = cross_gate.shape[0]
    repeat = heads // groups
    img = memory.shape[2]
    half = repeat * WINDOW
    seq, dp = lax.axis_size("seq"), lax.axis_size("dp")
    f32, bf16 = jnp.float32, jnp.bfloat16

    swaps = seq == 4 * GAP and dp == 2

    def send(value, where):
        return lax.ppermute(value, "seq", [(i, where(i)) for i in range(seq)])

    def send_all(value, where):
        pairs = [(s, d, *where(s, d)) for s in range(seq) for d in range(dp)]
        return lax.ppermute(value, ("seq", "dp"), [(s * dp + d, t * dp + e) for s, d, t, e in pairs])

    def send_near(value, step):
        if not swaps:
            return (send(value, lambda i: (i + step) % seq),)
        off_chip = lambda s, d: (s, d ^ 1) if s in (0, seq - 1) else (((s + 1) ^ 1) - 1, d)
        return send(value, lambda i: i ^ 1), send_all(value, off_chip)

    def merge(name, arrived, step, after):
        if len(arrived) == 1:
            return arrived[0]
        return call(name, functools.partial(near_kernel, step=step), [window], [VMEM] * 2 + [ANY])(*arrived, after)[0]

    def send_z(value, step):
        return send(value, lambda i: ((i if i % 2 == 0 else i ^ 2) + step * GAP) % seq)

    q, ctx, grad = queries[0], context[0], out_grad[0]
    gate_tanh = jnp.tanh(cross_gate)
    gate_rows = jnp.broadcast_to(gate_tanh[:, None], (heads, LANES))
    image = struct((img, width), bf16)
    window = struct((WINDOW, width), bf16)
    own = memory[0, 0]
    pair = send(own, lambda i: i ^ 1)
    pair_off = send(image_offset, lambda i: i ^ 1)
    tail = ctx[tok_rows - WINDOW :]
    chip, marked, chip_half, tail, off = call(
        "chip_image",
        functools.partial(chip_kernel, tok_rows=tok_rows),
        [image, struct((img, width + LANES), bf16), struct((img, width // 2), bf16), window, struct((8, LANES), jnp.int32)],
        [SMEM] * 2 + [VMEM] * 3,
    )(image_offset, pair_off, own, pair, tail)
    by_z = send_z(marked, 1)
    by_x = send(chip_half, lambda i: i ^ 2)
    halo = merge("halo", send_near(tail, 1), 1, chip)
    self_out, kept = [None, None], [None, None]

    def self_forward(block, after):
        self_out[block], kept[block] = call(
            f"self_forward_{block}",
            functools.partial(self_kernel, block=block, groups=groups, repeat=repeat),
            [struct((groups, HEAD_DIM, half), bf16), struct((groups, 2 * WINDOW, half), f32)],
            [VMEM] * 4 + [ANY],
            flops=10**6,
            moved=10**5,
        )(q, ctx, tail if block else halo, segment_start, after)

    self_forward(1, chip)
    arrived = call("arrived", join_kernel, [struct((img, width + LANES + width // 2), bf16)], [VMEM] * 2 + [ANY] * 2)(
        by_z, by_x, self_out[1], halo
    )[0]

    by_pair = send(arrived, lambda i: i ^ 1)
    self_forward(0, arrived)

    gate_shape = struct((heads * WINDOW // LANES, LANES), f32)
    grad_self, to_pair, in_chip, own_terms, masks = call(
        "cross",
        functools.partial(cross_kernel, groups=groups, repeat=repeat),
        [
            struct((groups, repeat * tok_rows, HEAD_DIM), bf16),
            struct((img, width + LANES), f32),
            struct((img, width), f32),
            struct((img, width), f32),
            struct((8, LANES), f32),
        ],
        [VMEM] * 9,
        scratch=[pltpu.VMEM((img, width), bf16)],
    )(off, gate_rows, *self_out, grad, own, chip, arrived, by_pair)
    from_pair = send(to_pair, lambda i: i ^ 1)
    to_z, to_x, gate_chip = call(
        "outside",
        outside_kernel,
        [struct((img, width + LANES), bf16), struct((img, width // 2 + LANES), bf16), gate_shape],
        [VMEM] * 3,
    )(to_pair, from_pair, masks)
    from_z = send_z(to_z, -1)
    from_x = send(to_x, lambda i: i ^ 2)

    def self_backward(block, after):
        return call(
            f"self_backward_{block}",
            functools.partial(self_back_kernel, block=block, groups=groups, repeat=repeat),
            [
                struct((tok_rows, model), bf16),
                struct((WINDOW, width), f32 if block else bf16),
                struct((WINDOW, width), f32),
            ],
            [VMEM] * 5 + [ANY],
            scratch=[pltpu.VMEM((WINDOW, model), bf16), pltpu.SemaphoreType.DMA((groups,))],
            out_specs=[ANY, VMEM, VMEM],
            aliases={5: 0} if block else None,
            flops=10**6,
            moved=10**5,
        )(q, ctx, tail if block else halo, kept[block], grad_self, after)

    query_grad, halo_terms, low = self_backward(0, to_z)
    query_grad, also, high = self_backward(1, query_grad)
    mine, gate_near, halo_terms = call(
        "chip_sum",
        chip_sum_kernel,
        [struct((img, width + LANES), f32), gate_shape, window],
        [VMEM] * 5 + [ANY],
    )(in_chip, from_x, from_z, gate_chip, halo_terms, high)
    other = send(mine, lambda i: i ^ 1)
    halo_back = merge("halo_back", send_near(halo_terms, -1), -1, mine)
    gate_sum = call("gate_sum", gate_kernel, [gate_shape], [VMEM] * 3)(gate_near, mine, other)[0]
    memory_grad, context_grad = call(
        "finish",
        functools.partial(finish_kernel, tok_rows=tok_rows),
        [image, struct((tok_rows, width), bf16)],
        [VMEM] * 8 + [ANY],
    )(off, own_terms, mine, other, low, also, high, halo_back, gate_sum)

    if not swaps:
        gate_total = lax.psum(to_pair[: gate_shape.shape[0], width:], ("seq", "dp"))
        gate_grad = (1.0 - gate_tanh * gate_tanh) * jnp.sum(gate_total.reshape(heads, WINDOW), axis=1)
        return (query_grad[None], context_grad[None], memory_grad[None, None], gate_grad)
    gate_sum = call("gate_docs", add_kernel, [gate_shape], [VMEM] * 2)(
        gate_sum, send_all(gate_sum, lambda s, d: (s, d ^ 1))
    )[0]
    gate_grad = call("gate_grad", gate_grad_kernel, [struct((1, heads), f32)], [VMEM] * 3)(
        gate_sum, send_all(gate_sum, lambda s, d: (s ^ 2 * GAP, d)), gate_rows
    )[0].reshape(heads)
    return (query_grad[None], context_grad[None], memory_grad[None, None], gate_grad)


def solution(mesh):
    placed = (
        P("dp", "seq", None),
        P("dp", "seq", None),
        P("dp", "seq"),
        P("dp", "seq", None, None),
        P("dp", "seq"),
        P(),
        P("dp", "seq", None),
    )
    return jax.shard_map(
        on_device,
        mesh=mesh,
        in_specs=placed,
        out_specs=(P("dp", "seq", None), P("dp", "seq", None), P("dp", "seq", None, None), P()),
        check_vma=False,
    )
```

```python
import functools
import math

import jax
import jax.numpy as jnp
from jax import lax
from jax.experimental import pallas as pl
from jax.experimental.pallas import tpu as pltpu
from jax.sharding import PartitionSpec as P

HEAD_DIM = 128
WINDOW = 64
GAP = 4
LANES = 128
SCALE = 1.0 / math.sqrt(HEAD_DIM)

VMEM = pl.BlockSpec(memory_space=pltpu.VMEM)
ANY = pl.BlockSpec(memory_space=pl.ANY)
SMEM = pl.BlockSpec(memory_space=pltpu.SMEM)

NN = (((1,), (0,)), ((), ()))
NT = (((1,), (1,)), ((), ()))
TN = (((0,), (0,)), ((), ()))


def dot(a, b, dims):
    return lax.dot_general(a, b, dims, preferred_element_type=jnp.float32)


def stack(ref, first, rows, group, repeat):
    return jnp.concatenate(
        [
            ref[first : first + rows, (group * repeat + h) * HEAD_DIM : (group * repeat + h + 1) * HEAD_DIM]
            for h in range(repeat)
        ],
        axis=0,
    )


def part(ref, index):
    return ref[:, index * HEAD_DIM : (index + 1) * HEAD_DIM]


def softmax_rows(scores):
    top = jnp.max(scores, axis=0, keepdims=True)
    powers = jnp.exp(scores - top)
    return powers * (1.0 / jnp.sum(powers, axis=0, keepdims=True))


def self_mask(segment_ref, block, base):
    segment = segment_ref[0:1, block * WINDOW : (block + 1) * WINDOW]
    segment = jnp.concatenate([segment] * (LANES // WINDOW), axis=1)
    shape = (2 * WINDOW, LANES)
    key = lax.broadcasted_iota(jnp.int32, shape, 0)
    query = lax.broadcasted_iota(jnp.int32, shape, 1) % WINDOW
    key_pos = key + (base + (block - 1) * WINDOW)
    return (key >= query) & (key <= query + WINDOW) & (key_pos >= segment)


def self_weights(query_rows, keys, allowed):
    scores = dot(keys, query_rows, NT) * SCALE
    allowed = jnp.concatenate([allowed] * (scores.shape[1] // LANES), axis=1)
    return softmax_rows(jnp.where(allowed, scores, -1e30))


def joined(context_ref, halo_ref, block, index):
    own = context_ref[:, index * HEAD_DIM : (index + 1) * HEAD_DIM]
    if block == 0:
        return jnp.concatenate([part(halo_ref, index), own[:WINDOW]], axis=0)
    return own[(block - 1) * WINDOW : (block + 1) * WINDOW]


def odd_core():
    return flag(lax.axis_index("seq") % 2 == 1)


def flag(cond):
    return jnp.where(cond, 1, 0)


def choose(here, mine_ref, other_ref, out_ref, width=None):
    here = jnp.broadcast_to(here, out_ref.shape) > 0
    width = width or mine_ref.shape[1]
    mine, other = mine_ref[:, :width].astype(jnp.float32), other_ref[:, :width].astype(jnp.float32)
    out_ref[...] = jnp.where(here, mine, other).astype(out_ref.dtype)


def owner(off_ref, row, tok_rows):
    return flag(off_ref[row : row + 1, 0:1] < tok_rows)


def chip_kernel(
    off_ref, pair_off_ref, mine_ref, other_ref, tail_ref, out_ref, marked_ref, half_ref, tail_out, owner_ref, *, tok_rows
):
    off, pair_off = off_ref[0, 0], pair_off_ref[0, 0]
    width = mine_ref.shape[1]
    tail_out[...] = tail_ref[...]
    choose(flag(off < tok_rows), mine_ref, other_ref, out_ref)
    marked_ref[:, :width] = out_ref[...]
    owns = jnp.where((off < tok_rows) | (pair_off < tok_rows), 1.0, 0.0)
    marked_ref[:, width:] = jnp.full((mine_ref.shape[0], LANES), owns, jnp.float32).astype(marked_ref.dtype)
    choose(odd_core(), out_ref.at[:, width // 2 :], out_ref.at[:, : width // 2], half_ref)
    row = lax.broadcasted_iota(jnp.int32, owner_ref.shape, 0)
    owner_ref[...] = jnp.where(row == 0, off, pair_off)


def join_kernel(z_ref, x_ref, _, __, out_ref):
    out_ref[:, : z_ref.shape[1]] = z_ref[...]
    out_ref[:, z_ref.shape[1] :] = x_ref[...]


def near_kernel(chip_ref, other_ref, _, out_ref, *, step):
    choose(flag(lax.axis_index("seq") % 2 == (1 if step > 0 else 0)), chip_ref, other_ref, out_ref)


def self_kernel(query_ref, context_ref, halo_ref, segment_ref, _, out_ref, weights_ref, *, block, groups, repeat):
    tok_rows = query_ref.shape[0]
    base = lax.axis_index("seq") * tok_rows
    allowed = self_mask(segment_ref, block, base)
    for g in range(groups):
        rows = stack(query_ref, block * WINDOW, WINDOW, g, repeat)
        weights = self_weights(rows, joined(context_ref, halo_ref, block, g), allowed)
        weights_ref[g] = weights
        values = joined(context_ref, halo_ref, block, groups + g)
        out_ref[g] = dot(values, weights.astype(jnp.bfloat16), TN).astype(jnp.bfloat16)


def split(values):
    high = values.astype(jnp.bfloat16)
    rest = values - high.astype(jnp.float32)
    middle = rest.astype(jnp.bfloat16)
    low = (rest - middle.astype(jnp.float32)).astype(jnp.bfloat16)
    return jnp.concatenate([high, middle, low, jnp.zeros_like(low)], axis=0)


def unsplit(parts):
    parts = parts.astype(jnp.float32)
    rows = parts.shape[0] // 4
    return parts[:rows] + (parts[rows : 2 * rows] + parts[2 * rows : 3 * rows])


def cross_kernel(
    off_ref, gate_ref, self_0_ref, self_1_ref, grad_ref, own_ref, chip_ref, mine_ref, pair_ref,
    grad_self_ref, to_pair_ref, in_chip_ref, own_terms_ref, mask_ref, prev, *, groups, repeat
):
    tok_rows, width = grad_ref.shape[0], own_ref.shape[1]
    img = own_ref.shape[0]
    shard = lax.axis_index("seq")
    off = off_ref[0:1, 0:1]
    is_owner, pair_owner = owner(off_ref, 0, tok_rows), owner(off_ref, 1, tok_rows)
    upper, odd = flag(shard % GAP >= 2), flag(shard % 2 == 1)
    from_chip = odd * pair_owner
    from_x = upper * (1 - (is_owner | pair_owner))
    from_z = flag(shard >= GAP) * (1 - (from_chip | from_x))
    has_prev = from_chip | from_x | from_z
    marked = width + LANES
    by_mine = flag(mine_ref[0:1, width : width + 1].astype(jnp.float32) > 0.5)
    choose(by_mine, mine_ref, pair_ref, prev, width)
    for first in (0, 1):
        cols = prev.at[:, first * width // 2 : (first + 1) * width // 2]
        mine = from_x * flag(odd == first)
        choose(mine, mine_ref.at[:, marked:], cols, cols)
        choose(from_x - mine, pair_ref.at[:, marked:], cols, cols)
    choose(from_chip, chip_ref, prev, prev)

    half = repeat * WINDOW
    rows = tok_rows * repeat
    lane = lax.broadcasted_iota(jnp.int32, (1, rows), 1)
    lane_tok = (lane // half) * WINDOW + lane % WINDOW
    own_from = jnp.minimum(off, tok_rows)
    has_from = own_from * (1 - has_prev)
    from_chip, from_x, from_z = (here.astype(jnp.float32) for here in (from_chip, from_x, from_z))
    use_own = lane_tok >= own_from
    has_lane = lane_tok >= has_from
    row_tok = lax.broadcasted_iota(jnp.int32, (WINDOW, HEAD_DIM), 0)

    gate_rows = []
    for g in range(groups):
        keys = jnp.concatenate([part(prev, g), part(own_ref, g)], axis=0)
        values = jnp.concatenate([part(prev, groups + g), part(own_ref, groups + g)], axis=0)
        out_t = jnp.concatenate([self_0_ref[g], self_1_ref[g]], axis=1)
        scores = dot(keys, out_t, NN)
        weights = softmax_rows(jnp.where(use_own, scores[img:], scores[:img]) * SCALE)
        narrow = weights.astype(jnp.bfloat16)
        grad_rows, cross_rows = [], []
        for block in range(tok_rows // WINDOW):
            has_rows = row_tok + block * WINDOW >= has_from
            for h in range(repeat):
                head = g * repeat + h
                tile = grad_ref[
                    block * WINDOW : (block + 1) * WINDOW, head * HEAD_DIM : (head + 1) * HEAD_DIM
                ]
                grad_rows.append(tile)
                factor = jnp.where(has_rows, gate_ref[head : head + 1, :], 0.0)
                cross_rows.append((tile.astype(jnp.float32) * factor).astype(jnp.bfloat16))
        grad_rows = jnp.concatenate(grad_rows, axis=0)
        cross_rows = jnp.concatenate(cross_rows, axis=0)
        plain = dot(values, grad_rows, NT)
        plain = jnp.where(use_own, plain[img:], plain[:img])
        gate_row = jnp.sum(narrow.astype(jnp.float32) * plain, axis=0, keepdims=True)
        gate_row = jnp.where(has_lane, gate_row, 0.0)
        gate_row = gate_row[:, :half] + gate_row[:, half:]
        gate_rows.extend(gate_row[:, i * LANES : (i + 1) * LANES] for i in range(half // LANES))
        grad_weights = dot(values, cross_rows, NT)
        grad_weights = jnp.where(use_own, grad_weights[img:], grad_weights[:img])
        delta = jnp.sum(weights * grad_weights, axis=0, keepdims=True)
        grad_scores = weights * (grad_weights - delta)
        scores_j = jnp.concatenate(
            [jnp.where(use_own, 0.0, grad_scores), jnp.where(use_own, grad_scores, 0.0)], axis=0
        ).astype(jnp.bfloat16)
        narrow_j = jnp.concatenate(
            [jnp.where(use_own, 0.0, weights), jnp.where(use_own, weights, 0.0)], axis=0
        ).astype(jnp.bfloat16)
        grad_key = dot(scores_j, out_t, NT) * SCALE
        grad_value = dot(narrow_j, cross_rows, NN)
        grad_query = dot(scores_j, keys, TN) * SCALE
        grad_self_ref[g] = (grad_rows.astype(jnp.float32) + grad_query).astype(jnp.bfloat16)
        for index, terms in ((g, grad_key), (groups + g, grad_value)):
            cols = slice(index * HEAD_DIM, (index + 1) * HEAD_DIM)
            own_terms_ref[:, cols] = terms[img:]
            to_pair_ref[:, cols] = terms[:img] * (from_x + from_z)
            in_chip_ref[:, cols] = terms[:img] * from_chip
    gate = jnp.concatenate(gate_rows, axis=0)
    to_pair_ref[:, width:] = jnp.concatenate([gate] * (img // gate.shape[0]), axis=0)
    row = lax.broadcasted_iota(jnp.int32, mask_ref.shape, 0)
    mask_ref[...] = jnp.where(row == 0, by_mine.astype(jnp.float32) * (1.0 - from_x), from_x)


def outside_kernel(mine_ref, pair_ref, mask_ref, _, to_z_ref, to_x_ref, gate_ref):
    width = mine_ref.shape[1] - LANES
    total = mine_ref[...] + pair_ref[...]
    gate = total[: gate_ref.shape[0], width:]
    terms = total[:, :width]
    to_z_ref[:, :width] = (terms * mask_ref[0:1, 0:1]).astype(to_z_ref.dtype)
    to_z_ref[:, width:] = split(gate)
    odd = jnp.broadcast_to(odd_core(), (terms.shape[0], width // 2)) > 0
    half = jnp.where(odd, terms[:, width // 2 :], terms[:, : width // 2])
    to_x_ref[:, : width // 2] = (half * mask_ref[1:2, 0:1]).astype(to_x_ref.dtype)
    to_x_ref[:, width // 2 :] = split(gate)
    gate_ref[...] = gate


def chip_sum_kernel(mine_ref, x_ref, z_ref, gate_ref, *refs):
    *gates, halo_ref, _, out_ref, gate_out, halo_out = refs
    halo_out[...] = halo_ref[...]
    width = mine_ref.shape[1]
    odd = odd_core().astype(jnp.float32)
    half = width // 2
    from_x = x_ref[:, :half].astype(jnp.float32)
    out_ref[:, :half] = mine_ref[:, :half] + (from_x * (1.0 - odd) + z_ref[:, :half].astype(jnp.float32))
    out_ref[:, half:width] = mine_ref[:, half:] + (from_x * odd + z_ref[:, half:width].astype(jnp.float32))
    gate_out[...] = gate_ref[...] + unsplit(x_ref[:, half:])
    gate = unsplit(z_ref[:, width:])
    for ref in gates:
        gate = gate + ref[...]
    out_ref[:, width:] = jnp.concatenate([gate] * (mine_ref.shape[0] // gate.shape[0]), axis=0)


def self_back_kernel(
    query_ref, context_ref, halo_ref, weights_ref, grad_ref, *refs, block, groups, repeat
):
    query_grad_ref, key_low_ref, key_high_ref, rows_out, sems = refs[-5:]
    copies = []
    half = repeat * WINDOW
    for g in range(groups):
        rows = stack(query_ref, block * WINDOW, WINDOW, g, repeat)
        keys = joined(context_ref, halo_ref, block, g)
        values = joined(context_ref, halo_ref, block, groups + g)
        weights = weights_ref[g]
        grads = grad_ref[g, block * half : (block + 1) * half, :]
        grad_weights = dot(values, grads, NT)
        delta = jnp.sum(weights * grad_weights, axis=0, keepdims=True)
        grad_scores = (weights * (grad_weights - delta)).astype(jnp.bfloat16)
        grad_query = (dot(grad_scores, keys, TN) * SCALE).astype(jnp.bfloat16)
        for h in range(repeat):
            head = g * repeat + h
            rows_out[:, head * HEAD_DIM : (head + 1) * HEAD_DIM] = grad_query[h * WINDOW : (h + 1) * WINDOW]
        cols = slice(g * repeat * HEAD_DIM, (g + 1) * repeat * HEAD_DIM)
        copies.append(
            pltpu.make_async_copy(
                rows_out.at[:, cols], query_grad_ref.at[block * WINDOW : (block + 1) * WINDOW, cols], sems.at[g]
            )
        )
        copies[-1].start()
        grad_key = dot(grad_scores, rows, NN) * SCALE
        grad_value = dot(weights.astype(jnp.bfloat16), grads, NN)
        for index, terms in ((g, grad_key), (groups + g, grad_value)):
            cols = slice(index * HEAD_DIM, (index + 1) * HEAD_DIM)
            key_low_ref[:, cols] = terms[:WINDOW].astype(key_low_ref.dtype)
            key_high_ref[:, cols] = terms[WINDOW:]
    for copy in copies:
        copy.wait()


def gate_kernel(chip_ref, mine_ref, pair_ref, out_ref):
    width = mine_ref.shape[1] - LANES
    rows = out_ref.shape[0]
    out_ref[...] = chip_ref[...] + (mine_ref[:rows, width:] + pair_ref[:rows, width:])


def gate_grad_kernel(one_ref, other_ref, gate_ref, out_ref):
    rows, heads = one_ref.shape[0], out_ref.shape[1]
    total = one_ref[...] + other_ref[...]
    lane = lax.broadcasted_iota(jnp.int32, total.shape, 1)
    first = jnp.sum(jnp.where(lane < WINDOW, total, 0.0), axis=1, keepdims=True)
    second = jnp.sum(jnp.where(lane < WINDOW, 0.0, total), axis=1, keepdims=True)
    row = lax.broadcasted_iota(jnp.int32, (rows, heads), 0)
    head = lax.broadcasted_iota(jnp.int32, (rows, heads), 1)
    sums = jnp.where(head == 2 * row, first, 0.0) + jnp.where(head == 2 * row + 1, second, 0.0)
    sums = jnp.sum(sums, axis=0, keepdims=True)
    tanh = gate_ref[:, :heads]
    same = lax.broadcasted_iota(jnp.int32, tanh.shape, 0) == lax.broadcasted_iota(jnp.int32, tanh.shape, 1)
    tanh = jnp.sum(jnp.where(same, tanh, 0.0), axis=0, keepdims=True)
    out_ref[...] = (1.0 - tanh * tanh) * sums


def finish_kernel(
    off_ref, own_ref, mine_ref, pair_ref, low_ref, also_ref, high_ref, halo_ref, _,
    memory_ref, context_ref, *, tok_rows
):
    width = own_ref.shape[1]
    keep = flag(off_ref[0:1, 0:1] < tok_rows).astype(jnp.float32)
    total = own_ref[...] + (mine_ref[:, :width] + pair_ref[:, :width])
    memory_ref[...] = (total * keep).astype(memory_ref.dtype)
    more = jnp.where(lax.axis_index("seq") < lax.axis_size("seq") - 1, 1.0, 0.0)
    first = tok_rows - WINDOW
    context_ref[:first] = (low_ref[...] + also_ref[...]).astype(context_ref.dtype)
    context_ref[first:] = (high_ref[...] + halo_ref[...].astype(jnp.float32) * more).astype(context_ref.dtype)


def struct(shape, dtype):
    return jax.ShapeDtypeStruct(shape, dtype)


def call(
    name, kernel, out_shape, in_specs, scratch=(), out_specs=None, aliases=None, flops=10**6, moved=10**6
):
    return pl.pallas_call(
        kernel,
        out_shape=out_shape,
        in_specs=in_specs,
        out_specs=[VMEM] * len(out_shape) if out_specs is None else out_specs,
        scratch_shapes=scratch,
        input_output_aliases=aliases or {},
        compiler_params=pltpu.CompilerParams(vmem_limit_bytes=40 * 2**20),
        cost_estimate=pl.CostEstimate(flops=flops, bytes_accessed=moved, transcendentals=0),
        name=name,
    )


def on_device(queries, context, segment_start, memory, image_offset, cross_gate, out_grad):
    tok_rows, model = queries.shape[1:]
    width = context.shape[2]
    groups = width // 2 // HEAD_DIM
    heads = cross_gate.shape[0]
    repeat = heads // groups
    img = memory.shape[2]
    half = repeat * WINDOW
    seq, dp = lax.axis_size("seq"), lax.axis_size("dp")
    f32, bf16 = jnp.float32, jnp.bfloat16

    swaps = seq == 4 * GAP and dp == 2

    def send(value, where):
        return lax.ppermute(value, "seq", [(i, where(i)) for i in range(seq)])

    def send_all(value, where):
        pairs = [(s, d, *where(s, d)) for s in range(seq) for d in range(dp)]
        return lax.ppermute(value, ("seq", "dp"), [(s * dp + d, t * dp + e) for s, d, t, e in pairs])

    def send_near(value, step):
        if not swaps:
            return (send(value, lambda i: (i + step) % seq),)
        off_chip = lambda s, d: (s, d ^ 1) if s in (0, seq - 1) else (((s + 1) ^ 1) - 1, d)
        return send(value, lambda i: i ^ 1), send_all(value, off_chip)

    def merge(name, arrived, step, after):
        if len(arrived) == 1:
            return arrived[0]
        return call(name, functools.partial(near_kernel, step=step), [window], [VMEM] * 2 + [ANY])(*arrived, after)[0]

    def send_z(value, step):
        return send(value, lambda i: ((i if i % 2 == 0 else i ^ 2) + step * GAP) % seq)

    q, ctx, grad = queries[0], context[0], out_grad[0]
    gate_tanh = jnp.tanh(cross_gate)
    gate_rows = jnp.broadcast_to(gate_tanh[:, None], (heads, LANES))
    image = struct((img, width), bf16)
    window = struct((WINDOW, width), bf16)
    own = memory[0, 0]
    pair = send(own, lambda i: i ^ 1)
    pair_off = send(image_offset, lambda i: i ^ 1)
    tail = ctx[tok_rows - WINDOW :]
    chip, marked, chip_half, tail, off = call(
        "chip_image",
        functools.partial(chip_kernel, tok_rows=tok_rows),
        [image, struct((img, width + LANES), bf16), struct((img, width // 2), bf16), window, struct((8, LANES), jnp.int32)],
        [SMEM] * 2 + [VMEM] * 3,
    )(image_offset, pair_off, own, pair, tail)
    by_z = send_z(marked, 1)
    by_x = send(chip_half, lambda i: i ^ 2)
    halo = merge("halo", send_near(tail, 1), 1, chip)
    self_out, kept = [None, None], [None, None]

    def self_forward(block, after):
        self_out[block], kept[block] = call(
            f"self_forward_{block}",
            functools.partial(self_kernel, block=block, groups=groups, repeat=repeat),
            [struct((groups, HEAD_DIM, half), bf16), struct((groups, 2 * WINDOW, half), f32)],
            [VMEM] * 4 + [ANY],
            flops=10**6,
            moved=10**5,
        )(q, ctx, tail if block else halo, segment_start, after)

    self_forward(1, chip)
    arrived = call("arrived", join_kernel, [struct((img, width + LANES + width // 2), bf16)], [VMEM] * 2 + [ANY] * 2)(
        by_z, by_x, self_out[1], halo
    )[0]

    by_pair = send(arrived, lambda i: i ^ 1)
    self_forward(0, arrived)

    gate_shape = struct((heads * WINDOW // LANES, LANES), f32)
    grad_self, to_pair, in_chip, own_terms, masks = call(
        "cross",
        functools.partial(cross_kernel, groups=groups, repeat=repeat),
        [
            struct((groups, repeat * tok_rows, HEAD_DIM), bf16),
            struct((img, width + LANES), f32),
            struct((img, width), f32),
            struct((img, width), f32),
            struct((8, LANES), f32),
        ],
        [VMEM] * 9,
        scratch=[pltpu.VMEM((img, width), bf16)],
    )(off, gate_rows, *self_out, grad, own, chip, arrived, by_pair)
    from_pair = send(to_pair, lambda i: i ^ 1)

    def self_backward(block, after, late=None):
        return call(
            f"self_backward_{block}",
            functools.partial(self_back_kernel, block=block, groups=groups, repeat=repeat),
            [
                struct((tok_rows, model), bf16),
                struct((WINDOW, width), f32 if block else bf16),
                struct((WINDOW, width), f32),
            ],
            [VMEM] * 5 + [ANY] * (1 if late is None else 2),
            scratch=[pltpu.VMEM((WINDOW, model), bf16), pltpu.SemaphoreType.DMA((groups,))],
            out_specs=[ANY, VMEM, VMEM],
            aliases={5: 0} if block else None,
            flops=10**6,
            moved=10**5,
        )(q, ctx, tail if block else halo, kept[block], grad_self, after, *([] if late is None else [late]))

    query_grad, halo_terms, low = self_backward(0, to_pair)
    to_z, to_x, gate = call(
        "outside",
        outside_kernel,
        [struct((img, width + LANES), bf16), struct((img, width // 2 + LANES), bf16), gate_shape],
        [VMEM] * 3 + [ANY],
    )(to_pair, from_pair, masks, halo_terms)
    from_z = send_z(to_z, -1)
    from_x = send(to_x, lambda i: i ^ 2)
    gates = []
    if swaps:
        gates = [send_z(gate, 1), send_z(gate, 2)]
    query_grad, also, high = self_backward(1, query_grad, to_z)
    mine, gate, halo_terms = call(
        "chip_sum",
        chip_sum_kernel,
        [struct((img, width + LANES), f32), gate_shape, window],
        [VMEM] * (5 + len(gates)) + [ANY],
    )(in_chip, from_x, from_z, gate, *gates, halo_terms, high)
    other = send(mine, lambda i: i ^ 1)
    halo_back = merge("halo_back", send_near(halo_terms, -1), -1, mine)
    gate = call("gate_sum", gate_kernel, [gate_shape], [VMEM] * 3)(gate, mine, other)[0]
    memory_grad, context_grad = call(
        "finish",
        functools.partial(finish_kernel, tok_rows=tok_rows),
        [image, struct((tok_rows, width), bf16)],
        [VMEM] * 8 + [ANY],
    )(off, own_terms, mine, other, low, also, high, halo_back, gate)

    if not swaps:
        gate_total = lax.psum(to_pair[: gate_shape.shape[0], width:], ("seq", "dp"))
        gate_grad = (1.0 - gate_tanh * gate_tanh) * jnp.sum(gate_total.reshape(heads, WINDOW), axis=1)
        return (query_grad[None], context_grad[None], memory_grad[None, None], gate_grad)
    gate_grad = call("gate_grad", gate_grad_kernel, [struct((1, heads), f32)], [VMEM] * 3)(
        gate, send_all(gate, lambda s, d: (s, d ^ 1)), gate_rows
    )[0].reshape(heads)
    return (query_grad[None], context_grad[None], memory_grad[None, None], gate_grad)


def solution(mesh):
    placed = (
        P("dp", "seq", None),
        P("dp", "seq", None),
        P("dp", "seq"),
        P("dp", "seq", None, None),
        P("dp", "seq"),
        P(),
        P("dp", "seq", None),
    )
    return jax.shard_map(
        on_device,
        mesh=mesh,
        in_specs=placed,
        out_specs=(P("dp", "seq", None), P("dp", "seq", None), P("dp", "seq", None, None), P()),
        check_vma=False,
    )
```

```python
import functools
import math

import jax
import jax.numpy as jnp
from jax import lax
from jax.experimental import pallas as pl
from jax.experimental.pallas import tpu as pltpu
from jax.sharding import PartitionSpec as P

HEAD_DIM = 128
WINDOW = 64
GAP = 4
LANES = 128
MORE = 16
MARKS = 384
SCALE = 1.0 / math.sqrt(HEAD_DIM)

VMEM = pl.BlockSpec(memory_space=pltpu.VMEM)
ANY = pl.BlockSpec(memory_space=pl.ANY)
SMEM = pl.BlockSpec(memory_space=pltpu.SMEM)

NN = (((1,), (0,)), ((), ()))
NT = (((1,), (1,)), ((), ()))
TN = (((0,), (0,)), ((), ()))


def dot(a, b, dims):
    return lax.dot_general(a, b, dims, preferred_element_type=jnp.float32)


def stack(ref, first, rows, group, repeat):
    return jnp.concatenate(
        [
            ref[first : first + rows, (group * repeat + h) * HEAD_DIM : (group * repeat + h + 1) * HEAD_DIM]
            for h in range(repeat)
        ],
        axis=0,
    )


def part(ref, index):
    return ref[:, index * HEAD_DIM : (index + 1) * HEAD_DIM]


def softmax_rows(scores):
    top = jnp.max(scores, axis=0, keepdims=True)
    powers = jnp.exp(scores - top)
    return powers * (1.0 / jnp.sum(powers, axis=0, keepdims=True))


def self_mask(segment_ref, block, base):
    segment = segment_ref[0:1, block * WINDOW : (block + 1) * WINDOW]
    segment = jnp.concatenate([segment] * (LANES // WINDOW), axis=1)
    shape = (2 * WINDOW, LANES)
    key = lax.broadcasted_iota(jnp.int32, shape, 0)
    query = lax.broadcasted_iota(jnp.int32, shape, 1) % WINDOW
    key_pos = key + (base + (block - 1) * WINDOW)
    return (key >= query) & (key <= query + WINDOW) & (key_pos >= segment)


def self_weights(query_rows, keys, allowed):
    scores = dot(keys, query_rows, NT) * SCALE
    allowed = jnp.concatenate([allowed] * (scores.shape[1] // LANES), axis=1)
    return softmax_rows(jnp.where(allowed, scores, -1e30))


def joined(context_ref, halo_ref, block, index):
    own = context_ref[:, index * HEAD_DIM : (index + 1) * HEAD_DIM]
    if block == 0:
        return jnp.concatenate([part(halo_ref, index), own[:WINDOW]], axis=0)
    return own[(block - 1) * WINDOW : (block + 1) * WINDOW]


def odd_core():
    return flag(lax.axis_index("seq") % 2 == 1)


def flag(cond):
    return jnp.where(cond, 1, 0)


def choose(here, mine_ref, other_ref, out_ref, width=None):
    here = jnp.broadcast_to(here, out_ref.shape) > 0
    width = width or mine_ref.shape[1]
    mine, other = mine_ref[:, :width].astype(jnp.float32), other_ref[:, :width].astype(jnp.float32)
    out_ref[...] = jnp.where(here, mine, other).astype(out_ref.dtype)


def owner(owner_ref, row):
    return flag(owner_ref[row : row + 1, 0:1] > 0.5)


def chip_kernel(mine_ref, other_ref, out_ref, marked_ref, half_ref, owner_ref):
    width = out_ref.shape[1]
    mine, other = mine_ref[0:1, width : width + 1], other_ref[0:1, width : width + 1]
    mine, other = mine.astype(jnp.float32), other.astype(jnp.float32)
    choose(flag(mine > 0.5), mine_ref, other_ref, out_ref, width)
    marked_ref[:, :width] = out_ref[...]
    owns = jnp.maximum(mine, other)
    marked_ref[:, width:] = jnp.broadcast_to(owns, (out_ref.shape[0], LANES)).astype(marked_ref.dtype)
    choose(odd_core(), out_ref.at[:, width // 2 :], out_ref.at[:, : width // 2], half_ref)
    row = lax.broadcasted_iota(jnp.int32, owner_ref.shape, 0)
    owner_ref[...] = jnp.where(row == 0, mine, other)


def join_kernel(z_ref, x_ref, _, __, out_ref):
    out_ref[:, : z_ref.shape[1]] = z_ref[...]
    out_ref[:, z_ref.shape[1] :] = x_ref[...]


def near_kernel(chip_ref, other_ref, _, out_ref, *, step):
    first = chip_ref.shape[0] - out_ref.shape[0]
    choose(flag(lax.axis_index("seq") % 2 == (1 if step > 0 else 0)), chip_ref.at[first:], other_ref.at[first:], out_ref)


def self_kernel(query_ref, context_ref, halo_ref, segment_ref, _, out_ref, weights_ref, *, block, groups, repeat):
    tok_rows = query_ref.shape[0]
    base = lax.axis_index("seq") * tok_rows
    allowed = self_mask(segment_ref, block, base)
    for g in range(groups):
        rows = stack(query_ref, block * WINDOW, WINDOW, g, repeat)
        weights = self_weights(rows, joined(context_ref, halo_ref, block, g), allowed)
        weights_ref[g] = weights
        values = joined(context_ref, halo_ref, block, groups + g)
        out_ref[g] = dot(values, weights.astype(jnp.bfloat16), TN).astype(jnp.bfloat16)


def split(values):
    high = values.astype(jnp.bfloat16)
    rest = values - high.astype(jnp.float32)
    middle = rest.astype(jnp.bfloat16)
    low = (rest - middle.astype(jnp.float32)).astype(jnp.bfloat16)
    return jnp.concatenate([high, middle, low, jnp.zeros_like(low)], axis=0)


def unsplit(parts):
    parts = parts.astype(jnp.float32)
    rows = parts.shape[0] // 4
    return parts[:rows] + (parts[rows : 2 * rows] + parts[2 * rows : 3 * rows])


def cross_kernel(
    off_ref, owner_ref, gate_ref, self_0_ref, self_1_ref, grad_ref, own_ref, chip_ref, mine_ref, pair_ref,
    scores_ref, to_pair_ref, in_chip_ref, own_terms_ref, mask_ref, prev, *, groups, repeat
):
    tok_rows, width = grad_ref.shape[0], chip_ref.shape[1]
    img = own_ref.shape[0]
    shard = lax.axis_index("seq")
    off = off_ref[0:1, 0:1]
    is_owner, pair_owner = owner(owner_ref, 0), owner(owner_ref, 1)
    upper, odd = flag(shard % GAP >= 2), flag(shard % 2 == 1)
    from_chip = odd * pair_owner
    from_x = upper * (1 - (is_owner | pair_owner))
    from_z = flag(shard >= GAP) * (1 - (from_chip | from_x))
    has_prev = from_chip | from_x | from_z
    marked = width + LANES
    by_mine = flag(mine_ref[0:1, width : width + 1].astype(jnp.float32) > 0.5)
    choose(by_mine, mine_ref, pair_ref, prev, width)
    for first in (0, 1):
        cols = prev.at[:, first * width // 2 : (first + 1) * width // 2]
        mine = from_x * flag(odd == first)
        choose(mine, mine_ref.at[:, marked:], cols, cols)
        choose(from_x - mine, pair_ref.at[:, marked:], cols, cols)
    choose(from_chip, chip_ref, prev, prev)

    half = repeat * WINDOW
    rows = tok_rows * repeat
    lane = lax.broadcasted_iota(jnp.int32, (1, rows), 1)
    lane_tok = (lane // half) * WINDOW + lane % WINDOW
    own_from = jnp.minimum(off, tok_rows)
    has_from = own_from * (1 - has_prev)
    from_chip, from_x, from_z = (here.astype(jnp.float32) for here in (from_chip, from_x, from_z))
    use_own = lane_tok >= own_from
    has_lane = lane_tok >= has_from
    row_tok = lax.broadcasted_iota(jnp.int32, (WINDOW, HEAD_DIM), 0)

    gate_rows = []
    for g in range(groups):
        keys = jnp.concatenate([part(prev, g), part(own_ref, g)], axis=0)
        values = jnp.concatenate([part(prev, groups + g), part(own_ref, groups + g)], axis=0)
        out_t = jnp.concatenate([self_0_ref[g], self_1_ref[g]], axis=1)
        scores = dot(keys, out_t, NN)
        weights = softmax_rows(jnp.where(use_own, scores[img:], scores[:img]) * SCALE)
        narrow = weights.astype(jnp.bfloat16)
        grad_rows, cross_rows = [], []
        for block in range(tok_rows // WINDOW):
            has_rows = row_tok + block * WINDOW >= has_from
            for h in range(repeat):
                head = g * repeat + h
                tile = grad_ref[
                    block * WINDOW : (block + 1) * WINDOW, head * HEAD_DIM : (head + 1) * HEAD_DIM
                ]
                grad_rows.append(tile)
                factor = jnp.where(has_rows, gate_ref[head : head + 1, :], 0.0)
                cross_rows.append((tile.astype(jnp.float32) * factor).astype(jnp.bfloat16))
        grad_rows = jnp.concatenate(grad_rows, axis=0)
        cross_rows = jnp.concatenate(cross_rows, axis=0)
        plain = dot(values, grad_rows, NT)
        plain = jnp.where(use_own, plain[img:], plain[:img])
        gate_row = jnp.sum(narrow.astype(jnp.float32) * plain, axis=0, keepdims=True)
        gate_row = jnp.where(has_lane, gate_row, 0.0)
        gate_row = gate_row[:, :half] + gate_row[:, half:]
        gate_rows.extend(gate_row[:, i * LANES : (i + 1) * LANES] for i in range(half // LANES))
        grad_weights = dot(values, cross_rows, NT)
        grad_weights = jnp.where(use_own, grad_weights[img:], grad_weights[:img])
        delta = jnp.sum(weights * grad_weights, axis=0, keepdims=True)
        grad_scores = weights * (grad_weights - delta)
        scores_j = jnp.concatenate(
            [jnp.where(use_own, 0.0, grad_scores), jnp.where(use_own, grad_scores, 0.0)], axis=0
        ).astype(jnp.bfloat16)
        narrow_j = jnp.concatenate(
            [jnp.where(use_own, 0.0, weights), jnp.where(use_own, weights, 0.0)], axis=0
        ).astype(jnp.bfloat16)
        grad_key = dot(scores_j, out_t, NT) * SCALE
        grad_value = dot(narrow_j, cross_rows, NN)
        scores_ref[g] = scores_j
        for index, terms in ((g, grad_key), (groups + g, grad_value)):
            cols = slice(index * HEAD_DIM, (index + 1) * HEAD_DIM)
            own_terms_ref[:, cols] = terms[img:]
            to_pair_ref[:, cols] = terms[:img] * (from_x + from_z)
            in_chip_ref[:, cols] = terms[:img] * from_chip
    gate = jnp.concatenate(gate_rows, axis=0)
    to_pair_ref[:, width:] = jnp.concatenate([gate] * (img // gate.shape[0]), axis=0)
    row = lax.broadcasted_iota(jnp.int32, mask_ref.shape, 0)
    mask_ref[...] = jnp.where(row == 0, by_mine.astype(jnp.float32) * (1.0 - from_x), from_x)


def cross_query_kernel(scores_ref, grad_ref, own_ref, prev, _, grad_self_ref, *, groups, repeat):
    for g in range(groups):
        keys = jnp.concatenate([part(prev, g), part(own_ref, g)], axis=0)
        grad_query = dot(scores_ref[g], keys, TN) * SCALE
        for block in range(grad_ref.shape[0] // WINDOW):
            rows = slice(block * repeat * WINDOW, (block + 1) * repeat * WINDOW)
            grad_rows = stack(grad_ref, block * WINDOW, WINDOW, g, repeat).astype(jnp.float32)
            grad_self_ref[g, rows, :] = (grad_rows + grad_query[rows]).astype(jnp.bfloat16)


def outside_kernel(mine_ref, pair_ref, mask_ref, _, to_z_ref, to_x_ref, gate_ref):
    width = mine_ref.shape[1] - LANES
    total = mine_ref[...] + pair_ref[...]
    gate = total[: gate_ref.shape[0], width:]
    terms = total[:, :width]
    to_z_ref[:, :width] = (terms * mask_ref[0:1, 0:1]).astype(to_z_ref.dtype)
    to_z_ref[:, width:] = split(gate)
    odd = jnp.broadcast_to(odd_core(), (terms.shape[0], width // 2)) > 0
    half = jnp.where(odd, terms[:, width // 2 :], terms[:, : width // 2])
    to_x_ref[:, : width // 2] = (half * mask_ref[1:2, 0:1]).astype(to_x_ref.dtype)
    to_x_ref[:, width // 2 :] = split(gate)
    gate_ref[...] = gate


def chip_sum_kernel(mine_ref, x_ref, z_ref, gate_ref, *refs):
    *gates, _, out_ref, gate_out = refs
    width = mine_ref.shape[1]
    odd = odd_core().astype(jnp.float32)
    half = width // 2
    from_x = x_ref[:, :half].astype(jnp.float32)
    out_ref[:, :half] = mine_ref[:, :half] + (from_x * (1.0 - odd) + z_ref[:, :half].astype(jnp.float32))
    out_ref[:, half:width] = mine_ref[:, half:] + (from_x * odd + z_ref[:, half:width].astype(jnp.float32))
    gate_out[...] = gate_ref[...] + unsplit(x_ref[:, half:])
    gate = unsplit(z_ref[:, width:])
    for ref in gates:
        gate = gate + ref[...]
    out_ref[:, width:] = jnp.concatenate([gate] * (mine_ref.shape[0] // gate.shape[0]), axis=0)


def self_back_kernel(
    query_ref, context_ref, halo_ref, weights_ref, grad_ref, *refs, block, groups, repeat
):
    query_grad_ref, key_low_ref, key_high_ref, rows_out, sems = refs[-5:]
    copies = []
    half = repeat * WINDOW
    for g in range(groups):
        rows = stack(query_ref, block * WINDOW, WINDOW, g, repeat)
        keys = joined(context_ref, halo_ref, block, g)
        values = joined(context_ref, halo_ref, block, groups + g)
        weights = weights_ref[g]
        grads = grad_ref[g, block * half : (block + 1) * half, :]
        grad_weights = dot(values, grads, NT)
        delta = jnp.sum(weights * grad_weights, axis=0, keepdims=True)
        grad_scores = (weights * (grad_weights - delta)).astype(jnp.bfloat16)
        grad_query = (dot(grad_scores, keys, TN) * SCALE).astype(jnp.bfloat16)
        for h in range(repeat):
            head = g * repeat + h
            rows_out[:, head * HEAD_DIM : (head + 1) * HEAD_DIM] = grad_query[h * WINDOW : (h + 1) * WINDOW]
        cols = slice(g * repeat * HEAD_DIM, (g + 1) * repeat * HEAD_DIM)
        copies.append(
            pltpu.make_async_copy(
                rows_out.at[:, cols], query_grad_ref.at[block * WINDOW : (block + 1) * WINDOW, cols], sems.at[g]
            )
        )
        copies[-1].start()
        grad_key = dot(grad_scores, rows, NN) * SCALE
        grad_value = dot(weights.astype(jnp.bfloat16), grads, NN)
        for index, terms in ((g, grad_key), (groups + g, grad_value)):
            cols = slice(index * HEAD_DIM, (index + 1) * HEAD_DIM)
            key_low_ref[:, cols] = terms[:WINDOW].astype(key_low_ref.dtype)
            key_high_ref[:, cols] = terms[WINDOW:]
    for copy in copies:
        copy.wait()


def gate_kernel(chip_ref, mine_ref, pair_ref, out_ref):
    width = mine_ref.shape[1] - LANES
    rows = out_ref.shape[0]
    out_ref[...] = chip_ref[...] + (mine_ref[:rows, width:] + pair_ref[:rows, width:])


def gate_grad(total, gate_ref):
    rows, heads = total.shape[0], gate_ref.shape[0]
    lane = lax.broadcasted_iota(jnp.int32, total.shape, 1)
    first = jnp.sum(jnp.where(lane < WINDOW, total, 0.0), axis=1, keepdims=True)
    second = jnp.sum(jnp.where(lane < WINDOW, 0.0, total), axis=1, keepdims=True)
    row = lax.broadcasted_iota(jnp.int32, (rows, heads), 0)
    head = lax.broadcasted_iota(jnp.int32, (rows, heads), 1)
    sums = jnp.where(head == 2 * row, first, 0.0) + jnp.where(head == 2 * row + 1, second, 0.0)
    sums = jnp.sum(sums, axis=0, keepdims=True)
    tanh = gate_ref[:, :heads]
    same = lax.broadcasted_iota(jnp.int32, tanh.shape, 0) == lax.broadcasted_iota(jnp.int32, tanh.shape, 1)
    tanh = jnp.sum(jnp.where(same, tanh, 0.0), axis=0, keepdims=True)
    return (1.0 - tanh * tanh) * sums


def finish_kernel(
    owner_ref, own_ref, mine_ref, pair_ref, low_ref, also_ref, high_ref, halo_ref, gate_ref, *refs, tok_rows
):
    *far_refs, tanh_ref, memory_ref, context_ref, gate_out = refs
    width = own_ref.shape[1]
    keep = owner(owner_ref, 0).astype(jnp.float32)
    total = own_ref[...] + (mine_ref[:, :width] + pair_ref[:, :width])
    memory_ref[...] = (total * keep).astype(memory_ref.dtype)
    more = jnp.where(lax.axis_index("seq") < lax.axis_size("seq") - 1, 1.0, 0.0)
    first = tok_rows - WINDOW
    context_ref[:first] = (low_ref[...] + also_ref[...]).astype(context_ref.dtype)
    context_ref[first:] = (high_ref[...] + halo_ref[...].astype(jnp.float32) * more).astype(context_ref.dtype)
    gate = gate_ref[...]
    for ref in far_refs:
        gate = gate + ref[...]
    gate_out[...] = gate_grad(gate, tanh_ref)


def struct(shape, dtype):
    return jax.ShapeDtypeStruct(shape, dtype)


def call(
    name, kernel, out_shape, in_specs, scratch=(), out_specs=None, aliases=None, flops=1000, moved=1000
):
    return pl.pallas_call(
        kernel,
        out_shape=out_shape,
        in_specs=in_specs,
        out_specs=[VMEM] * len(out_shape) if out_specs is None else out_specs,
        scratch_shapes=scratch,
        input_output_aliases=aliases or {},
        compiler_params=pltpu.CompilerParams(vmem_limit_bytes=40 * 2**20),
        cost_estimate=pl.CostEstimate(flops=flops, bytes_accessed=moved, transcendentals=0),
        name=name,
    )


def on_device(queries, context, segment_start, memory, image_offset, cross_gate, out_grad):
    tok_rows, model = queries.shape[1:]
    width = context.shape[2]
    groups = width // 2 // HEAD_DIM
    heads = cross_gate.shape[0]
    repeat = heads // groups
    img = memory.shape[2]
    half = repeat * WINDOW
    seq, dp = lax.axis_size("seq"), lax.axis_size("dp")
    f32, bf16 = jnp.float32, jnp.bfloat16

    swaps = seq == 4 * GAP and dp == 2

    def send(value, where):
        return lax.ppermute(value, "seq", [(i, where(i)) for i in range(seq)])

    def send_all(value, where):
        pairs = [(s, d, *where(s, d)) for s in range(seq) for d in range(dp)]
        return lax.ppermute(value, ("seq", "dp"), [(s * dp + d, t * dp + e) for s, d, t, e in pairs])

    def send_near(value, step):
        if not swaps:
            return (send(value, lambda i: (i + step) % seq),)
        off_chip = lambda s, d: (s, d ^ 1) if s in (0, seq - 1) else (((s + 1) ^ 1) - 1, d)
        return send(value, lambda i: i ^ 1), send_all(value, off_chip)

    def merge(name, arrived, step, after):
        if len(arrived) == 1:
            return arrived[0][arrived[0].shape[0] - WINDOW :]
        return call(name, functools.partial(near_kernel, step=step), [window], [VMEM] * 2 + [ANY])(*arrived, after)[0]

    def send_z(value, step, straight=False):
        def where(i):
            wraps = not 0 <= i + step * GAP < seq
            return ((i if i % 2 == 0 or (straight and wraps) else i ^ 2) + step * GAP) % seq

        return send(value, where)

    q, ctx, grad = queries[0], context[0], out_grad[0]
    gate_tanh = jnp.tanh(cross_gate)
    gate_rows = jnp.broadcast_to(gate_tanh[:, None], (heads, LANES))
    image = struct((img, width), bf16)
    window = struct((WINDOW, width), bf16)
    own = memory[0, 0]
    is_owner = (image_offset < tok_rows).astype(bf16)
    own = jnp.concatenate([own, jnp.broadcast_to(is_owner, (img, MARKS))], axis=1)
    pair = send(own, lambda i: i ^ 1)
    tail = ctx[tok_rows - WINDOW - MORE :]
    halos = send_near(tail, 1)
    chip, marked, chip_half, owners = call(
        "chip_image",
        chip_kernel,
        [image, struct((img, width + LANES), bf16), struct((img, width // 2), bf16), struct((8, LANES), f32)],
        [VMEM] * 2,
    )(own, pair)
    off = jnp.broadcast_to(image_offset, (8, LANES))
    by_z = send_z(marked, 1, True)
    by_x = send(chip_half, lambda i: i ^ 2)
    self_out, kept = [None, None], [None, None]

    def self_forward(block, after):
        self_out[block], kept[block] = call(
            f"self_forward_{block}",
            functools.partial(self_kernel, block=block, groups=groups, repeat=repeat),
            [struct((groups, HEAD_DIM, half), bf16), struct((groups, 2 * WINDOW, half), f32)],
            [VMEM] * 4 + [ANY],
            flops=10**6,
            moved=10**5,
        )(q, ctx, tail if block else halo, segment_start, after)

    self_forward(1, chip)
    halo = merge("halo", halos, 1, self_out[1])
    arrived = call("arrived", join_kernel, [struct((img, width + LANES + width // 2), bf16)], [VMEM] * 2 + [ANY] * 2)(
        by_z, by_x, self_out[1], halo
    )[0]

    by_pair = send(arrived, lambda i: i ^ 1)
    self_forward(0, arrived)

    gate_shape = struct((heads * WINDOW // LANES, LANES), f32)
    scores, to_pair, in_chip, own_terms, masks, prev = call(
        "cross",
        functools.partial(cross_kernel, groups=groups, repeat=repeat),
        [
            struct((groups, 2 * img, repeat * tok_rows), bf16),
            struct((img, width + LANES), f32),
            struct((img, width), f32),
            struct((img, width), f32),
            struct((8, LANES), f32),
            image,
        ],
        [VMEM] * 10,
    )(off, owners, gate_rows, *self_out, grad, own, chip, arrived, by_pair)
    from_pair = send(to_pair, lambda i: i ^ 1)
    grad_self = call(
        "cross_query",
        functools.partial(cross_query_kernel, groups=groups, repeat=repeat),
        [struct((groups, repeat * tok_rows, HEAD_DIM), bf16)],
        [VMEM] * 4 + [ANY],
    )(scores, grad, own, prev, to_pair)[0]

    def self_backward(block, after, late=None):
        return call(
            f"self_backward_{block}",
            functools.partial(self_back_kernel, block=block, groups=groups, repeat=repeat),
            [
                struct((tok_rows, model), bf16),
                struct((WINDOW, width), f32 if block else bf16),
                struct((WINDOW, width), f32),
            ],
            [VMEM] * 5 + [ANY] * (1 if late is None else 2),
            scratch=[pltpu.VMEM((WINDOW, model), bf16), pltpu.SemaphoreType.DMA((groups,))],
            out_specs=[ANY, VMEM, VMEM],
            aliases={5: 0} if block else None,
            flops=10**6,
            moved=10**5,
        )(q, ctx, tail if block else halo, kept[block], grad_self, after, *([] if late is None else [late]))

    to_z, to_x, gate = call(
        "outside",
        outside_kernel,
        [struct((img, width + LANES), bf16), struct((img, width // 2 + LANES), bf16), gate_shape],
        [VMEM] * 3 + [ANY],
    )(to_pair, from_pair, masks, grad_self)
    from_z = send_z(to_z, -1)
    from_x = send(to_x, lambda i: i ^ 2)
    gates = []
    if swaps:
        gates = [send_z(gate, 1), send_z(gate, 2)]
    query_grad, halo_terms, low = self_backward(0, to_z)
    mine, gate = call(
        "chip_sum",
        chip_sum_kernel,
        [struct((img, width + LANES), f32), gate_shape],
        [VMEM] * (4 + len(gates)) + [ANY],
    )(in_chip, from_x, from_z, gate, *gates, low)
    other = send(mine, lambda i: i ^ 1)
    halo_back = send_near(halo_terms, -1)
    query_grad, also, high = self_backward(1, query_grad, mine)
    halo_back = merge("halo_back", halo_back, -1, high)
    gate = call("gate_sum", gate_kernel, [gate_shape], [VMEM] * 3)(gate, mine, other)[0]
    if swaps:
        far = [send_all(gate, lambda s, d: (s, d ^ 1))]
    else:
        gate = lax.psum(to_pair[: gate_shape.shape[0], width:], ("seq", "dp"))
        far = []
    memory_grad, context_grad, cross_gate_grad = call(
        "finish",
        functools.partial(finish_kernel, tok_rows=tok_rows),
        [image, struct((tok_rows, width), bf16), struct((1, heads), f32)],
        [VMEM] * (10 + len(far)),
    )(owners, own_terms, mine, other, low, also, high, halo_back, gate, *far, gate_rows)
    return (query_grad[None], context_grad[None], memory_grad[None, None], cross_gate_grad.reshape(heads))


def solution(mesh):
    placed = (
        P("dp", "seq", None),
        P("dp", "seq", None),
        P("dp", "seq"),
        P("dp", "seq", None, None),
        P("dp", "seq"),
        P(),
        P("dp", "seq", None),
    )
    return jax.shard_map(
        on_device,
        mesh=mesh,
        in_specs=placed,
        out_specs=(P("dp", "seq", None), P("dp", "seq", None), P("dp", "seq", None, None), P()),
        check_vma=False,
    )
```

```python
import functools
import math

import jax
import jax.numpy as jnp
from jax import lax
from jax.experimental import pallas as pl
from jax.experimental.pallas import tpu as pltpu
from jax.sharding import PartitionSpec as P

HEAD_DIM = 128
WINDOW = 64
GAP = 4
LANES = 128
MORE = 16
MARKS = 384
SCALE = 1.0 / math.sqrt(HEAD_DIM)

VMEM = pl.BlockSpec(memory_space=pltpu.VMEM)
ANY = pl.BlockSpec(memory_space=pl.ANY)
SMEM = pl.BlockSpec(memory_space=pltpu.SMEM)

NN = (((1,), (0,)), ((), ()))
NT = (((1,), (1,)), ((), ()))
TN = (((0,), (0,)), ((), ()))


def dot(a, b, dims):
    return lax.dot_general(a, b, dims, preferred_element_type=jnp.float32)


def stack(ref, first, rows, group, repeat):
    return jnp.concatenate(
        [
            ref[first : first + rows, (group * repeat + h) * HEAD_DIM : (group * repeat + h + 1) * HEAD_DIM]
            for h in range(repeat)
        ],
        axis=0,
    )


def part(ref, index):
    return ref[:, index * HEAD_DIM : (index + 1) * HEAD_DIM]


def softmax_rows(scores):
    top = jnp.max(scores, axis=0, keepdims=True)
    powers = jnp.exp(scores - top)
    return powers * (1.0 / jnp.sum(powers, axis=0, keepdims=True))


def self_mask(segment_ref, block, base):
    segment = segment_ref[0:1, block * WINDOW : (block + 1) * WINDOW]
    segment = jnp.concatenate([segment] * (LANES // WINDOW), axis=1)
    shape = (2 * WINDOW, LANES)
    key = lax.broadcasted_iota(jnp.int32, shape, 0)
    query = lax.broadcasted_iota(jnp.int32, shape, 1) % WINDOW
    key_pos = key + (base + (block - 1) * WINDOW)
    return (key >= query) & (key <= query + WINDOW) & (key_pos >= segment)


def self_weights(scores, allowed):
    allowed = jnp.concatenate([allowed] * (scores.shape[1] // LANES), axis=1)
    return softmax_rows(jnp.where(allowed, scores * SCALE, -1e30))


def joined(context_ref, halo_ref, block, index):
    own = context_ref[:, index * HEAD_DIM : (index + 1) * HEAD_DIM]
    if block == 0:
        return jnp.concatenate([part(halo_ref, index), own[:WINDOW]], axis=0)
    return own[(block - 1) * WINDOW : (block + 1) * WINDOW]


def odd_core():
    return flag(lax.axis_index("seq") % 2 == 1)


def flag(cond):
    return jnp.where(cond, 1, 0)


def choose(here, mine_ref, other_ref, out_ref, width=None):
    here = jnp.broadcast_to(here, out_ref.shape) > 0
    width = width or mine_ref.shape[1]
    mine, other = mine_ref[:, :width].astype(jnp.float32), other_ref[:, :width].astype(jnp.float32)
    out_ref[...] = jnp.where(here, mine, other).astype(out_ref.dtype)


def owner(owner_ref, row):
    return flag(owner_ref[row : row + 1, 0:1] > 0.5)


def chip_kernel(mine_ref, other_ref, out_ref, marked_ref, half_ref, owner_ref):
    width = out_ref.shape[1]
    mine, other = mine_ref[0:1, width : width + 1], other_ref[0:1, width : width + 1]
    mine, other = mine.astype(jnp.float32), other.astype(jnp.float32)
    choose(flag(mine > 0.5), mine_ref, other_ref, out_ref, width)
    marked_ref[:, :width] = out_ref[...]
    owns = jnp.maximum(mine, other)
    marked_ref[:, width:] = jnp.broadcast_to(owns, (out_ref.shape[0], LANES)).astype(marked_ref.dtype)
    choose(odd_core(), out_ref.at[:, width // 2 :], out_ref.at[:, : width // 2], half_ref)
    row = lax.broadcasted_iota(jnp.int32, owner_ref.shape, 0)
    owner_ref[...] = jnp.where(row == 0, mine, other)


def join_kernel(z_ref, x_ref, _, __, out_ref):
    out_ref[:, : z_ref.shape[1]] = z_ref[...]
    out_ref[:, z_ref.shape[1] :] = x_ref[...]


def near_kernel(chip_ref, other_ref, _, out_ref, *, step):
    first = chip_ref.shape[0] - out_ref.shape[0]
    choose(flag(lax.axis_index("seq") % 2 == (1 if step > 0 else 0)), chip_ref.at[first:], other_ref.at[first:], out_ref)


def self_kernel(query_ref, context_ref, halo_ref, segment_ref, _, out_ref, weights_ref, *, block, groups, repeat):
    tok_rows = query_ref.shape[0]
    base = lax.axis_index("seq") * tok_rows
    allowed = self_mask(segment_ref, block, base)
    scores = [
        dot(joined(context_ref, halo_ref, block, g), stack(query_ref, block * WINDOW, WINDOW, g, repeat), NT)
        for g in range(groups)
    ]
    weights = [self_weights(scores[g], allowed) for g in range(groups)]
    for g in range(groups):
        weights_ref[g] = weights[g]
        values = joined(context_ref, halo_ref, block, groups + g)
        out_ref[g] = dot(values, weights[g].astype(jnp.bfloat16), TN).astype(jnp.bfloat16)


def split(values):
    high = values.astype(jnp.bfloat16)
    rest = values - high.astype(jnp.float32)
    middle = rest.astype(jnp.bfloat16)
    low = (rest - middle.astype(jnp.float32)).astype(jnp.bfloat16)
    return jnp.concatenate([high, middle, low, jnp.zeros_like(low)], axis=0)


def unsplit(parts):
    parts = parts.astype(jnp.float32)
    rows = parts.shape[0] // 4
    return parts[:rows] + (parts[rows : 2 * rows] + parts[2 * rows : 3 * rows])


def cross_kernel(
    off_ref, owner_ref, gate_ref, self_0_ref, self_1_ref, grad_ref, own_ref, chip_ref, mine_ref, pair_ref,
    scores_ref, to_pair_ref, in_chip_ref, own_terms_ref, mask_ref, prev, *, groups, repeat, step=2
):
    tok_rows, width = grad_ref.shape[0], chip_ref.shape[1]
    img = own_ref.shape[0]
    shard = lax.axis_index("seq")
    off = off_ref[0:1, 0:1]
    is_owner, pair_owner = owner(owner_ref, 0), owner(owner_ref, 1)
    upper, odd = flag(shard % GAP >= 2), flag(shard % 2 == 1)
    from_chip = odd * pair_owner
    from_x = upper * (1 - (is_owner | pair_owner))
    from_z = flag(shard >= GAP) * (1 - (from_chip | from_x))
    has_prev = from_chip | from_x | from_z
    marked = width + LANES
    by_mine = flag(mine_ref[0:1, width : width + 1].astype(jnp.float32) > 0.5)
    choose(by_mine, mine_ref, pair_ref, prev, width)
    for first in (0, 1):
        cols = prev.at[:, first * width // 2 : (first + 1) * width // 2]
        mine = from_x * flag(odd == first)
        choose(mine, mine_ref.at[:, marked:], cols, cols)
        choose(from_x - mine, pair_ref.at[:, marked:], cols, cols)
    choose(from_chip, chip_ref, prev, prev)

    half = repeat * WINDOW
    rows = tok_rows * repeat
    lane = lax.broadcasted_iota(jnp.int32, (1, rows), 1)
    lane_tok = (lane // half) * WINDOW + lane % WINDOW
    own_from = jnp.minimum(off, tok_rows)
    has_from = own_from * (1 - has_prev)
    from_chip, from_x, from_z = (here.astype(jnp.float32) for here in (from_chip, from_x, from_z))
    use_own = lane_tok >= own_from
    has_lane = lane_tok >= has_from
    row_tok = lax.broadcasted_iota(jnp.int32, (WINDOW, HEAD_DIM), 0)

    def pick(joint):
        return jnp.where(use_own, joint[img:], joint[:img])

    def join(values):
        zero = jnp.zeros_like(values)
        both = [jnp.where(use_own, zero, values), jnp.where(use_own, values, zero)]
        return jnp.concatenate(both, axis=0).astype(jnp.bfloat16)

    blocks = range(tok_rows // WINDOW)
    gate_rows = []
    for first in range(0, groups, step):
        every = range(first, first + step)
        keys = {g: jnp.concatenate([part(prev, g), part(own_ref, g)], axis=0) for g in every}
        values = {g: jnp.concatenate([part(prev, groups + g), part(own_ref, groups + g)], axis=0) for g in every}
        out_t = {g: jnp.concatenate([self_0_ref[g], self_1_ref[g]], axis=1) for g in every}
        scores = {g: dot(keys[g], out_t[g], NN) for g in every}
        plain, cross_rows, grad_weights = {}, {}, {}
        for g in every:
            tiles = [stack(grad_ref, block * WINDOW, WINDOW, g, repeat) for block in blocks]
            plain[g] = dot(values[g], jnp.concatenate(tiles, axis=0), NT)
            scaled = []
            for block in blocks:
                has_rows = row_tok + block * WINDOW >= has_from
                factors = [
                    jnp.where(has_rows, gate_ref[g * repeat + h : g * repeat + h + 1, :], 0.0) for h in range(repeat)
                ]
                scaled.append(
                    (tiles[block].astype(jnp.float32) * jnp.concatenate(factors, axis=0)).astype(jnp.bfloat16)
                )
            cross_rows[g] = jnp.concatenate(scaled, axis=0)
            grad_weights[g] = dot(values[g], cross_rows[g], NT)
        weights = {g: softmax_rows(pick(scores[g]) * SCALE) for g in every}
        score_terms = {}
        for g in every:
            gate_row = jnp.sum(weights[g].astype(jnp.bfloat16).astype(jnp.float32) * pick(plain[g]), axis=0, keepdims=True)
            gate_row = jnp.where(has_lane, gate_row, 0.0)
            gate_row = gate_row[:, :half] + gate_row[:, half:]
            gate_rows.extend(gate_row[:, i * LANES : (i + 1) * LANES] for i in range(half // LANES))
            weight_terms = pick(grad_weights[g])
            delta = jnp.sum(weights[g] * weight_terms, axis=0, keepdims=True)
            score_terms[g] = join(weights[g] * (weight_terms - delta))
            scores_ref[g] = score_terms[g]
        for g in every:
            grad_key = dot(score_terms[g], out_t[g], NT) * SCALE
            grad_value = dot(join(weights[g]), cross_rows[g], NN)
            for index, terms in ((g, grad_key), (groups + g, grad_value)):
                cols = slice(index * HEAD_DIM, (index + 1) * HEAD_DIM)
                own_terms_ref[:, cols] = terms[img:]
                to_pair_ref[:, cols] = terms[:img] * (from_x + from_z)
                in_chip_ref[:, cols] = terms[:img] * from_chip
    gate = jnp.concatenate(gate_rows, axis=0)
    to_pair_ref[:, width:] = jnp.concatenate([gate] * (img // gate.shape[0]), axis=0)
    row = lax.broadcasted_iota(jnp.int32, mask_ref.shape, 0)
    mask_ref[...] = jnp.where(row == 0, by_mine.astype(jnp.float32) * (1.0 - from_x), from_x)


def cross_query_kernel(scores_ref, grad_ref, own_ref, prev, _, grad_self_ref, *, groups, repeat):
    for g in range(groups):
        keys = jnp.concatenate([part(prev, g), part(own_ref, g)], axis=0)
        grad_query = dot(scores_ref[g], keys, TN) * SCALE
        for block in range(grad_ref.shape[0] // WINDOW):
            rows = slice(block * repeat * WINDOW, (block + 1) * repeat * WINDOW)
            grad_rows = stack(grad_ref, block * WINDOW, WINDOW, g, repeat).astype(jnp.float32)
            grad_self_ref[g, rows, :] = (grad_rows + grad_query[rows]).astype(jnp.bfloat16)


def outside_kernel(mine_ref, pair_ref, mask_ref, _, to_z_ref, to_x_ref, gate_ref):
    width = mine_ref.shape[1] - LANES
    total = mine_ref[...] + pair_ref[...]
    gate = total[: gate_ref.shape[0], width:]
    terms = total[:, :width]
    to_z_ref[:, :width] = (terms * mask_ref[0:1, 0:1]).astype(to_z_ref.dtype)
    to_z_ref[:, width:] = split(gate)
    odd = jnp.broadcast_to(odd_core(), (terms.shape[0], width // 2)) > 0
    half = jnp.where(odd, terms[:, width // 2 :], terms[:, : width // 2])
    to_x_ref[:, : width // 2] = (half * mask_ref[1:2, 0:1]).astype(to_x_ref.dtype)
    to_x_ref[:, width // 2 :] = split(gate)
    gate_ref[...] = gate


def chip_sum_kernel(mine_ref, x_ref, z_ref, gate_ref, *refs):
    *gates, _, out_ref, gate_out, to_pair_ref = refs
    width = mine_ref.shape[1]
    odd = odd_core().astype(jnp.float32)
    half = width // 2
    from_x = x_ref[:, :half].astype(jnp.float32)
    first = mine_ref[:, :half] + (from_x * (1.0 - odd) + z_ref[:, :half].astype(jnp.float32))
    second = mine_ref[:, half:] + (from_x * odd + z_ref[:, half:width].astype(jnp.float32))
    for cols, terms in ((slice(0, half), first), (slice(half, width), second)):
        out_ref[:, cols] = terms
        to_pair_ref[:, cols] = terms.astype(to_pair_ref.dtype)
    gate = unsplit(z_ref[:, width:])
    for ref in gates:
        gate = gate + ref[...]
    gate_out[...] = gate_ref[...] + unsplit(x_ref[:, half:]) + gate
    to_pair_ref[:, width:] = split(gate)


def self_back_kernel(
    query_ref, context_ref, halo_ref, weights_ref, grad_ref, *refs, block, groups, repeat
):
    query_grad_ref, key_low_ref, key_high_ref, rows_out, sems = refs[-5:]
    half = repeat * WINDOW
    every = range(groups)
    rows = [stack(query_ref, block * WINDOW, WINDOW, g, repeat) for g in every]
    keys = [joined(context_ref, halo_ref, block, g) for g in every]
    grads = [grad_ref[g, block * half : (block + 1) * half, :] for g in every]
    grad_weights = [dot(joined(context_ref, halo_ref, block, groups + g), grads[g], NT) for g in every]
    grad_scores = []
    for g in every:
        delta = jnp.sum(weights_ref[g] * grad_weights[g], axis=0, keepdims=True)
        grad_scores.append((weights_ref[g] * (grad_weights[g] - delta)).astype(jnp.bfloat16))
    copies = []
    for g in every:
        grad_query = (dot(grad_scores[g], keys[g], TN) * SCALE).astype(jnp.bfloat16)
        for h in range(repeat):
            head = g * repeat + h
            rows_out[:, head * HEAD_DIM : (head + 1) * HEAD_DIM] = grad_query[h * WINDOW : (h + 1) * WINDOW]
        cols = slice(g * repeat * HEAD_DIM, (g + 1) * repeat * HEAD_DIM)
        copies.append(
            pltpu.make_async_copy(
                rows_out.at[:, cols], query_grad_ref.at[block * WINDOW : (block + 1) * WINDOW, cols], sems.at[g]
            )
        )
        copies[-1].start()
    for g in every:
        grad_key = dot(grad_scores[g], rows[g], NN) * SCALE
        grad_value = dot(weights_ref[g].astype(jnp.bfloat16), grads[g], NN)
        for index, terms in ((g, grad_key), (groups + g, grad_value)):
            cols = slice(index * HEAD_DIM, (index + 1) * HEAD_DIM)
            key_low_ref[key_low_ref.shape[0] - WINDOW :, cols] = terms[:WINDOW].astype(key_low_ref.dtype)
            key_high_ref[:, cols] = terms[WINDOW:]
    for copy in copies:
        copy.wait()


def gate_kernel(mine_ref, pair_ref, out_ref):
    out_ref[...] = mine_ref[...] + unsplit(pair_ref[:, pair_ref.shape[1] - LANES :])


def gate_grad(total, gate_ref):
    rows, heads = total.shape[0], gate_ref.shape[0]
    lane = lax.broadcasted_iota(jnp.int32, total.shape, 1)
    first = jnp.sum(jnp.where(lane < WINDOW, total, 0.0), axis=1, keepdims=True)
    second = jnp.sum(jnp.where(lane < WINDOW, 0.0, total), axis=1, keepdims=True)
    row = lax.broadcasted_iota(jnp.int32, (rows, heads), 0)
    head = lax.broadcasted_iota(jnp.int32, (rows, heads), 1)
    sums = jnp.where(head == 2 * row, first, 0.0) + jnp.where(head == 2 * row + 1, second, 0.0)
    sums = jnp.sum(sums, axis=0, keepdims=True)
    tanh = gate_ref[:, :heads]
    same = lax.broadcasted_iota(jnp.int32, tanh.shape, 0) == lax.broadcasted_iota(jnp.int32, tanh.shape, 1)
    tanh = jnp.sum(jnp.where(same, tanh, 0.0), axis=0, keepdims=True)
    return (1.0 - tanh * tanh) * sums


def finish_kernel(
    owner_ref, own_ref, mine_ref, pair_ref, low_ref, also_ref, high_ref, halo_ref, gate_ref, *refs, tok_rows
):
    *far_refs, tanh_ref, memory_ref, context_ref, gate_out = refs
    width = mine_ref.shape[1]
    keep = owner(owner_ref, 0).astype(jnp.float32)
    total = own_ref[...] + (mine_ref[...] + pair_ref[:, :width].astype(jnp.float32))
    memory_ref[...] = (total * keep).astype(memory_ref.dtype)
    more = jnp.where(lax.axis_index("seq") < lax.axis_size("seq") - 1, 1.0, 0.0)
    first = tok_rows - WINDOW
    context_ref[:first] = (low_ref[...] + also_ref[...]).astype(context_ref.dtype)
    context_ref[first:] = (high_ref[...] + halo_ref[...].astype(jnp.float32) * more).astype(context_ref.dtype)
    gate = gate_ref[...]
    for ref in far_refs:
        gate = gate + ref[...]
    gate_out[...] = gate_grad(gate, tanh_ref)


def struct(shape, dtype):
    return jax.ShapeDtypeStruct(shape, dtype)


def call(
    name, kernel, out_shape, in_specs, scratch=(), out_specs=None, aliases=None, flops=1000, moved=1000
):
    return pl.pallas_call(
        kernel,
        out_shape=out_shape,
        in_specs=in_specs,
        out_specs=[VMEM] * len(out_shape) if out_specs is None else out_specs,
        scratch_shapes=scratch,
        input_output_aliases=aliases or {},
        compiler_params=pltpu.CompilerParams(vmem_limit_bytes=40 * 2**20),
        cost_estimate=pl.CostEstimate(flops=flops, bytes_accessed=moved, transcendentals=0),
        name=name,
    )


def on_device(queries, context, segment_start, memory, image_offset, cross_gate, out_grad):
    tok_rows, model = queries.shape[1:]
    width = context.shape[2]
    groups = width // 2 // HEAD_DIM
    heads = cross_gate.shape[0]
    repeat = heads // groups
    img = memory.shape[2]
    half = repeat * WINDOW
    seq, dp = lax.axis_size("seq"), lax.axis_size("dp")
    f32, bf16 = jnp.float32, jnp.bfloat16

    swaps = seq == 4 * GAP and dp == 2

    def send(value, where):
        return lax.ppermute(value, "seq", [(i, where(i)) for i in range(seq)])

    def send_all(value, where):
        pairs = [(s, d, *where(s, d)) for s in range(seq) for d in range(dp)]
        return lax.ppermute(value, ("seq", "dp"), [(s * dp + d, t * dp + e) for s, d, t, e in pairs])

    def send_near(value, step):
        if not swaps:
            return (send(value, lambda i: (i + step) % seq),)
        off_chip = lambda s, d: (s, d ^ 1) if s in (0, seq - 1) else (((s + 1) ^ 1) - 1, d)
        return send(value, lambda i: i ^ 1), send_all(value, off_chip)

    def merge(name, arrived, step, after):
        if len(arrived) == 1:
            return arrived[0][arrived[0].shape[0] - WINDOW :]
        return call(name, functools.partial(near_kernel, step=step), [window], [VMEM] * 2 + [ANY])(*arrived, after)[0]

    def send_z(value, step, straight=False):
        def where(i):
            wraps = not 0 <= i + step * GAP < seq
            return ((i if i % 2 == 0 or (straight and wraps) else i ^ 2) + step * GAP) % seq

        return send(value, where)

    q, ctx, grad = queries[0], context[0], out_grad[0]
    gate_tanh = jnp.tanh(cross_gate)
    gate_rows = jnp.broadcast_to(gate_tanh[:, None], (heads, LANES))
    image = struct((img, width), bf16)
    window = struct((WINDOW, width), bf16)
    own = memory[0, 0]
    is_owner = (image_offset < tok_rows).astype(bf16)
    own = jnp.concatenate([own, jnp.broadcast_to(is_owner, (img, MARKS))], axis=1)
    pair = send(own, lambda i: i ^ 1)
    tail = ctx[tok_rows - WINDOW - MORE :]
    halos = send_near(tail, 1)
    chip, marked, chip_half, owners = call(
        "chip_image",
        chip_kernel,
        [image, struct((img, width + LANES), bf16), struct((img, width // 2), bf16), struct((8, LANES), f32)],
        [VMEM] * 2,
    )(own, pair)
    off = jnp.broadcast_to(image_offset, (8, LANES))
    by_z = send_z(marked, 1, True)
    by_x = send(chip_half, lambda i: i ^ 2)
    self_out, kept = [None, None], [None, None]

    def self_forward(block, after):
        self_out[block], kept[block] = call(
            f"self_forward_{block}",
            functools.partial(self_kernel, block=block, groups=groups, repeat=repeat),
            [struct((groups, HEAD_DIM, half), bf16), struct((groups, 2 * WINDOW, half), f32)],
            [VMEM] * 4 + [ANY],
            flops=10**6,
            moved=10**5,
        )(q, ctx, tail if block else halo, segment_start, after)

    self_forward(1, chip)
    halo = merge("halo", halos, 1, self_out[1])
    arrived = call("arrived", join_kernel, [struct((img, width + LANES + width // 2), bf16)], [VMEM] * 2 + [ANY] * 2)(
        by_z, by_x, self_out[1], halo
    )[0]

    by_pair = send(arrived, lambda i: i ^ 1)
    self_forward(0, arrived)

    gate_shape = struct((heads * WINDOW // LANES, LANES), f32)
    scores, to_pair, in_chip, own_terms, masks, prev = call(
        "cross",
        functools.partial(cross_kernel, groups=groups, repeat=repeat),
        [
            struct((groups, 2 * img, repeat * tok_rows), bf16),
            struct((img, width + LANES), f32),
            struct((img, width), f32),
            struct((img, width), f32),
            struct((8, LANES), f32),
            image,
        ],
        [VMEM] * 10,
    )(off, owners, gate_rows, *self_out, grad, own, chip, arrived, by_pair)
    from_pair = send(to_pair, lambda i: i ^ 1)
    grad_self = call(
        "cross_query",
        functools.partial(cross_query_kernel, groups=groups, repeat=repeat),
        [struct((groups, repeat * tok_rows, HEAD_DIM), bf16)],
        [VMEM] * 4 + [ANY],
    )(scores, grad, own, prev, to_pair)[0]

    def self_backward(block, after, late=None):
        return call(
            f"self_backward_{block}",
            functools.partial(self_back_kernel, block=block, groups=groups, repeat=repeat),
            [
                struct((tok_rows, model), bf16),
                struct((WINDOW, width), f32) if block else struct((WINDOW + MORE, width), bf16),
                struct((WINDOW, width), f32),
            ],
            [VMEM] * 5 + [ANY] * (1 if late is None else 2),
            scratch=[pltpu.VMEM((WINDOW, model), bf16), pltpu.SemaphoreType.DMA((groups,))],
            out_specs=[ANY, VMEM, VMEM],
            aliases={5: 0} if block else None,
            flops=10**6,
            moved=10**5,
        )(q, ctx, tail if block else halo, kept[block], grad_self, after, *([] if late is None else [late]))

    to_z, to_x, gate = call(
        "outside",
        outside_kernel,
        [struct((img, width + LANES), bf16), struct((img, width // 2 + LANES), bf16), gate_shape],
        [VMEM] * 3 + [ANY],
    )(to_pair, from_pair, masks, grad_self)
    from_z = send_z(to_z, -1)
    from_x = send(to_x, lambda i: i ^ 2)
    gates = []
    if swaps:
        gates = [send_z(gate, 1), send_z(gate, 2)]
    query_grad, halo_terms, low = self_backward(0, to_z)
    mine, gate, to_chip = call(
        "chip_sum",
        chip_sum_kernel,
        [struct((img, width), f32), gate_shape, struct((img, width + LANES), bf16)],
        [VMEM] * (4 + len(gates)) + [ANY],
    )(in_chip, from_x, from_z, gate, *gates, low)
    other = send(to_chip, lambda i: i ^ 1)
    halo_back = send_near(halo_terms, -1)
    query_grad, also, high = self_backward(1, query_grad, mine)
    halo_back = merge("halo_back", halo_back, -1, high)
    gate = call("gate_sum", gate_kernel, [gate_shape], [VMEM] * 2)(gate, other)[0]
    if swaps:
        far = [send_all(gate, lambda s, d: (s, d ^ 1))]
    else:
        gate = lax.psum(to_pair[: gate_shape.shape[0], width:], ("seq", "dp"))
        far = []
    memory_grad, context_grad, cross_gate_grad = call(
        "finish",
        functools.partial(finish_kernel, tok_rows=tok_rows),
        [image, struct((tok_rows, width), bf16), struct((1, heads), f32)],
        [VMEM] * (10 + len(far)),
    )(owners, own_terms, mine, other, low, also, high, halo_back, gate, *far, gate_rows)
    return (query_grad[None], context_grad[None], memory_grad[None, None], cross_gate_grad.reshape(heads))


def solution(mesh):
    placed = (
        P("dp", "seq", None),
        P("dp", "seq", None),
        P("dp", "seq"),
        P("dp", "seq", None, None),
        P("dp", "seq"),
        P(),
        P("dp", "seq", None),
    )
    return jax.shard_map(
        on_device,
        mesh=mesh,
        in_specs=placed,
        out_specs=(P("dp", "seq", None), P("dp", "seq", None), P("dp", "seq", None, None), P()),
        check_vma=False,
    )
```

```python
import functools
import math

import jax
import jax.numpy as jnp
from jax import lax
from jax.experimental import pallas as pl
from jax.experimental.pallas import tpu as pltpu
from jax.sharding import PartitionSpec as P

HEAD_DIM = 128
WINDOW = 64
GAP = 4
LANES = 128
WIDE = 2
MORE = 16
MARKS = 384
SCALE = 1.0 / math.sqrt(HEAD_DIM)

VMEM = pl.BlockSpec(memory_space=pltpu.VMEM)
ANY = pl.BlockSpec(memory_space=pl.ANY)
SMEM = pl.BlockSpec(memory_space=pltpu.SMEM)

NN = (((1,), (0,)), ((), ()))
NT = (((1,), (1,)), ((), ()))
TN = (((0,), (0,)), ((), ()))


def dot(a, b, dims):
    return lax.dot_general(a, b, dims, preferred_element_type=jnp.float32)


def stack(ref, first, rows, group, repeat):
    return jnp.concatenate(
        [
            ref[first : first + rows, (group * repeat + h) * HEAD_DIM : (group * repeat + h + 1) * HEAD_DIM]
            for h in range(repeat)
        ],
        axis=0,
    )


def part(ref, index):
    return ref[:, index * HEAD_DIM : (index + 1) * HEAD_DIM]


def softmax_rows(scores):
    top = jnp.max(scores, axis=0, keepdims=True)
    powers = jnp.exp(scores - top)
    return powers * (1.0 / jnp.sum(powers, axis=0, keepdims=True))


def self_mask(segment_ref, block, base):
    segment = segment_ref[0:1, block * WINDOW : (block + 1) * WINDOW]
    segment = jnp.concatenate([segment] * (LANES // WINDOW), axis=1)
    shape = (2 * WINDOW, LANES)
    key = lax.broadcasted_iota(jnp.int32, shape, 0)
    query = lax.broadcasted_iota(jnp.int32, shape, 1) % WINDOW
    key_pos = key + (base + (block - 1) * WINDOW)
    return (key >= query) & (key <= query + WINDOW) & (key_pos >= segment)


def self_weights(scores, allowed):
    allowed = jnp.concatenate([allowed] * (scores.shape[1] // LANES), axis=1)
    return softmax_rows(jnp.where(allowed, scores * SCALE, -1e30))


def joined(context_ref, halo_ref, block, index):
    own = context_ref[:, index * HEAD_DIM : (index + 1) * HEAD_DIM]
    if block == 0:
        return jnp.concatenate([part(halo_ref, index), own[:WINDOW]], axis=0)
    return own[(block - 1) * WINDOW : (block + 1) * WINDOW]


def odd_core():
    return flag(lax.axis_index("seq") % 2 == 1)


def flag(cond):
    return jnp.where(cond, 1, 0)


def choose(here, mine_ref, other_ref, out_ref, width=None):
    here = jnp.broadcast_to(here, out_ref.shape) > 0
    width = width or mine_ref.shape[1]
    mine, other = mine_ref[:, :width].astype(jnp.float32), other_ref[:, :width].astype(jnp.float32)
    out_ref[...] = jnp.where(here, mine, other).astype(out_ref.dtype)


def owner(owner_ref, row):
    return flag(owner_ref[row : row + 1, 0:1] > 0.5)


def chip_kernel(mine_ref, other_ref, out_ref, marked_ref, half_ref, owner_ref):
    width = out_ref.shape[1]
    mine, other = mine_ref[0:1, width : width + 1], other_ref[0:1, width : width + 1]
    mine, other = mine.astype(jnp.float32), other.astype(jnp.float32)
    choose(flag(mine > 0.5), mine_ref, other_ref, out_ref, width)
    marked_ref[:, :width] = out_ref[...]
    owns = jnp.maximum(mine, other)
    marked_ref[:, width:] = jnp.broadcast_to(owns, (out_ref.shape[0], LANES)).astype(marked_ref.dtype)
    choose(odd_core(), out_ref.at[:, width // 2 :], out_ref.at[:, : width // 2], half_ref)
    row = lax.broadcasted_iota(jnp.int32, owner_ref.shape, 0)
    owner_ref[...] = jnp.where(row == 0, mine, other)


def join_kernel(z_ref, x_ref, _, __, out_ref):
    out_ref[:, : z_ref.shape[1]] = z_ref[...]
    out_ref[:, z_ref.shape[1] :] = x_ref[...]


def near_kernel(chip_ref, other_ref, _, out_ref, *, step):
    first = chip_ref.shape[0] - out_ref.shape[0]
    choose(flag(lax.axis_index("seq") % 2 == (1 if step > 0 else 0)), chip_ref.at[first:], other_ref.at[first:], out_ref)


def self_kernel(query_ref, context_ref, halo_ref, segment_ref, _, out_ref, weights_ref, *, block, groups, repeat):
    tok_rows = query_ref.shape[0]
    base = lax.axis_index("seq") * tok_rows
    allowed = self_mask(segment_ref, block, base)
    scores = [
        dot(joined(context_ref, halo_ref, block, g), stack(query_ref, block * WINDOW, WINDOW, g, repeat), NT)
        for g in range(groups)
    ]
    weights = [self_weights(scores[g], allowed) for g in range(groups)]
    for g in range(groups):
        weights_ref[g] = weights[g]
        values = joined(context_ref, halo_ref, block, groups + g)
        out_ref[g] = dot(values, weights[g].astype(jnp.bfloat16), TN).astype(jnp.bfloat16)


def split(values):
    high = values.astype(jnp.bfloat16)
    rest = values - high.astype(jnp.float32)
    middle = rest.astype(jnp.bfloat16)
    low = (rest - middle.astype(jnp.float32)).astype(jnp.bfloat16)
    return jnp.concatenate([high, middle, low, jnp.zeros_like(low)], axis=0)


def unsplit(parts):
    parts = parts.astype(jnp.float32)
    rows = parts.shape[0] // 4
    return parts[:rows] + (parts[rows : 2 * rows] + parts[2 * rows : 3 * rows])


def cross_kernel(
    off_ref, owner_ref, gate_ref, self_0_ref, self_1_ref, grad_ref, own_ref, chip_ref, mine_ref, pair_ref,
    scores_ref, to_pair_ref, to_x_ref, in_chip_ref, own_terms_ref, mask_ref, prev, *, groups, repeat, step=2
):
    tok_rows, width = grad_ref.shape[0], chip_ref.shape[1]
    img = own_ref.shape[0]
    shard = lax.axis_index("seq")
    off = off_ref[0:1, 0:1]
    is_owner, pair_owner = owner(owner_ref, 0), owner(owner_ref, 1)
    upper, odd = flag(shard % GAP >= 2), flag(shard % 2 == 1)
    from_chip = odd * pair_owner
    from_x = upper * (1 - (is_owner | pair_owner))
    from_z = flag(shard >= GAP) * (1 - (from_chip | from_x))
    has_prev = from_chip | from_x | from_z
    marked = width + LANES
    by_mine = flag(mine_ref[0:1, width : width + 1].astype(jnp.float32) > 0.5)
    choose(by_mine, mine_ref, pair_ref, prev, width)
    for first in (0, 1):
        cols = prev.at[:, first * width // 2 : (first + 1) * width // 2]
        mine = from_x * flag(odd == first)
        choose(mine, mine_ref.at[:, marked:], cols, cols)
        choose(from_x - mine, pair_ref.at[:, marked:], cols, cols)
    choose(from_chip, chip_ref, prev, prev)

    half = repeat * WINDOW
    rows = tok_rows * repeat
    lane = lax.broadcasted_iota(jnp.int32, (1, rows), 1)
    lane_tok = (lane // half) * WINDOW + lane % WINDOW
    own_from = jnp.minimum(off, tok_rows)
    has_from = own_from * (1 - has_prev)
    from_chip, from_x, from_z = (here.astype(jnp.float32) for here in (from_chip, from_x, from_z))
    use_own = lane_tok >= own_from
    has_lane = lane_tok >= has_from
    row_tok = lax.broadcasted_iota(jnp.int32, (WINDOW, HEAD_DIM), 0)

    def pick(joint):
        return jnp.where(use_own, joint[img:], joint[:img])

    def join(values):
        zero = jnp.zeros_like(values)
        both = [jnp.where(use_own, zero, values), jnp.where(use_own, values, zero)]
        return jnp.concatenate(both, axis=0).astype(jnp.bfloat16)

    blocks = range(tok_rows // WINDOW)
    gate_rows = []
    for first in range(0, groups, step):
        every = range(first, first + step)
        keys = {g: jnp.concatenate([part(prev, g), part(own_ref, g)], axis=0) for g in every}
        values = {g: jnp.concatenate([part(prev, groups + g), part(own_ref, groups + g)], axis=0) for g in every}
        out_t = {g: jnp.concatenate([self_0_ref[g], self_1_ref[g]], axis=1) for g in every}
        scores = {g: dot(keys[g], out_t[g], NN) for g in every}
        plain, cross_rows, grad_weights = {}, {}, {}
        for g in every:
            tiles = [stack(grad_ref, block * WINDOW, WINDOW, g, repeat) for block in blocks]
            plain[g] = dot(values[g], jnp.concatenate(tiles, axis=0), NT)
            scaled = []
            for block in blocks:
                has_rows = row_tok + block * WINDOW >= has_from
                factors = [
                    jnp.where(has_rows, gate_ref[g * repeat + h : g * repeat + h + 1, :], 0.0) for h in range(repeat)
                ]
                scaled.append(
                    (tiles[block].astype(jnp.float32) * jnp.concatenate(factors, axis=0)).astype(jnp.bfloat16)
                )
            cross_rows[g] = jnp.concatenate(scaled, axis=0)
            grad_weights[g] = dot(values[g], cross_rows[g], NT)
        weights = {g: softmax_rows(pick(scores[g]) * SCALE) for g in every}
        score_terms = {}
        for g in every:
            gate_row = jnp.sum(weights[g].astype(jnp.bfloat16).astype(jnp.float32) * pick(plain[g]), axis=0, keepdims=True)
            gate_row = jnp.where(has_lane, gate_row, 0.0)
            gate_row = gate_row[:, :half] + gate_row[:, half:]
            gate_rows.extend(gate_row[:, i * LANES : (i + 1) * LANES] for i in range(half // LANES))
            weight_terms = pick(grad_weights[g])
            delta = jnp.sum(weights[g] * weight_terms, axis=0, keepdims=True)
            score_terms[g] = join(weights[g] * (weight_terms - delta))
            scores_ref[g] = score_terms[g]
        for g in every:
            grad_key = dot(score_terms[g], out_t[g], NT) * SCALE
            grad_value = dot(join(weights[g]), cross_rows[g], NN)
            for index, terms in ((g, grad_key), (groups + g, grad_value)):
                cols = slice(index * HEAD_DIM, (index + 1) * HEAD_DIM)
                own_terms_ref[:, cols] = terms[img:]
                to_pair_ref[:, cols] = terms[:img] * from_z
                to_x_ref[:, cols] = (terms[:img] * from_x).astype(to_x_ref.dtype)
                in_chip_ref[:, cols] = terms[:img] * from_chip
    gate = jnp.concatenate(gate_rows, axis=0)
    to_pair_ref[:, width:] = jnp.concatenate([gate] * (img // gate.shape[0]), axis=0)
    to_x_ref[:, width:] = jnp.concatenate([split(gate)] * (to_x_ref.shape[1] // LANES - width // LANES), axis=1)
    row = lax.broadcasted_iota(jnp.int32, mask_ref.shape, 0)
    mask_ref[...] = jnp.where(row == 0, by_mine.astype(jnp.float32) * (1.0 - from_x), from_x)


def cross_query_kernel(scores_ref, grad_ref, own_ref, prev, _, grad_self_ref, *, groups, repeat):
    for g in range(groups):
        keys = jnp.concatenate([part(prev, g), part(own_ref, g)], axis=0)
        grad_query = dot(scores_ref[g], keys, TN) * SCALE
        for block in range(grad_ref.shape[0] // WINDOW):
            rows = slice(block * repeat * WINDOW, (block + 1) * repeat * WINDOW)
            grad_rows = stack(grad_ref, block * WINDOW, WINDOW, g, repeat).astype(jnp.float32)
            grad_self_ref[g, rows, :] = (grad_rows + grad_query[rows]).astype(jnp.bfloat16)


def outside_kernel(mine_ref, pair_ref, mask_ref, _, to_z_ref, gate_ref):
    width = mine_ref.shape[1] - LANES
    total = mine_ref[...] + pair_ref[...]
    gate = total[: gate_ref.shape[0], width:]
    to_z_ref[:, :width] = (total[:, :width] * mask_ref[0:1, 0:1]).astype(to_z_ref.dtype)
    to_z_ref[:, width:] = split(gate)
    gate_ref[...] = gate


def chip_sum_kernel(mine_ref, x_ref, z_ref, gate_ref, *refs):
    *gates, _, out_ref, gate_out, to_pair_ref = refs
    width = mine_ref.shape[1]
    terms = mine_ref[...] + (x_ref[:, :width].astype(jnp.float32) + z_ref[:, :width].astype(jnp.float32))
    out_ref[...] = terms
    to_pair_ref[:, :width] = terms.astype(to_pair_ref.dtype)
    gate = unsplit(z_ref[:, width:]) + unsplit(x_ref[:, width : width + LANES])
    for ref in gates:
        gate = gate + ref[...]
    gate_out[...] = gate_ref[...] + gate
    to_pair_ref[:, width:] = split(gate)


def self_back_kernel(
    query_ref, context_ref, halo_ref, weights_ref, grad_ref, *refs, block, groups, repeat
):
    query_grad_ref, key_low_ref, key_high_ref, rows_out, sems = refs[-5:]
    half = repeat * WINDOW
    every = range(groups)
    rows = [stack(query_ref, block * WINDOW, WINDOW, g, repeat) for g in every]
    keys = [joined(context_ref, halo_ref, block, g) for g in every]
    grads = [grad_ref[g, block * half : (block + 1) * half, :] for g in every]
    grad_weights = [dot(joined(context_ref, halo_ref, block, groups + g), grads[g], NT) for g in every]
    grad_scores = []
    for g in every:
        delta = jnp.sum(weights_ref[g] * grad_weights[g], axis=0, keepdims=True)
        grad_scores.append((weights_ref[g] * (grad_weights[g] - delta)).astype(jnp.bfloat16))
    copies = []
    for g in every:
        grad_query = (dot(grad_scores[g], keys[g], TN) * SCALE).astype(jnp.bfloat16)
        for h in range(repeat):
            head = g * repeat + h
            rows_out[:, head * HEAD_DIM : (head + 1) * HEAD_DIM] = grad_query[h * WINDOW : (h + 1) * WINDOW]
        cols = slice(g * repeat * HEAD_DIM, (g + 1) * repeat * HEAD_DIM)
        copies.append(
            pltpu.make_async_copy(
                rows_out.at[:, cols], query_grad_ref.at[block * WINDOW : (block + 1) * WINDOW, cols], sems.at[g]
            )
        )
        copies[-1].start()
    for g in every:
        grad_key = dot(grad_scores[g], rows[g], NN) * SCALE
        grad_value = dot(weights_ref[g].astype(jnp.bfloat16), grads[g], NN)
        for index, terms in ((g, grad_key), (groups + g, grad_value)):
            cols = slice(index * HEAD_DIM, (index + 1) * HEAD_DIM)
            key_low_ref[key_low_ref.shape[0] - WINDOW :, cols] = terms[:WINDOW].astype(key_low_ref.dtype)
            key_high_ref[:, cols] = terms[WINDOW:]
    for copy in copies:
        copy.wait()


def gate_kernel(mine_ref, pair_ref, out_ref):
    out_ref[...] = mine_ref[...] + unsplit(pair_ref[:, pair_ref.shape[1] - LANES :])


def gate_grad(total, gate_ref):
    rows, heads = total.shape[0], gate_ref.shape[0]
    lane = lax.broadcasted_iota(jnp.int32, total.shape, 1)
    first = jnp.sum(jnp.where(lane < WINDOW, total, 0.0), axis=1, keepdims=True)
    second = jnp.sum(jnp.where(lane < WINDOW, 0.0, total), axis=1, keepdims=True)
    row = lax.broadcasted_iota(jnp.int32, (rows, heads), 0)
    head = lax.broadcasted_iota(jnp.int32, (rows, heads), 1)
    sums = jnp.where(head == 2 * row, first, 0.0) + jnp.where(head == 2 * row + 1, second, 0.0)
    sums = jnp.sum(sums, axis=0, keepdims=True)
    tanh = gate_ref[:, :heads]
    same = lax.broadcasted_iota(jnp.int32, tanh.shape, 0) == lax.broadcasted_iota(jnp.int32, tanh.shape, 1)
    tanh = jnp.sum(jnp.where(same, tanh, 0.0), axis=0, keepdims=True)
    return (1.0 - tanh * tanh) * sums


def finish_kernel(
    owner_ref, own_ref, mine_ref, pair_ref, low_ref, also_ref, high_ref, halo_ref, gate_ref, *refs, tok_rows
):
    *far_refs, tanh_ref, memory_ref, context_ref, gate_out = refs
    width = mine_ref.shape[1]
    keep = owner(owner_ref, 0).astype(jnp.float32)
    total = own_ref[...] + (mine_ref[...] + pair_ref[:, :width].astype(jnp.float32))
    memory_ref[...] = (total * keep).astype(memory_ref.dtype)
    more = jnp.where(lax.axis_index("seq") < lax.axis_size("seq") - 1, 1.0, 0.0)
    first = tok_rows - WINDOW
    context_ref[:first] = (low_ref[...] + also_ref[...]).astype(context_ref.dtype)
    context_ref[first:] = (high_ref[...] + halo_ref[...].astype(jnp.float32) * more).astype(context_ref.dtype)
    gate = gate_ref[...]
    for ref in far_refs:
        gate = gate + ref[...]
    gate_out[...] = gate_grad(gate, tanh_ref)


def struct(shape, dtype):
    return jax.ShapeDtypeStruct(shape, dtype)


def call(
    name, kernel, out_shape, in_specs, scratch=(), out_specs=None, aliases=None, flops=1000, moved=1000
):
    return pl.pallas_call(
        kernel,
        out_shape=out_shape,
        in_specs=in_specs,
        out_specs=[VMEM] * len(out_shape) if out_specs is None else out_specs,
        scratch_shapes=scratch,
        input_output_aliases=aliases or {},
        compiler_params=pltpu.CompilerParams(vmem_limit_bytes=40 * 2**20),
        cost_estimate=pl.CostEstimate(flops=flops, bytes_accessed=moved, transcendentals=0),
        name=name,
    )


def on_device(queries, context, segment_start, memory, image_offset, cross_gate, out_grad):
    tok_rows, model = queries.shape[1:]
    width = context.shape[2]
    groups = width // 2 // HEAD_DIM
    heads = cross_gate.shape[0]
    repeat = heads // groups
    img = memory.shape[2]
    half = repeat * WINDOW
    seq, dp = lax.axis_size("seq"), lax.axis_size("dp")
    f32, bf16 = jnp.float32, jnp.bfloat16

    swaps = seq == 4 * GAP and dp == 2

    def send(value, where):
        return lax.ppermute(value, "seq", [(i, where(i)) for i in range(seq)])

    def send_all(value, where):
        pairs = [(s, d, *where(s, d)) for s in range(seq) for d in range(dp)]
        return lax.ppermute(value, ("seq", "dp"), [(s * dp + d, t * dp + e) for s, d, t, e in pairs])

    def send_near(value, step):
        if not swaps:
            return (send(value, lambda i: (i + step) % seq),)
        off_chip = lambda s, d: (s, d ^ 1) if s in (0, seq - 1) else (((s + 1) ^ 1) - 1, d)
        return send(value, lambda i: i ^ 1), send_all(value, off_chip)

    def merge(name, arrived, step, after):
        if len(arrived) == 1:
            return arrived[0][arrived[0].shape[0] - WINDOW :]
        return call(name, functools.partial(near_kernel, step=step), [window], [VMEM] * 2 + [ANY])(*arrived, after)[0]

    def send_z(value, step, straight=False):
        def where(i):
            wraps = not 0 <= i + step * GAP < seq
            return ((i if i % 2 == 0 or (straight and wraps) else i ^ 2) + step * GAP) % seq

        return send(value, where)

    q, ctx, grad = queries[0], context[0], out_grad[0]
    gate_tanh = jnp.tanh(cross_gate)
    gate_rows = jnp.broadcast_to(gate_tanh[:, None], (heads, LANES))
    image = struct((img, width), bf16)
    window = struct((WINDOW, width), bf16)
    own = memory[0, 0]
    is_owner = (image_offset < tok_rows).astype(bf16)
    own = jnp.concatenate([own, jnp.broadcast_to(is_owner, (img, MARKS))], axis=1)
    pair = send(own, lambda i: i ^ 1)
    tail = ctx[tok_rows - WINDOW - MORE :]
    halos = send_near(tail, 1)
    chip, marked, chip_half, owners = call(
        "chip_image",
        chip_kernel,
        [image, struct((img, width + LANES), bf16), struct((img, width // 2), bf16), struct((8, LANES), f32)],
        [VMEM] * 2,
    )(own, pair)
    off = jnp.broadcast_to(image_offset, (8, LANES))
    by_z = send_z(marked, 1, True)
    by_x = send(chip_half, lambda i: i ^ 2)
    self_out, kept = [None, None], [None, None]

    def self_forward(block, after):
        self_out[block], kept[block] = call(
            f"self_forward_{block}",
            functools.partial(self_kernel, block=block, groups=groups, repeat=repeat),
            [struct((groups, HEAD_DIM, half), bf16), struct((groups, 2 * WINDOW, half), f32)],
            [VMEM] * 4 + [ANY],
            flops=10**6,
            moved=10**5,
        )(q, ctx, tail if block else halo, segment_start, after)

    self_forward(1, chip)
    halo = merge("halo", halos, 1, self_out[1])
    arrived = call("arrived", join_kernel, [struct((img, width + LANES + width // 2), bf16)], [VMEM] * 2 + [ANY] * 2)(
        by_z, by_x, self_out[1], halo
    )[0]

    by_pair = send(arrived, lambda i: i ^ 1)
    self_forward(0, arrived)

    gate_shape = struct((heads * WINDOW // LANES, LANES), f32)
    scores, to_pair, to_x, in_chip, own_terms, masks, prev = call(
        "cross",
        functools.partial(cross_kernel, groups=groups, repeat=repeat),
        [
            struct((groups, 2 * img, repeat * tok_rows), bf16),
            struct((img, width + LANES), f32),
            struct((img, width + WIDE * LANES), bf16),
            struct((img, width), f32),
            struct((img, width), f32),
            struct((8, LANES), f32),
            image,
        ],
        [VMEM] * 10,
    )(off, owners, gate_rows, *self_out, grad, own, chip, arrived, by_pair)
    from_pair = send(to_pair, lambda i: i ^ 1)
    from_x = send(to_x, lambda i: i ^ 2)
    grad_self = call(
        "cross_query",
        functools.partial(cross_query_kernel, groups=groups, repeat=repeat),
        [struct((groups, repeat * tok_rows, HEAD_DIM), bf16)],
        [VMEM] * 4 + [ANY],
    )(scores, grad, own, prev, to_pair)[0]

    def self_backward(block, after, late=None):
        return call(
            f"self_backward_{block}",
            functools.partial(self_back_kernel, block=block, groups=groups, repeat=repeat),
            [
                struct((tok_rows, model), bf16),
                struct((WINDOW, width), f32) if block else struct((WINDOW + MORE, width), bf16),
                struct((WINDOW, width), f32),
            ],
            [VMEM] * 5 + [ANY] * (1 if late is None else 2),
            scratch=[pltpu.VMEM((WINDOW, model), bf16), pltpu.SemaphoreType.DMA((groups,))],
            out_specs=[ANY, VMEM, VMEM],
            aliases={5: 0} if block else None,
            flops=10**6,
            moved=10**5,
        )(q, ctx, tail if block else halo, kept[block], grad_self, after, *([] if late is None else [late]))

    to_z, gate = call(
        "outside",
        outside_kernel,
        [struct((img, width + LANES), bf16), gate_shape],
        [VMEM] * 3 + [ANY],
    )(to_pair, from_pair, masks, grad_self)
    from_z = send_z(to_z, -1)
    gates = []
    if swaps:
        gates = [send_z(gate, 1), send_z(gate, 2)]
    query_grad, halo_terms, low = self_backward(0, to_z)
    mine, gate, to_chip = call(
        "chip_sum",
        chip_sum_kernel,
        [struct((img, width), f32), gate_shape, struct((img, width + LANES), bf16)],
        [VMEM] * (4 + len(gates)) + [ANY],
    )(in_chip, from_x, from_z, gate, *gates, low)
    other = send(to_chip, lambda i: i ^ 1)
    halo_back = send_near(halo_terms, -1)
    query_grad, also, high = self_backward(1, query_grad, mine)
    halo_back = merge("halo_back", halo_back, -1, high)
    gate = call("gate_sum", gate_kernel, [gate_shape], [VMEM] * 2)(gate, other)[0]
    if swaps:
        far = [send_all(gate, lambda s, d: (s, d ^ 1))]
    else:
        gate = lax.psum(to_pair[: gate_shape.shape[0], width:], ("seq", "dp"))
        far = []
    memory_grad, context_grad, cross_gate_grad = call(
        "finish",
        functools.partial(finish_kernel, tok_rows=tok_rows),
        [image, struct((tok_rows, width), bf16), struct((1, heads), f32)],
        [VMEM] * (10 + len(far)),
    )(owners, own_terms, mine, other, low, also, high, halo_back, gate, *far, gate_rows)
    return (query_grad[None], context_grad[None], memory_grad[None, None], cross_gate_grad.reshape(heads))


def solution(mesh):
    placed = (
        P("dp", "seq", None),
        P("dp", "seq", None),
        P("dp", "seq"),
        P("dp", "seq", None, None),
        P("dp", "seq"),
        P(),
        P("dp", "seq", None),
    )
    return jax.shard_map(
        on_device,
        mesh=mesh,
        in_specs=placed,
        out_specs=(P("dp", "seq", None), P("dp", "seq", None), P("dp", "seq", None, None), P()),
        check_vma=False,
    )
```

```python
import functools
import math

import jax
import jax.numpy as jnp
from jax import lax
from jax.experimental import pallas as pl
from jax.experimental.pallas import tpu as pltpu
from jax.sharding import PartitionSpec as P

HEAD_DIM = 128
WINDOW = 64
GAP = 4
LANES = 128
WIDE = 2
MORE = 16
MARKS = 384
SCALE = 1.0 / math.sqrt(HEAD_DIM)

VMEM = pl.BlockSpec(memory_space=pltpu.VMEM)
ANY = pl.BlockSpec(memory_space=pl.ANY)
SMEM = pl.BlockSpec(memory_space=pltpu.SMEM)

NN = (((1,), (0,)), ((), ()))
NT = (((1,), (1,)), ((), ()))
TN = (((0,), (0,)), ((), ()))


def dot(a, b, dims):
    return lax.dot_general(a, b, dims, preferred_element_type=jnp.float32)


def stack(ref, first, rows, group, repeat):
    return jnp.concatenate(
        [
            ref[first : first + rows, (group * repeat + h) * HEAD_DIM : (group * repeat + h + 1) * HEAD_DIM]
            for h in range(repeat)
        ],
        axis=0,
    )


def part(ref, index):
    return ref[:, index * HEAD_DIM : (index + 1) * HEAD_DIM]


def softmax_rows(scores):
    top = jnp.max(scores, axis=0, keepdims=True)
    powers = jnp.exp(scores - top)
    return powers * (1.0 / jnp.sum(powers, axis=0, keepdims=True))


def self_mask(segment_ref, block, base):
    segment = segment_ref[0:1, block * WINDOW : (block + 1) * WINDOW]
    segment = jnp.concatenate([segment] * (LANES // WINDOW), axis=1)
    shape = (2 * WINDOW, LANES)
    key = lax.broadcasted_iota(jnp.int32, shape, 0)
    query = lax.broadcasted_iota(jnp.int32, shape, 1) % WINDOW
    key_pos = key + (base + (block - 1) * WINDOW)
    return (key >= query) & (key <= query + WINDOW) & (key_pos >= segment)


def self_weights(scores, allowed):
    allowed = jnp.concatenate([allowed] * (scores.shape[1] // LANES), axis=1)
    return softmax_rows(jnp.where(allowed, scores * SCALE, -1e30))


def joined(context_ref, halo_ref, block, index):
    own = context_ref[:, index * HEAD_DIM : (index + 1) * HEAD_DIM]
    if block == 0:
        return jnp.concatenate([part(halo_ref, index), own[:WINDOW]], axis=0)
    return own[(block - 1) * WINDOW : (block + 1) * WINDOW]


def odd_core():
    return flag(lax.axis_index("seq") % 2 == 1)


def flag(cond):
    return jnp.where(cond, 1, 0)


def choose(here, mine_ref, other_ref, out_ref, width=None):
    here = jnp.broadcast_to(here, out_ref.shape) > 0
    width = width or mine_ref.shape[1]
    mine, other = mine_ref[:, :width].astype(jnp.float32), other_ref[:, :width].astype(jnp.float32)
    out_ref[...] = jnp.where(here, mine, other).astype(out_ref.dtype)


def owner(owner_ref, row):
    return flag(owner_ref[row : row + 1, 0:1] > 0.5)


def read_mark(ref, first):
    return ref[0:16, first : first + LANES].astype(jnp.float32)[0:1, 0:1]


def chip_kernel(mine_ref, other_ref, out_ref, marked_ref, half_ref, owner_ref):
    width = out_ref.shape[1]
    mine, other = read_mark(mine_ref, width), read_mark(other_ref, width)
    choose(flag(mine > 0.5), mine_ref, other_ref, out_ref, width)
    marked_ref[:, :width] = out_ref[...]
    owns = jnp.maximum(mine, other)
    marked_ref[:, width:] = jnp.broadcast_to(owns, (out_ref.shape[0], LANES)).astype(marked_ref.dtype)
    choose(odd_core(), out_ref.at[:, width // 2 :], out_ref.at[:, : width // 2], half_ref)
    row = lax.broadcasted_iota(jnp.int32, owner_ref.shape, 0)
    owner_ref[...] = jnp.where(row == 0, mine, other)


def join_kernel(z_ref, x_ref, _, __, out_ref):
    out_ref[:, : z_ref.shape[1]] = z_ref[...]
    out_ref[:, z_ref.shape[1] :] = x_ref[...]


def near_kernel(chip_ref, other_ref, _, out_ref, *, step):
    first = chip_ref.shape[0] - out_ref.shape[0]
    choose(flag(lax.axis_index("seq") % 2 == (1 if step > 0 else 0)), chip_ref.at[first:], other_ref.at[first:], out_ref)


def self_kernel(query_ref, context_ref, halo_ref, segment_ref, _, out_ref, weights_ref, *, block, groups, repeat):
    tok_rows = query_ref.shape[0]
    base = lax.axis_index("seq") * tok_rows
    allowed = self_mask(segment_ref, block, base)
    scores = [
        dot(joined(context_ref, halo_ref, block, g), stack(query_ref, block * WINDOW, WINDOW, g, repeat), NT)
        for g in range(groups)
    ]
    weights = [self_weights(scores[g], allowed) for g in range(groups)]
    for g in range(groups):
        weights_ref[g] = weights[g]
        values = joined(context_ref, halo_ref, block, groups + g)
        out_ref[g] = dot(values, weights[g].astype(jnp.bfloat16), TN).astype(jnp.bfloat16)


def split(values):
    high = values.astype(jnp.bfloat16)
    rest = values - high.astype(jnp.float32)
    middle = rest.astype(jnp.bfloat16)
    low = (rest - middle.astype(jnp.float32)).astype(jnp.bfloat16)
    return jnp.concatenate([high, middle, low, jnp.zeros_like(low)], axis=0)


def unsplit(parts):
    parts = parts.astype(jnp.float32)
    rows = parts.shape[0] // 4
    return parts[:rows] + (parts[rows : 2 * rows] + parts[2 * rows : 3 * rows])


def cross_kernel(
    off_ref, owner_ref, gate_ref, self_0_ref, self_1_ref, grad_ref, own_ref, chip_ref, mine_ref, pair_ref,
    scores_ref, to_pair_ref, to_x_ref, in_chip_ref, own_terms_ref, mask_ref, prev, *, groups, repeat, step=2
):
    tok_rows, width = grad_ref.shape[0], chip_ref.shape[1]
    img = own_ref.shape[0]
    shard = lax.axis_index("seq")
    off = off_ref[0:1, 0:1]
    is_owner, pair_owner = owner(owner_ref, 0), owner(owner_ref, 1)
    upper, odd = flag(shard % GAP >= 2), flag(shard % 2 == 1)
    from_chip = odd * pair_owner
    from_x = upper * (1 - (is_owner | pair_owner))
    from_z = flag(shard >= GAP) * (1 - (from_chip | from_x))
    has_prev = from_chip | from_x | from_z
    marked = width + LANES
    by_mine = flag(read_mark(mine_ref, width) > 0.5)
    choose(by_mine, mine_ref, pair_ref, prev, width)
    for first in (0, 1):
        cols = prev.at[:, first * width // 2 : (first + 1) * width // 2]
        mine = from_x * flag(odd == first)
        choose(mine, mine_ref.at[:, marked:], cols, cols)
        choose(from_x - mine, pair_ref.at[:, marked:], cols, cols)
    choose(from_chip, chip_ref, prev, prev)

    half = repeat * WINDOW
    rows = tok_rows * repeat
    lane = lax.broadcasted_iota(jnp.int32, (1, rows), 1)
    lane_tok = (lane // half) * WINDOW + lane % WINDOW
    own_from = jnp.minimum(off, tok_rows)
    has_from = own_from * (1 - has_prev)
    from_chip, from_x, from_z = (here.astype(jnp.float32) for here in (from_chip, from_x, from_z))
    use_own = lane_tok >= own_from
    has_lane = lane_tok >= has_from
    row_tok = lax.broadcasted_iota(jnp.int32, (WINDOW, HEAD_DIM), 0)

    def pick(joint):
        return jnp.where(use_own, joint[img:], joint[:img])

    def join(values):
        zero = jnp.zeros_like(values)
        both = [jnp.where(use_own, zero, values), jnp.where(use_own, values, zero)]
        return jnp.concatenate(both, axis=0).astype(jnp.bfloat16)

    blocks = range(tok_rows // WINDOW)
    gate_rows = []
    for first in range(0, groups, step):
        every = range(first, first + step)
        keys = {g: jnp.concatenate([part(prev, g), part(own_ref, g)], axis=0) for g in every}
        values = {g: jnp.concatenate([part(prev, groups + g), part(own_ref, groups + g)], axis=0) for g in every}
        out_t = {g: jnp.concatenate([self_0_ref[g], self_1_ref[g]], axis=1) for g in every}
        scores = {g: dot(keys[g], out_t[g], NN) for g in every}
        plain, cross_rows, grad_weights = {}, {}, {}
        for g in every:
            tiles = [stack(grad_ref, block * WINDOW, WINDOW, g, repeat) for block in blocks]
            plain[g] = dot(values[g], jnp.concatenate(tiles, axis=0), NT)
            scaled = []
            for block in blocks:
                has_rows = row_tok + block * WINDOW >= has_from
                factors = [
                    jnp.where(has_rows, gate_ref[g * repeat + h : g * repeat + h + 1, :], 0.0) for h in range(repeat)
                ]
                scaled.append(
                    (tiles[block].astype(jnp.float32) * jnp.concatenate(factors, axis=0)).astype(jnp.bfloat16)
                )
            cross_rows[g] = jnp.concatenate(scaled, axis=0)
            grad_weights[g] = dot(values[g], cross_rows[g], NT)
        weights = {g: softmax_rows(pick(scores[g]) * SCALE) for g in every}
        score_terms = {}
        for g in every:
            gate_row = jnp.sum(weights[g].astype(jnp.bfloat16).astype(jnp.float32) * pick(plain[g]), axis=0, keepdims=True)
            gate_row = jnp.where(has_lane, gate_row, 0.0)
            gate_row = gate_row[:, :half] + gate_row[:, half:]
            gate_rows.extend(gate_row[:, i * LANES : (i + 1) * LANES] for i in range(half // LANES))
            weight_terms = pick(grad_weights[g])
            delta = jnp.sum(weights[g] * weight_terms, axis=0, keepdims=True)
            score_terms[g] = join(weights[g] * (weight_terms - delta))
            scores_ref[g] = score_terms[g]
        for g in every:
            grad_key = dot(score_terms[g], out_t[g], NT) * SCALE
            grad_value = dot(join(weights[g]), cross_rows[g], NN)
            for index, terms in ((g, grad_key), (groups + g, grad_value)):
                cols = slice(index * HEAD_DIM, (index + 1) * HEAD_DIM)
                own_terms_ref[:, cols] = terms[img:]
                to_pair_ref[:, cols] = terms[:img] * from_z
                to_x_ref[:, cols] = (terms[:img] * from_x).astype(to_x_ref.dtype)
                in_chip_ref[:, cols] = terms[:img] * from_chip
    gate = jnp.concatenate(gate_rows, axis=0)
    to_pair_ref[:, width:] = jnp.concatenate([gate] * (img // gate.shape[0]), axis=0)
    to_x_ref[:, width:] = jnp.concatenate([split(gate)] * (to_x_ref.shape[1] // LANES - width // LANES), axis=1)
    row = lax.broadcasted_iota(jnp.int32, mask_ref.shape, 0)
    mask_ref[...] = jnp.where(row == 0, by_mine.astype(jnp.float32) * (1.0 - from_x), from_x)


def cross_query_kernel(scores_ref, grad_ref, own_ref, prev, _, grad_self_ref, *, groups, repeat):
    for g in range(groups):
        keys = jnp.concatenate([part(prev, g), part(own_ref, g)], axis=0)
        grad_query = dot(scores_ref[g], keys, TN) * SCALE
        for block in range(grad_ref.shape[0] // WINDOW):
            rows = slice(block * repeat * WINDOW, (block + 1) * repeat * WINDOW)
            grad_rows = stack(grad_ref, block * WINDOW, WINDOW, g, repeat).astype(jnp.float32)
            grad_self_ref[g, rows, :] = (grad_rows + grad_query[rows]).astype(jnp.bfloat16)


def outside_kernel(mine_ref, pair_ref, mask_ref, _, to_z_ref, gate_ref):
    width = mine_ref.shape[1] - LANES
    total = mine_ref[...] + pair_ref[...]
    gate = total[: gate_ref.shape[0], width:]
    to_z_ref[:, :width] = (total[:, :width] * mask_ref[0:1, 0:1]).astype(to_z_ref.dtype)
    to_z_ref[:, width:] = split(gate)
    gate_ref[...] = gate


def chip_sum_kernel(mine_ref, x_ref, z_ref, gate_ref, *refs):
    *gates, _, out_ref, gate_out, to_pair_ref = refs
    width = mine_ref.shape[1]
    terms = mine_ref[...] + (x_ref[:, :width].astype(jnp.float32) + z_ref[:, :width].astype(jnp.float32))
    out_ref[...] = terms
    to_pair_ref[:, :width] = terms.astype(to_pair_ref.dtype)
    gate = unsplit(z_ref[:, width:]) + unsplit(x_ref[:, width : width + LANES])
    for ref in gates:
        gate = gate + ref[...]
    gate_out[...] = gate_ref[...] + gate
    to_pair_ref[:, width:] = split(gate)


def self_back_kernel(
    query_ref, context_ref, halo_ref, weights_ref, grad_ref, *refs, block, groups, repeat
):
    query_grad_ref, key_low_ref, key_high_ref, rows_out, sems = refs[-5:]
    half = repeat * WINDOW
    every = range(groups)
    rows = [stack(query_ref, block * WINDOW, WINDOW, g, repeat) for g in every]
    keys = [joined(context_ref, halo_ref, block, g) for g in every]
    grads = [grad_ref[g, block * half : (block + 1) * half, :] for g in every]
    grad_weights = [dot(joined(context_ref, halo_ref, block, groups + g), grads[g], NT) for g in every]
    grad_scores = []
    for g in every:
        delta = jnp.sum(weights_ref[g] * grad_weights[g], axis=0, keepdims=True)
        grad_scores.append((weights_ref[g] * (grad_weights[g] - delta)).astype(jnp.bfloat16))
    copies = []
    for g in every:
        grad_query = (dot(grad_scores[g], keys[g], TN) * SCALE).astype(jnp.bfloat16)
        for h in range(repeat):
            head = g * repeat + h
            rows_out[:, head * HEAD_DIM : (head + 1) * HEAD_DIM] = grad_query[h * WINDOW : (h + 1) * WINDOW]
        cols = slice(g * repeat * HEAD_DIM, (g + 1) * repeat * HEAD_DIM)
        copies.append(
            pltpu.make_async_copy(
                rows_out.at[:, cols], query_grad_ref.at[block * WINDOW : (block + 1) * WINDOW, cols], sems.at[g]
            )
        )
        copies[-1].start()
    for g in every:
        grad_key = dot(grad_scores[g], rows[g], NN) * SCALE
        grad_value = dot(weights_ref[g].astype(jnp.bfloat16), grads[g], NN)
        for index, terms in ((g, grad_key), (groups + g, grad_value)):
            cols = slice(index * HEAD_DIM, (index + 1) * HEAD_DIM)
            key_low_ref[key_low_ref.shape[0] - WINDOW :, cols] = terms[:WINDOW].astype(key_low_ref.dtype)
            key_high_ref[:, cols] = terms[WINDOW:]
    for copy in copies:
        copy.wait()


def gate_kernel(mine_ref, pair_ref, out_ref):
    out_ref[...] = mine_ref[...] + unsplit(pair_ref[:, pair_ref.shape[1] - LANES :])


def gate_grad(total, gate_ref):
    rows, heads = total.shape[0], gate_ref.shape[0]
    lane = lax.broadcasted_iota(jnp.int32, total.shape, 1)
    first = jnp.sum(jnp.where(lane < WINDOW, total, 0.0), axis=1, keepdims=True)
    second = jnp.sum(jnp.where(lane < WINDOW, 0.0, total), axis=1, keepdims=True)
    row = lax.broadcasted_iota(jnp.int32, (rows, heads), 0)
    head = lax.broadcasted_iota(jnp.int32, (rows, heads), 1)
    sums = jnp.where(head == 2 * row, first, 0.0) + jnp.where(head == 2 * row + 1, second, 0.0)
    sums = jnp.sum(sums, axis=0, keepdims=True)
    tanh = gate_ref[:, :heads]
    same = lax.broadcasted_iota(jnp.int32, tanh.shape, 0) == lax.broadcasted_iota(jnp.int32, tanh.shape, 1)
    tanh = jnp.sum(jnp.where(same, tanh, 0.0), axis=0, keepdims=True)
    return (1.0 - tanh * tanh) * sums


def finish_kernel(
    owner_ref, own_ref, mine_ref, pair_ref, low_ref, also_ref, high_ref, halo_ref, gate_ref, *refs, tok_rows
):
    *far_refs, tanh_ref, memory_ref, context_ref, gate_out = refs
    width = mine_ref.shape[1]
    keep = owner(owner_ref, 0).astype(jnp.float32)
    total = own_ref[...] + (mine_ref[...] + pair_ref[:, :width].astype(jnp.float32))
    memory_ref[...] = (total * keep).astype(memory_ref.dtype)
    more = jnp.where(lax.axis_index("seq") < lax.axis_size("seq") - 1, 1.0, 0.0)
    first = tok_rows - WINDOW
    context_ref[:first] = (low_ref[...] + also_ref[...]).astype(context_ref.dtype)
    context_ref[first:] = (high_ref[...] + halo_ref[...].astype(jnp.float32) * more).astype(context_ref.dtype)
    gate = gate_ref[...]
    for ref in far_refs:
        gate = gate + ref[...]
    gate_out[...] = gate_grad(gate, tanh_ref)


def struct(shape, dtype):
    return jax.ShapeDtypeStruct(shape, dtype)


def call(
    name, kernel, out_shape, in_specs, scratch=(), out_specs=None, aliases=None, flops=1000, moved=1000
):
    return pl.pallas_call(
        kernel,
        out_shape=out_shape,
        in_specs=in_specs,
        out_specs=[VMEM] * len(out_shape) if out_specs is None else out_specs,
        scratch_shapes=scratch,
        input_output_aliases=aliases or {},
        compiler_params=pltpu.CompilerParams(vmem_limit_bytes=40 * 2**20),
        cost_estimate=pl.CostEstimate(flops=flops, bytes_accessed=moved, transcendentals=0),
        name=name,
    )


def on_device(queries, context, segment_start, memory, image_offset, cross_gate, out_grad):
    tok_rows, model = queries.shape[1:]
    width = context.shape[2]
    groups = width // 2 // HEAD_DIM
    heads = cross_gate.shape[0]
    repeat = heads // groups
    img = memory.shape[2]
    half = repeat * WINDOW
    seq, dp = lax.axis_size("seq"), lax.axis_size("dp")
    f32, bf16 = jnp.float32, jnp.bfloat16

    swaps = seq == 4 * GAP and dp == 2

    def send(value, where):
        return lax.ppermute(value, "seq", [(i, where(i)) for i in range(seq)])

    def send_all(value, where):
        pairs = [(s, d, *where(s, d)) for s in range(seq) for d in range(dp)]
        return lax.ppermute(value, ("seq", "dp"), [(s * dp + d, t * dp + e) for s, d, t, e in pairs])

    def send_near(value, step):
        if not swaps:
            return (send(value, lambda i: (i + step) % seq),)
        off_chip = lambda s, d: (s, d ^ 1) if s in (0, seq - 1) else (((s + 1) ^ 1) - 1, d)
        return send(value, lambda i: i ^ 1), send_all(value, off_chip)

    def merge(name, arrived, step, after):
        if len(arrived) == 1:
            return arrived[0][arrived[0].shape[0] - WINDOW :]
        return call(name, functools.partial(near_kernel, step=step), [window], [VMEM] * 2 + [ANY])(*arrived, after)[0]

    def send_z(value, step, straight=False):
        def where(i):
            wraps = not 0 <= i + step * GAP < seq
            return ((i if i % 2 == 0 or (straight and wraps) else i ^ 2) + step * GAP) % seq

        return send(value, where)

    q, ctx, grad = queries[0], context[0], out_grad[0]
    gate_tanh = jnp.tanh(cross_gate)
    gate_rows = jnp.broadcast_to(gate_tanh[:, None], (heads, LANES))
    image = struct((img, width), bf16)
    window = struct((WINDOW, width), bf16)
    own = memory[0, 0]
    is_owner = (image_offset < tok_rows).astype(bf16)
    own = jnp.concatenate([own, jnp.broadcast_to(is_owner, (img, MARKS))], axis=1)
    pair = send(own, lambda i: i ^ 1)
    tail = ctx[tok_rows - WINDOW - MORE :]
    halos = send_near(tail, 1)
    chip, marked, chip_half, owners = call(
        "chip_image",
        chip_kernel,
        [image, struct((img, width + LANES), bf16), struct((img, width // 2), bf16), struct((8, LANES), f32)],
        [VMEM] * 2,
    )(own, pair)
    off = jnp.broadcast_to(image_offset, (8, LANES))
    by_z = send_z(marked, 1, True)
    by_x = send(chip_half, lambda i: i ^ 2)
    self_out, kept = [None, None], [None, None]

    def self_forward(block, after):
        self_out[block], kept[block] = call(
            f"self_forward_{block}",
            functools.partial(self_kernel, block=block, groups=groups, repeat=repeat),
            [struct((groups, HEAD_DIM, half), bf16), struct((groups, 2 * WINDOW, half), f32)],
            [VMEM] * 4 + [ANY],
            flops=10**6,
            moved=10**5,
        )(q, ctx, tail if block else halo, segment_start, after)

    self_forward(1, chip)
    halo = merge("halo", halos, 1, self_out[1])
    arrived = call("arrived", join_kernel, [struct((img, width + LANES + width // 2), bf16)], [VMEM] * 2 + [ANY] * 2)(
        by_z, by_x, self_out[1], halo
    )[0]

    by_pair = send(arrived, lambda i: i ^ 1)
    self_forward(0, arrived)

    gate_shape = struct((heads * WINDOW // LANES, LANES), f32)
    scores, to_pair, to_x, in_chip, own_terms, masks, prev = call(
        "cross",
        functools.partial(cross_kernel, groups=groups, repeat=repeat),
        [
            struct((groups, 2 * img, repeat * tok_rows), bf16),
            struct((img, width + LANES), f32),
            struct((img, width + WIDE * LANES), bf16),
            struct((img, width), f32),
            struct((img, width), f32),
            struct((8, LANES), f32),
            image,
        ],
        [VMEM] * 10,
    )(off, owners, gate_rows, *self_out, grad, own, chip, arrived, by_pair)
    from_pair = send(to_pair, lambda i: i ^ 1)
    from_x = send(to_x, lambda i: i ^ 2)
    grad_self = call(
        "cross_query",
        functools.partial(cross_query_kernel, groups=groups, repeat=repeat),
        [struct((groups, repeat * tok_rows, HEAD_DIM), bf16)],
        [VMEM] * 4 + [ANY],
    )(scores, grad, own, prev, to_pair)[0]

    def self_backward(block, after, late=None):
        return call(
            f"self_backward_{block}",
            functools.partial(self_back_kernel, block=block, groups=groups, repeat=repeat),
            [
                struct((tok_rows, model), bf16),
                struct((WINDOW, width), f32) if block else struct((WINDOW + MORE, width), bf16),
                struct((WINDOW, width), f32),
            ],
            [VMEM] * 5 + [ANY] * (1 if late is None else 2),
            scratch=[pltpu.VMEM((WINDOW, model), bf16), pltpu.SemaphoreType.DMA((groups,))],
            out_specs=[ANY, VMEM, VMEM],
            aliases={5: 0} if block else None,
            flops=10**6,
            moved=10**5,
        )(q, ctx, tail if block else halo, kept[block], grad_self, after, *([] if late is None else [late]))

    to_z, gate = call(
        "outside",
        outside_kernel,
        [struct((img, width + LANES), bf16), gate_shape],
        [VMEM] * 3 + [ANY],
    )(to_pair, from_pair, masks, grad_self)
    from_z = send_z(to_z, -1)
    gates = []
    if swaps:
        gates = [send_z(gate, 1), send_z(gate, 2)]
    query_grad, halo_terms, low = self_backward(0, to_z)
    mine, gate, to_chip = call(
        "chip_sum",
        chip_sum_kernel,
        [struct((img, width), f32), gate_shape, struct((img, width + LANES), bf16)],
        [VMEM] * (4 + len(gates)) + [ANY],
    )(in_chip, from_x, from_z, gate, *gates, low)
    other = send(to_chip, lambda i: i ^ 1)
    halo_back = send_near(halo_terms, -1)
    query_grad, also, high = self_backward(1, query_grad, mine)
    halo_back = merge("halo_back", halo_back, -1, high)
    gate = call("gate_sum", gate_kernel, [gate_shape], [VMEM] * 2)(gate, other)[0]
    if swaps:
        far = [send_all(gate, lambda s, d: (s, d ^ 1))]
    else:
        gate = lax.psum(to_pair[: gate_shape.shape[0], width:], ("seq", "dp"))
        far = []
    memory_grad, context_grad, cross_gate_grad = call(
        "finish",
        functools.partial(finish_kernel, tok_rows=tok_rows),
        [image, struct((tok_rows, width), bf16), struct((1, heads), f32)],
        [VMEM] * (10 + len(far)),
    )(owners, own_terms, mine, other, low, also, high, halo_back, gate, *far, gate_rows)
    return (query_grad[None], context_grad[None], memory_grad[None, None], cross_gate_grad.reshape(heads))


def solution(mesh):
    placed = (
        P("dp", "seq", None),
        P("dp", "seq", None),
        P("dp", "seq"),
        P("dp", "seq", None, None),
        P("dp", "seq"),
        P(),
        P("dp", "seq", None),
    )
    return jax.shard_map(
        on_device,
        mesh=mesh,
        in_specs=placed,
        out_specs=(P("dp", "seq", None), P("dp", "seq", None), P("dp", "seq", None, None), P()),
        check_vma=False,
    )
```

```python
import functools
import math

import jax
import jax.numpy as jnp
from jax import lax
from jax.experimental import pallas as pl
from jax.experimental.pallas import tpu as pltpu
from jax.sharding import PartitionSpec as P

HEAD_DIM = 128
WINDOW = 64
GAP = 4
LANES = 128
WIDE = 1
MORE = 16
MARKS = 384
SCALE = 1.0 / math.sqrt(HEAD_DIM)

VMEM = pl.BlockSpec(memory_space=pltpu.VMEM)
ANY = pl.BlockSpec(memory_space=pl.ANY)
SMEM = pl.BlockSpec(memory_space=pltpu.SMEM)

NN = (((1,), (0,)), ((), ()))
NT = (((1,), (1,)), ((), ()))
TN = (((0,), (0,)), ((), ()))


def dot(a, b, dims):
    return lax.dot_general(a, b, dims, preferred_element_type=jnp.float32)


def stack(ref, first, rows, group, repeat):
    return jnp.concatenate(
        [
            ref[first : first + rows, (group * repeat + h) * HEAD_DIM : (group * repeat + h + 1) * HEAD_DIM]
            for h in range(repeat)
        ],
        axis=0,
    )


def part(ref, index):
    return ref[:, index * HEAD_DIM : (index + 1) * HEAD_DIM]


def softmax_rows(scores):
    top = jnp.max(scores, axis=0, keepdims=True)
    powers = jnp.exp(scores - top)
    return powers * (1.0 / jnp.sum(powers, axis=0, keepdims=True))


def self_mask(segment_ref, block, base):
    segment = segment_ref[0:1, block * WINDOW : (block + 1) * WINDOW]
    segment = jnp.concatenate([segment] * (LANES // WINDOW), axis=1)
    shape = (2 * WINDOW, LANES)
    key = lax.broadcasted_iota(jnp.int32, shape, 0)
    query = lax.broadcasted_iota(jnp.int32, shape, 1) % WINDOW
    key_pos = key + (base + (block - 1) * WINDOW)
    return (key >= query) & (key <= query + WINDOW) & (key_pos >= segment)


def self_weights(scores, allowed):
    allowed = jnp.concatenate([allowed] * (scores.shape[1] // LANES), axis=1)
    return softmax_rows(jnp.where(allowed, scores * SCALE, -1e30))


def joined(context_ref, halo_ref, block, index):
    own = context_ref[:, index * HEAD_DIM : (index + 1) * HEAD_DIM]
    if block == 0:
        return jnp.concatenate([part(halo_ref, index), own[:WINDOW]], axis=0)
    return own[(block - 1) * WINDOW : (block + 1) * WINDOW]


def odd_core():
    return flag(lax.axis_index("seq") % 2 == 1)


def flag(cond):
    return jnp.where(cond, 1, 0)


def choose(here, mine_ref, other_ref, out_ref, width=None):
    here = jnp.broadcast_to(here, out_ref.shape) > 0
    width = width or mine_ref.shape[1]
    mine, other = mine_ref[:, :width].astype(jnp.float32), other_ref[:, :width].astype(jnp.float32)
    out_ref[...] = jnp.where(here, mine, other).astype(out_ref.dtype)


def owner(owner_ref, row):
    return flag(owner_ref[row : row + 1, 0:1] > 0.5)


def read_mark(ref, first):
    return ref[0:16, first : first + LANES].astype(jnp.float32)[0:1, 0:1]


def chip_kernel(mine_ref, other_ref, out_ref, marked_ref, half_ref, owner_ref):
    width = out_ref.shape[1]
    mine, other = read_mark(mine_ref, width), read_mark(other_ref, width)
    choose(flag(mine > 0.5), mine_ref, other_ref, out_ref, width)
    marked_ref[:, :width] = out_ref[...]
    owns = jnp.maximum(mine, other)
    marked_ref[:, width:] = jnp.broadcast_to(owns, (out_ref.shape[0], LANES)).astype(marked_ref.dtype)
    choose(odd_core(), out_ref.at[:, width // 2 :], out_ref.at[:, : width // 2], half_ref)
    row = lax.broadcasted_iota(jnp.int32, owner_ref.shape, 0)
    owner_ref[...] = jnp.where(row == 0, mine, other)


def join_kernel(z_ref, x_ref, _, __, out_ref):
    out_ref[:, : z_ref.shape[1]] = z_ref[...]
    out_ref[:, z_ref.shape[1] :] = x_ref[...]


def near_kernel(chip_ref, other_ref, _, out_ref, *, step):
    first = chip_ref.shape[0] - out_ref.shape[0]
    choose(flag(lax.axis_index("seq") % 2 == (1 if step > 0 else 0)), chip_ref.at[first:], other_ref.at[first:], out_ref)


def self_kernel(query_ref, context_ref, halo_ref, segment_ref, _, out_ref, weights_ref, *, block, groups, repeat):
    tok_rows = query_ref.shape[0]
    base = lax.axis_index("seq") * tok_rows
    allowed = self_mask(segment_ref, block, base)
    scores = [
        dot(joined(context_ref, halo_ref, block, g), stack(query_ref, block * WINDOW, WINDOW, g, repeat), NT)
        for g in range(groups)
    ]
    weights = [self_weights(scores[g], allowed) for g in range(groups)]
    for g in range(groups):
        weights_ref[g] = weights[g]
        values = joined(context_ref, halo_ref, block, groups + g)
        out_ref[g] = dot(values, weights[g].astype(jnp.bfloat16), TN).astype(jnp.bfloat16)


def split(values):
    high = values.astype(jnp.bfloat16)
    rest = values - high.astype(jnp.float32)
    middle = rest.astype(jnp.bfloat16)
    low = (rest - middle.astype(jnp.float32)).astype(jnp.bfloat16)
    return jnp.concatenate([high, middle, low, jnp.zeros_like(low)], axis=0)


def unsplit(parts):
    parts = parts.astype(jnp.float32)
    rows = parts.shape[0] // 4
    return parts[:rows] + (parts[rows : 2 * rows] + parts[2 * rows : 3 * rows])


def cross_kernel(
    off_ref, owner_ref, gate_ref, self_0_ref, self_1_ref, grad_ref, own_ref, chip_ref, mine_ref, pair_ref,
    scores_ref, to_pair_ref, to_x_ref, in_chip_ref, own_terms_ref, mask_ref, prev, *, groups, repeat, step=2
):
    tok_rows, width = grad_ref.shape[0], chip_ref.shape[1]
    img = own_ref.shape[0]
    shard = lax.axis_index("seq")
    off = off_ref[0:1, 0:1]
    is_owner, pair_owner = owner(owner_ref, 0), owner(owner_ref, 1)
    upper, odd = flag(shard % GAP >= 2), flag(shard % 2 == 1)
    from_chip = odd * pair_owner
    from_x = upper * (1 - (is_owner | pair_owner))
    from_z = flag(shard >= GAP) * (1 - (from_chip | from_x))
    has_prev = from_chip | from_x | from_z
    marked = width + LANES
    by_mine = flag(read_mark(mine_ref, width) > 0.5)
    choose(by_mine, mine_ref, pair_ref, prev, width)
    for first in (0, 1):
        cols = prev.at[:, first * width // 2 : (first + 1) * width // 2]
        mine = from_x * flag(odd == first)
        choose(mine, mine_ref.at[:, marked:], cols, cols)
        choose(from_x - mine, pair_ref.at[:, marked:], cols, cols)
    choose(from_chip, chip_ref, prev, prev)

    half = repeat * WINDOW
    rows = tok_rows * repeat
    lane = lax.broadcasted_iota(jnp.int32, (1, rows), 1)
    lane_tok = (lane // half) * WINDOW + lane % WINDOW
    own_from = jnp.minimum(off, tok_rows)
    has_from = own_from * (1 - has_prev)
    from_chip, from_x, from_z = (here.astype(jnp.float32) for here in (from_chip, from_x, from_z))
    use_own = lane_tok >= own_from
    has_lane = lane_tok >= has_from
    row_tok = lax.broadcasted_iota(jnp.int32, (WINDOW, HEAD_DIM), 0)

    def pick(joint):
        return jnp.where(use_own, joint[img:], joint[:img])

    def join(values):
        zero = jnp.zeros_like(values)
        both = [jnp.where(use_own, zero, values), jnp.where(use_own, values, zero)]
        return jnp.concatenate(both, axis=0).astype(jnp.bfloat16)

    blocks = range(tok_rows // WINDOW)
    gate_rows = []
    for first in range(0, groups, step):
        every = range(first, first + step)
        keys = {g: jnp.concatenate([part(prev, g), part(own_ref, g)], axis=0) for g in every}
        values = {g: jnp.concatenate([part(prev, groups + g), part(own_ref, groups + g)], axis=0) for g in every}
        out_t = {g: jnp.concatenate([self_0_ref[g], self_1_ref[g]], axis=1) for g in every}
        scores = {g: dot(keys[g], out_t[g], NN) for g in every}
        plain, cross_rows, grad_weights = {}, {}, {}
        for g in every:
            tiles = [stack(grad_ref, block * WINDOW, WINDOW, g, repeat) for block in blocks]
            plain[g] = dot(values[g], jnp.concatenate(tiles, axis=0), NT)
            scaled = []
            for block in blocks:
                has_rows = row_tok + block * WINDOW >= has_from
                factors = [
                    jnp.where(has_rows, gate_ref[g * repeat + h : g * repeat + h + 1, :], 0.0) for h in range(repeat)
                ]
                scaled.append(
                    (tiles[block].astype(jnp.float32) * jnp.concatenate(factors, axis=0)).astype(jnp.bfloat16)
                )
            cross_rows[g] = jnp.concatenate(scaled, axis=0)
            grad_weights[g] = dot(values[g], cross_rows[g], NT)
        weights = {g: softmax_rows(pick(scores[g]) * SCALE) for g in every}
        score_terms = {}
        for g in every:
            gate_row = jnp.sum(weights[g].astype(jnp.bfloat16).astype(jnp.float32) * pick(plain[g]), axis=0, keepdims=True)
            gate_row = jnp.where(has_lane, gate_row, 0.0)
            gate_row = gate_row[:, :half] + gate_row[:, half:]
            gate_rows.extend(gate_row[:, i * LANES : (i + 1) * LANES] for i in range(half // LANES))
            weight_terms = pick(grad_weights[g])
            delta = jnp.sum(weights[g] * weight_terms, axis=0, keepdims=True)
            score_terms[g] = join(weights[g] * (weight_terms - delta))
            scores_ref[g] = score_terms[g]
        for g in every:
            grad_key = dot(score_terms[g], out_t[g], NT) * SCALE
            grad_value = dot(join(weights[g]), cross_rows[g], NN)
            for index, terms in ((g, grad_key), (groups + g, grad_value)):
                cols = slice(index * HEAD_DIM, (index + 1) * HEAD_DIM)
                own_terms_ref[:, cols] = terms[img:]
                to_pair_ref[:, cols] = terms[:img] * from_z
                to_x_ref[:, cols] = (terms[:img] * from_x).astype(to_x_ref.dtype)
                in_chip_ref[:, cols] = terms[:img] * from_chip
    gate = jnp.concatenate(gate_rows, axis=0)
    to_pair_ref[:, width:] = jnp.concatenate([gate] * (img // gate.shape[0]), axis=0)
    to_x_ref[:, width:] = jnp.concatenate([split(gate)] * (to_x_ref.shape[1] // LANES - width // LANES), axis=1)
    row = lax.broadcasted_iota(jnp.int32, mask_ref.shape, 0)
    mask_ref[...] = jnp.where(row == 0, by_mine.astype(jnp.float32) * (1.0 - from_x), from_x)


def cross_query_kernel(scores_ref, grad_ref, own_ref, prev, _, grad_self_ref, *, groups, repeat):
    for g in range(groups):
        keys = jnp.concatenate([part(prev, g), part(own_ref, g)], axis=0)
        grad_query = dot(scores_ref[g], keys, TN) * SCALE
        for block in range(grad_ref.shape[0] // WINDOW):
            rows = slice(block * repeat * WINDOW, (block + 1) * repeat * WINDOW)
            grad_rows = stack(grad_ref, block * WINDOW, WINDOW, g, repeat).astype(jnp.float32)
            grad_self_ref[g, rows, :] = (grad_rows + grad_query[rows]).astype(jnp.bfloat16)


def outside_kernel(mine_ref, pair_ref, mask_ref, _, to_z_ref, gate_ref):
    width = mine_ref.shape[1] - LANES
    total = mine_ref[...] + pair_ref[...]
    gate = total[: gate_ref.shape[0], width:]
    to_z_ref[:, :width] = (total[:, :width] * mask_ref[0:1, 0:1]).astype(to_z_ref.dtype)
    to_z_ref[:, width:] = split(gate)
    gate_ref[...] = gate


def chip_sum_kernel(mine_ref, x_ref, z_ref, gate_ref, *refs):
    *gates, _, out_ref, gate_out, to_pair_ref = refs
    width = mine_ref.shape[1]
    terms = mine_ref[...] + (x_ref[:, :width].astype(jnp.float32) + z_ref[:, :width].astype(jnp.float32))
    out_ref[...] = terms
    to_pair_ref[:, :width] = terms.astype(to_pair_ref.dtype)
    gate = unsplit(z_ref[:, width:]) + unsplit(x_ref[:, width : width + LANES])
    for ref in gates:
        gate = gate + ref[...]
    gate_out[...] = gate_ref[...] + gate
    to_pair_ref[:, width:] = split(gate)


def self_back_kernel(
    query_ref, context_ref, halo_ref, weights_ref, grad_ref, *refs, block, groups, repeat
):
    query_grad_ref, key_low_ref, key_high_ref, rows_out, sems = refs[-5:]
    half = repeat * WINDOW
    every = range(groups)
    rows = [stack(query_ref, block * WINDOW, WINDOW, g, repeat) for g in every]
    keys = [joined(context_ref, halo_ref, block, g) for g in every]
    grads = [grad_ref[g, block * half : (block + 1) * half, :] for g in every]
    grad_weights = [dot(joined(context_ref, halo_ref, block, groups + g), grads[g], NT) for g in every]
    grad_scores = []
    for g in every:
        delta = jnp.sum(weights_ref[g] * grad_weights[g], axis=0, keepdims=True)
        grad_scores.append((weights_ref[g] * (grad_weights[g] - delta)).astype(jnp.bfloat16))
    copies = []
    for g in every:
        grad_query = (dot(grad_scores[g], keys[g], TN) * SCALE).astype(jnp.bfloat16)
        for h in range(repeat):
            head = g * repeat + h
            rows_out[:, head * HEAD_DIM : (head + 1) * HEAD_DIM] = grad_query[h * WINDOW : (h + 1) * WINDOW]
        cols = slice(g * repeat * HEAD_DIM, (g + 1) * repeat * HEAD_DIM)
        copies.append(
            pltpu.make_async_copy(
                rows_out.at[:, cols], query_grad_ref.at[block * WINDOW : (block + 1) * WINDOW, cols], sems.at[g]
            )
        )
        copies[-1].start()
    for g in every:
        grad_key = dot(grad_scores[g], rows[g], NN) * SCALE
        grad_value = dot(weights_ref[g].astype(jnp.bfloat16), grads[g], NN)
        for index, terms in ((g, grad_key), (groups + g, grad_value)):
            cols = slice(index * HEAD_DIM, (index + 1) * HEAD_DIM)
            key_low_ref[key_low_ref.shape[0] - WINDOW :, cols] = terms[:WINDOW].astype(key_low_ref.dtype)
            key_high_ref[:, cols] = terms[WINDOW:]
    for copy in copies:
        copy.wait()


def gate_kernel(mine_ref, pair_ref, out_ref):
    out_ref[...] = mine_ref[...] + unsplit(pair_ref[:, pair_ref.shape[1] - LANES :])


def gate_grad(total, gate_ref):
    rows, heads = total.shape[0], gate_ref.shape[0]
    lane = lax.broadcasted_iota(jnp.int32, total.shape, 1)
    first = jnp.sum(jnp.where(lane < WINDOW, total, 0.0), axis=1, keepdims=True)
    second = jnp.sum(jnp.where(lane < WINDOW, 0.0, total), axis=1, keepdims=True)
    row = lax.broadcasted_iota(jnp.int32, (rows, heads), 0)
    head = lax.broadcasted_iota(jnp.int32, (rows, heads), 1)
    sums = jnp.where(head == 2 * row, first, 0.0) + jnp.where(head == 2 * row + 1, second, 0.0)
    sums = jnp.sum(sums, axis=0, keepdims=True)
    tanh = gate_ref[:, :heads]
    same = lax.broadcasted_iota(jnp.int32, tanh.shape, 0) == lax.broadcasted_iota(jnp.int32, tanh.shape, 1)
    tanh = jnp.sum(jnp.where(same, tanh, 0.0), axis=0, keepdims=True)
    return (1.0 - tanh * tanh) * sums


def finish_kernel(
    owner_ref, own_ref, mine_ref, pair_ref, low_ref, also_ref, high_ref, halo_ref, gate_ref, *refs, tok_rows
):
    *far_refs, tanh_ref, memory_ref, context_ref, gate_out = refs
    width = mine_ref.shape[1]
    keep = owner(owner_ref, 0).astype(jnp.float32)
    total = own_ref[...] + (mine_ref[...] + pair_ref[:, :width].astype(jnp.float32))
    memory_ref[...] = (total * keep).astype(memory_ref.dtype)
    more = jnp.where(lax.axis_index("seq") < lax.axis_size("seq") - 1, 1.0, 0.0)
    first = tok_rows - WINDOW
    context_ref[:first] = (low_ref[...] + also_ref[...]).astype(context_ref.dtype)
    context_ref[first:] = (high_ref[...] + halo_ref[...].astype(jnp.float32) * more).astype(context_ref.dtype)
    gate = gate_ref[...]
    for ref in far_refs:
        gate = gate + ref[...]
    gate_out[...] = gate_grad(gate, tanh_ref)


def struct(shape, dtype):
    return jax.ShapeDtypeStruct(shape, dtype)


def call(
    name, kernel, out_shape, in_specs, scratch=(), out_specs=None, aliases=None, flops=1000, moved=1000
):
    return pl.pallas_call(
        kernel,
        out_shape=out_shape,
        in_specs=in_specs,
        out_specs=[VMEM] * len(out_shape) if out_specs is None else out_specs,
        scratch_shapes=scratch,
        input_output_aliases=aliases or {},
        compiler_params=pltpu.CompilerParams(vmem_limit_bytes=40 * 2**20),
        cost_estimate=pl.CostEstimate(flops=flops, bytes_accessed=moved, transcendentals=0),
        name=name,
    )


def on_device(queries, context, segment_start, memory, image_offset, cross_gate, out_grad):
    tok_rows, model = queries.shape[1:]
    width = context.shape[2]
    groups = width // 2 // HEAD_DIM
    heads = cross_gate.shape[0]
    repeat = heads // groups
    img = memory.shape[2]
    half = repeat * WINDOW
    seq, dp = lax.axis_size("seq"), lax.axis_size("dp")
    f32, bf16 = jnp.float32, jnp.bfloat16

    swaps = seq == 4 * GAP and dp == 2

    def send(value, where):
        return lax.ppermute(value, "seq", [(i, where(i)) for i in range(seq)])

    def send_all(value, where):
        pairs = [(s, d, *where(s, d)) for s in range(seq) for d in range(dp)]
        return lax.ppermute(value, ("seq", "dp"), [(s * dp + d, t * dp + e) for s, d, t, e in pairs])

    def send_near(value, step):
        if not swaps:
            return (send(value, lambda i: (i + step) % seq),)
        off_chip = lambda s, d: (s, d ^ 1) if s in (0, seq - 1) else (((s + 1) ^ 1) - 1, d)
        return send(value, lambda i: i ^ 1), send_all(value, off_chip)

    def merge(name, arrived, step, after):
        if len(arrived) == 1:
            return arrived[0][arrived[0].shape[0] - WINDOW :]
        return call(name, functools.partial(near_kernel, step=step), [window], [VMEM] * 2 + [ANY])(*arrived, after)[0]

    def send_z(value, step, straight=False):
        def where(i):
            wraps = not 0 <= i + step * GAP < seq
            return ((i if i % 2 == 0 or (straight and wraps) else i ^ 2) + step * GAP) % seq

        return send(value, where)

    q, ctx, grad = queries[0], context[0], out_grad[0]
    gate_tanh = jnp.tanh(cross_gate)
    gate_rows = jnp.broadcast_to(gate_tanh[:, None], (heads, LANES))
    image = struct((img, width), bf16)
    window = struct((WINDOW, width), bf16)
    own = memory[0, 0]
    is_owner = (image_offset < tok_rows).astype(bf16)
    own = jnp.concatenate([own, jnp.broadcast_to(is_owner, (img, MARKS))], axis=1)
    pair = send(own, lambda i: i ^ 1)
    tail = ctx[tok_rows - WINDOW - MORE :]
    halos = send_near(tail, 1)
    chip, marked, chip_half, owners = call(
        "chip_image",
        chip_kernel,
        [image, struct((img, width + LANES), bf16), struct((img, width // 2), bf16), struct((8, LANES), f32)],
        [VMEM] * 2,
    )(own, pair)
    off = jnp.broadcast_to(image_offset, (8, LANES))
    by_z = send_z(marked, 1, True)
    by_x = send(chip_half, lambda i: i ^ 2)
    self_out, kept = [None, None], [None, None]

    def self_forward(block, after):
        self_out[block], kept[block] = call(
            f"self_forward_{block}",
            functools.partial(self_kernel, block=block, groups=groups, repeat=repeat),
            [struct((groups, HEAD_DIM, half), bf16), struct((groups, 2 * WINDOW, half), f32)],
            [VMEM] * 4 + [ANY],
            flops=10**6,
            moved=10**5,
        )(q, ctx, tail if block else halo, segment_start, after)

    self_forward(1, chip)
    halo = merge("halo", halos, 1, self_out[1])
    arrived = call("arrived", join_kernel, [struct((img, width + LANES + width // 2), bf16)], [VMEM] * 2 + [ANY] * 2)(
        by_z, by_x, self_out[1], halo
    )[0]

    by_pair = send(arrived, lambda i: i ^ 1)
    self_forward(0, arrived)

    gate_shape = struct((heads * WINDOW // LANES, LANES), f32)
    scores, to_pair, to_x, in_chip, own_terms, masks, prev = call(
        "cross",
        functools.partial(cross_kernel, groups=groups, repeat=repeat),
        [
            struct((groups, 2 * img, repeat * tok_rows), bf16),
            struct((img, width + LANES), f32),
            struct((img, width + WIDE * LANES), bf16),
            struct((img, width), f32),
            struct((img, width), f32),
            struct((8, LANES), f32),
            image,
        ],
        [VMEM] * 10,
    )(off, owners, gate_rows, *self_out, grad, own, chip, arrived, by_pair)
    from_pair = send(to_pair, lambda i: i ^ 1)
    from_x = send(to_x, lambda i: i ^ 2)
    grad_self = call(
        "cross_query",
        functools.partial(cross_query_kernel, groups=groups, repeat=repeat),
        [struct((groups, repeat * tok_rows, HEAD_DIM), bf16)],
        [VMEM] * 4 + [ANY],
    )(scores, grad, own, prev, to_pair)[0]

    def self_backward(block, after, late=None):
        return call(
            f"self_backward_{block}",
            functools.partial(self_back_kernel, block=block, groups=groups, repeat=repeat),
            [
                struct((tok_rows, model), bf16),
                struct((WINDOW, width), f32) if block else struct((WINDOW + MORE, width), bf16),
                struct((WINDOW, width), f32),
            ],
            [VMEM] * 5 + [ANY] * (1 if late is None else 2),
            scratch=[pltpu.VMEM((WINDOW, model), bf16), pltpu.SemaphoreType.DMA((groups,))],
            out_specs=[ANY, VMEM, VMEM],
            aliases={5: 0} if block else None,
            flops=10**6,
            moved=10**5,
        )(q, ctx, tail if block else halo, kept[block], grad_self, after, *([] if late is None else [late]))

    to_z, gate = call(
        "outside",
        outside_kernel,
        [struct((img, width + LANES), bf16), gate_shape],
        [VMEM] * 3 + [ANY],
    )(to_pair, from_pair, masks, grad_self)
    from_z = send_z(to_z, -1)
    gates = []
    if swaps:
        gates = [send_z(gate, 1), send_z(gate, 2)]
    query_grad, halo_terms, low = self_backward(0, to_z)
    mine, gate, to_chip = call(
        "chip_sum",
        chip_sum_kernel,
        [struct((img, width), f32), gate_shape, struct((img, width + LANES), bf16)],
        [VMEM] * (4 + len(gates)) + [ANY],
    )(in_chip, from_x, from_z, gate, *gates, low)
    other = send(to_chip, lambda i: i ^ 1)
    halo_back = send_near(halo_terms, -1)
    query_grad, also, high = self_backward(1, query_grad, mine)
    halo_back = merge("halo_back", halo_back, -1, high)
    gate = call("gate_sum", gate_kernel, [gate_shape], [VMEM] * 2)(gate, other)[0]
    if swaps:
        far = [send_all(gate, lambda s, d: (s, d ^ 1))]
    else:
        gate = lax.psum(to_pair[: gate_shape.shape[0], width:], ("seq", "dp"))
        far = []
    memory_grad, context_grad, cross_gate_grad = call(
        "finish",
        functools.partial(finish_kernel, tok_rows=tok_rows),
        [image, struct((tok_rows, width), bf16), struct((1, heads), f32)],
        [VMEM] * (10 + len(far)),
    )(owners, own_terms, mine, other, low, also, high, halo_back, gate, *far, gate_rows)
    return (query_grad[None], context_grad[None], memory_grad[None, None], cross_gate_grad.reshape(heads))


def solution(mesh):
    placed = (
        P("dp", "seq", None),
        P("dp", "seq", None),
        P("dp", "seq"),
        P("dp", "seq", None, None),
        P("dp", "seq"),
        P(),
        P("dp", "seq", None),
    )
    return jax.shard_map(
        on_device,
        mesh=mesh,
        in_specs=placed,
        out_specs=(P("dp", "seq", None), P("dp", "seq", None), P("dp", "seq", None, None), P()),
        check_vma=False,
    )
```

```python
import functools
import math

import jax
import jax.numpy as jnp
from jax import lax
from jax.experimental import pallas as pl
from jax.experimental.pallas import tpu as pltpu
from jax.sharding import PartitionSpec as P

HEAD_DIM = 128
WINDOW = 64
GAP = 4
LANES = 128
WIDE = 1
MORE = 16
MARKS = 384
SCALE = 1.0 / math.sqrt(HEAD_DIM)

VMEM = pl.BlockSpec(memory_space=pltpu.VMEM)
ANY = pl.BlockSpec(memory_space=pl.ANY)
SMEM = pl.BlockSpec(memory_space=pltpu.SMEM)

NN = (((1,), (0,)), ((), ()))
NT = (((1,), (1,)), ((), ()))
TN = (((0,), (0,)), ((), ()))


def dot(a, b, dims):
    return lax.dot_general(a, b, dims, preferred_element_type=jnp.float32)


def stack(ref, first, rows, group, repeat):
    return jnp.concatenate(
        [
            ref[first : first + rows, (group * repeat + h) * HEAD_DIM : (group * repeat + h + 1) * HEAD_DIM]
            for h in range(repeat)
        ],
        axis=0,
    )


def part(ref, index):
    return ref[:, index * HEAD_DIM : (index + 1) * HEAD_DIM]


def softmax_rows(scores):
    top = jnp.max(scores, axis=0, keepdims=True)
    powers = jnp.exp(scores - top)
    return powers * (1.0 / jnp.sum(powers, axis=0, keepdims=True))


def self_mask(segment_ref, block, base):
    segment = segment_ref[0:1, block * WINDOW : (block + 1) * WINDOW]
    segment = jnp.concatenate([segment] * (LANES // WINDOW), axis=1)
    shape = (2 * WINDOW, LANES)
    key = lax.broadcasted_iota(jnp.int32, shape, 0)
    query = lax.broadcasted_iota(jnp.int32, shape, 1) % WINDOW
    key_pos = key + (base + (block - 1) * WINDOW)
    return (key >= query) & (key <= query + WINDOW) & (key_pos >= segment)


def self_weights(scores, allowed):
    allowed = jnp.concatenate([allowed] * (scores.shape[1] // LANES), axis=1)
    return softmax_rows(jnp.where(allowed, scores * SCALE, -1e30))


def joined(context_ref, halo_ref, block, index):
    own = context_ref[:, index * HEAD_DIM : (index + 1) * HEAD_DIM]
    if block == 0:
        return jnp.concatenate([part(halo_ref, index), own[:WINDOW]], axis=0)
    return own[(block - 1) * WINDOW : (block + 1) * WINDOW]


def odd_core():
    return flag(lax.axis_index("seq") % 2 == 1)


def flag(cond):
    return jnp.where(cond, 1, 0)


def choose(here, mine_ref, other_ref, out_ref, width=None):
    here = jnp.broadcast_to(here, out_ref.shape) > 0
    width = width or mine_ref.shape[1]
    mine, other = mine_ref[:, :width].astype(jnp.float32), other_ref[:, :width].astype(jnp.float32)
    out_ref[...] = jnp.where(here, mine, other).astype(out_ref.dtype)


def owner(owner_ref, row):
    return flag(owner_ref[row : row + 1, 0:1] > 0.5)


def read_mark(ref, first):
    return ref[0:16, first : first + LANES].astype(jnp.float32)[0:1, 0:1]


def chip_kernel(mine_ref, other_ref, out_ref, marked_ref, half_ref, owner_ref):
    width = out_ref.shape[1]
    mine, other = read_mark(mine_ref, width), read_mark(other_ref, width)
    choose(flag(mine > 0.5), mine_ref, other_ref, out_ref, width)
    marked_ref[:, :width] = out_ref[...]
    owns = jnp.maximum(mine, other)
    marked_ref[:, width:] = jnp.broadcast_to(owns, (out_ref.shape[0], LANES)).astype(marked_ref.dtype)
    choose(odd_core(), out_ref.at[:, width // 2 :], out_ref.at[:, : width // 2], half_ref)
    row = lax.broadcasted_iota(jnp.int32, owner_ref.shape, 0)
    owner_ref[...] = jnp.where(row == 0, mine, other)


def join_kernel(z_ref, x_ref, _, __, out_ref):
    out_ref[:, : z_ref.shape[1]] = z_ref[...]
    out_ref[:, z_ref.shape[1] :] = x_ref[...]


def near_kernel(chip_ref, other_ref, _, out_ref, *, step):
    first = chip_ref.shape[0] - out_ref.shape[0]
    choose(flag(lax.axis_index("seq") % 2 == (1 if step > 0 else 0)), chip_ref.at[first:], other_ref.at[first:], out_ref)


def self_kernel(query_ref, context_ref, halo_ref, segment_ref, _, out_ref, weights_ref, *, block, groups, repeat):
    tok_rows = query_ref.shape[0]
    base = lax.axis_index("seq") * tok_rows
    allowed = self_mask(segment_ref, block, base)
    scores = [
        dot(joined(context_ref, halo_ref, block, g), stack(query_ref, block * WINDOW, WINDOW, g, repeat), NT)
        for g in range(groups)
    ]
    weights = [self_weights(scores[g], allowed) for g in range(groups)]
    for g in range(groups):
        weights_ref[g] = weights[g]
        values = joined(context_ref, halo_ref, block, groups + g)
        out_ref[g] = dot(values, weights[g].astype(jnp.bfloat16), TN).astype(jnp.bfloat16)


def split(values):
    high = values.astype(jnp.bfloat16)
    rest = values - high.astype(jnp.float32)
    middle = rest.astype(jnp.bfloat16)
    low = (rest - middle.astype(jnp.float32)).astype(jnp.bfloat16)
    return jnp.concatenate([high, middle, low, jnp.zeros_like(low)], axis=0)


def unsplit(parts):
    parts = parts.astype(jnp.float32)
    rows = parts.shape[0] // 4
    return parts[:rows] + (parts[rows : 2 * rows] + parts[2 * rows : 3 * rows])


def scale_kernel(off_ref, owner_ref, gate_ref, grad_ref, _, out_ref, *, groups, repeat):
    tok_rows = grad_ref.shape[0]
    half = repeat * WINDOW
    shard = lax.axis_index("seq")
    is_owner, pair_owner = owner(owner_ref, 0), owner(owner_ref, 1)
    from_chip = flag(shard % 2 == 1) * pair_owner
    from_x = flag(shard % GAP >= 2) * (1 - (is_owner | pair_owner))
    has_prev = from_chip | from_x | flag(shard >= GAP)
    has_from = jnp.minimum(off_ref[0:1, 0:1], tok_rows) * (1 - has_prev)
    row_tok = lax.broadcasted_iota(jnp.int32, (WINDOW, HEAD_DIM), 0)
    for g in range(groups):
        for block in range(tok_rows // WINDOW):
            has_rows = row_tok + block * WINDOW >= has_from
            rows = stack(grad_ref, block * WINDOW, WINDOW, g, repeat).astype(jnp.float32)
            factors = [
                jnp.where(has_rows, gate_ref[g * repeat + h : g * repeat + h + 1, :], 0.0) for h in range(repeat)
            ]
            rows = rows * jnp.concatenate(factors, axis=0)
            out_ref[g, block * half : (block + 1) * half, :] = rows.astype(out_ref.dtype)


def cross_kernel(
    off_ref, owner_ref, cross_rows_ref, self_0_ref, self_1_ref, grad_ref, own_ref, chip_ref, mine_ref, pair_ref,
    scores_ref, to_pair_ref, to_x_ref, in_chip_ref, own_terms_ref, mask_ref, prev, *, groups, repeat, step=2
):
    tok_rows, width = grad_ref.shape[0], chip_ref.shape[1]
    img = own_ref.shape[0]
    shard = lax.axis_index("seq")
    off = off_ref[0:1, 0:1]
    is_owner, pair_owner = owner(owner_ref, 0), owner(owner_ref, 1)
    upper, odd = flag(shard % GAP >= 2), flag(shard % 2 == 1)
    from_chip = odd * pair_owner
    from_x = upper * (1 - (is_owner | pair_owner))
    from_z = flag(shard >= GAP) * (1 - (from_chip | from_x))
    has_prev = from_chip | from_x | from_z
    marked = width + LANES
    by_mine = flag(read_mark(mine_ref, width) > 0.5)
    choose(by_mine, mine_ref, pair_ref, prev, width)
    for first in (0, 1):
        cols = prev.at[:, first * width // 2 : (first + 1) * width // 2]
        mine = from_x * flag(odd == first)
        choose(mine, mine_ref.at[:, marked:], cols, cols)
        choose(from_x - mine, pair_ref.at[:, marked:], cols, cols)
    choose(from_chip, chip_ref, prev, prev)

    half = repeat * WINDOW
    rows = tok_rows * repeat
    lane = lax.broadcasted_iota(jnp.int32, (1, rows), 1)
    lane_tok = (lane // half) * WINDOW + lane % WINDOW
    own_from = jnp.minimum(off, tok_rows)
    has_from = own_from * (1 - has_prev)
    from_chip, from_x, from_z = (here.astype(jnp.float32) for here in (from_chip, from_x, from_z))
    use_own = lane_tok >= own_from
    has_lane = lane_tok >= has_from

    def pick(joint):
        return jnp.where(use_own, joint[img:], joint[:img])

    def join(values):
        zero = jnp.zeros_like(values)
        both = [jnp.where(use_own, zero, values), jnp.where(use_own, values, zero)]
        return jnp.concatenate(both, axis=0).astype(jnp.bfloat16)

    blocks = range(tok_rows // WINDOW)
    gate_rows = []
    for first in range(0, groups, step):
        every = range(first, first + step)
        keys = {g: jnp.concatenate([part(prev, g), part(own_ref, g)], axis=0) for g in every}
        values = {g: jnp.concatenate([part(prev, groups + g), part(own_ref, groups + g)], axis=0) for g in every}
        out_t = {g: jnp.concatenate([self_0_ref[g], self_1_ref[g]], axis=1) for g in every}
        scores = {g: dot(keys[g], out_t[g], NN) for g in every}
        plain, cross_rows, grad_weights = {}, {}, {}
        for g in every:
            tiles = [stack(grad_ref, block * WINDOW, WINDOW, g, repeat) for block in blocks]
            plain[g] = dot(values[g], jnp.concatenate(tiles, axis=0), NT)
            cross_rows[g] = cross_rows_ref[g]
            grad_weights[g] = dot(values[g], cross_rows[g], NT)
        weights = {g: softmax_rows(pick(scores[g]) * SCALE) for g in every}
        score_terms = {}
        for g in every:
            gate_row = jnp.sum(weights[g].astype(jnp.bfloat16).astype(jnp.float32) * pick(plain[g]), axis=0, keepdims=True)
            gate_row = jnp.where(has_lane, gate_row, 0.0)
            gate_row = gate_row[:, :half] + gate_row[:, half:]
            gate_rows.extend(gate_row[:, i * LANES : (i + 1) * LANES] for i in range(half // LANES))
            weight_terms = pick(grad_weights[g])
            delta = jnp.sum(weights[g] * weight_terms, axis=0, keepdims=True)
            score_terms[g] = join(weights[g] * (weight_terms - delta))
            scores_ref[g] = score_terms[g]
        for g in every:
            grad_key = dot(score_terms[g], out_t[g], NT) * SCALE
            grad_value = dot(join(weights[g]), cross_rows[g], NN)
            for index, terms in ((g, grad_key), (groups + g, grad_value)):
                cols = slice(index * HEAD_DIM, (index + 1) * HEAD_DIM)
                own_terms_ref[:, cols] = terms[img:]
                to_pair_ref[:, cols] = terms[:img] * from_z
                to_x_ref[:, cols] = (terms[:img] * from_x).astype(to_x_ref.dtype)
                in_chip_ref[:, cols] = terms[:img] * from_chip
    gate = jnp.concatenate(gate_rows, axis=0)
    to_pair_ref[:, width:] = jnp.concatenate([gate] * (img // gate.shape[0]), axis=0)
    to_x_ref[:, width:] = jnp.concatenate([split(gate)] * (to_x_ref.shape[1] // LANES - width // LANES), axis=1)
    row = lax.broadcasted_iota(jnp.int32, mask_ref.shape, 0)
    mask_ref[...] = jnp.where(row == 0, by_mine.astype(jnp.float32) * (1.0 - from_x), from_x)


def cross_query_kernel(scores_ref, grad_ref, own_ref, prev, _, grad_self_ref, *, groups, repeat):
    for g in range(groups):
        keys = jnp.concatenate([part(prev, g), part(own_ref, g)], axis=0)
        grad_query = dot(scores_ref[g], keys, TN) * SCALE
        for block in range(grad_ref.shape[0] // WINDOW):
            rows = slice(block * repeat * WINDOW, (block + 1) * repeat * WINDOW)
            grad_rows = stack(grad_ref, block * WINDOW, WINDOW, g, repeat).astype(jnp.float32)
            grad_self_ref[g, rows, :] = (grad_rows + grad_query[rows]).astype(jnp.bfloat16)


def outside_kernel(mine_ref, pair_ref, mask_ref, _, to_z_ref, gate_ref):
    width = mine_ref.shape[1] - LANES
    total = mine_ref[...] + pair_ref[...]
    gate = total[: gate_ref.shape[0], width:]
    to_z_ref[:, :width] = (total[:, :width] * mask_ref[0:1, 0:1]).astype(to_z_ref.dtype)
    to_z_ref[:, width:] = split(gate)
    gate_ref[...] = gate


def chip_sum_kernel(mine_ref, x_ref, z_ref, gate_ref, *refs):
    *gates, _, out_ref, gate_out, to_pair_ref = refs
    width = mine_ref.shape[1]
    terms = mine_ref[...] + (x_ref[:, :width].astype(jnp.float32) + z_ref[:, :width].astype(jnp.float32))
    out_ref[...] = terms
    to_pair_ref[:, :width] = terms.astype(to_pair_ref.dtype)
    gate = unsplit(z_ref[:, width:]) + unsplit(x_ref[:, width : width + LANES])
    for ref in gates:
        gate = gate + ref[...]
    gate_out[...] = gate_ref[...] + gate
    to_pair_ref[:, width:] = split(gate)


def self_back_kernel(
    query_ref, context_ref, halo_ref, weights_ref, grad_ref, *refs, block, groups, repeat
):
    query_grad_ref, key_low_ref, key_high_ref, rows_out, sems = refs[-5:]
    half = repeat * WINDOW
    every = range(groups)
    rows = [stack(query_ref, block * WINDOW, WINDOW, g, repeat) for g in every]
    keys = [joined(context_ref, halo_ref, block, g) for g in every]
    grads = [grad_ref[g, block * half : (block + 1) * half, :] for g in every]
    grad_weights = [dot(joined(context_ref, halo_ref, block, groups + g), grads[g], NT) for g in every]
    grad_scores = []
    for g in every:
        delta = jnp.sum(weights_ref[g] * grad_weights[g], axis=0, keepdims=True)
        grad_scores.append((weights_ref[g] * (grad_weights[g] - delta)).astype(jnp.bfloat16))
    copies = []
    for g in every:
        grad_query = (dot(grad_scores[g], keys[g], TN) * SCALE).astype(jnp.bfloat16)
        for h in range(repeat):
            head = g * repeat + h
            rows_out[:, head * HEAD_DIM : (head + 1) * HEAD_DIM] = grad_query[h * WINDOW : (h + 1) * WINDOW]
        cols = slice(g * repeat * HEAD_DIM, (g + 1) * repeat * HEAD_DIM)
        copies.append(
            pltpu.make_async_copy(
                rows_out.at[:, cols], query_grad_ref.at[block * WINDOW : (block + 1) * WINDOW, cols], sems.at[g]
            )
        )
        copies[-1].start()
    for g in every:
        grad_key = dot(grad_scores[g], rows[g], NN) * SCALE
        grad_value = dot(weights_ref[g].astype(jnp.bfloat16), grads[g], NN)
        for index, terms in ((g, grad_key), (groups + g, grad_value)):
            cols = slice(index * HEAD_DIM, (index + 1) * HEAD_DIM)
            key_low_ref[key_low_ref.shape[0] - WINDOW :, cols] = terms[:WINDOW].astype(key_low_ref.dtype)
            key_high_ref[:, cols] = terms[WINDOW:]
    for copy in copies:
        copy.wait()


def gate_kernel(mine_ref, pair_ref, out_ref):
    out_ref[...] = mine_ref[...] + unsplit(pair_ref[:, pair_ref.shape[1] - LANES :])


def gate_grad(total, gate_ref):
    rows, heads = total.shape[0], gate_ref.shape[0]
    lane = lax.broadcasted_iota(jnp.int32, total.shape, 1)
    first = jnp.sum(jnp.where(lane < WINDOW, total, 0.0), axis=1, keepdims=True)
    second = jnp.sum(jnp.where(lane < WINDOW, 0.0, total), axis=1, keepdims=True)
    row = lax.broadcasted_iota(jnp.int32, (rows, heads), 0)
    head = lax.broadcasted_iota(jnp.int32, (rows, heads), 1)
    sums = jnp.where(head == 2 * row, first, 0.0) + jnp.where(head == 2 * row + 1, second, 0.0)
    sums = jnp.sum(sums, axis=0, keepdims=True)
    tanh = gate_ref[:, :heads]
    same = lax.broadcasted_iota(jnp.int32, tanh.shape, 0) == lax.broadcasted_iota(jnp.int32, tanh.shape, 1)
    tanh = jnp.sum(jnp.where(same, tanh, 0.0), axis=0, keepdims=True)
    return (1.0 - tanh * tanh) * sums


def finish_kernel(
    owner_ref, own_ref, mine_ref, pair_ref, low_ref, also_ref, high_ref, halo_ref, gate_ref, *refs, tok_rows
):
    *far_refs, tanh_ref, memory_ref, context_ref, gate_out = refs
    width = mine_ref.shape[1]
    keep = owner(owner_ref, 0).astype(jnp.float32)
    total = own_ref[...] + (mine_ref[...] + pair_ref[:, :width].astype(jnp.float32))
    memory_ref[...] = (total * keep).astype(memory_ref.dtype)
    more = jnp.where(lax.axis_index("seq") < lax.axis_size("seq") - 1, 1.0, 0.0)
    first = tok_rows - WINDOW
    context_ref[:first] = (low_ref[...] + also_ref[...]).astype(context_ref.dtype)
    context_ref[first:] = (high_ref[...] + halo_ref[...].astype(jnp.float32) * more).astype(context_ref.dtype)
    gate = gate_ref[...]
    for ref in far_refs:
        gate = gate + ref[...]
    gate_out[...] = gate_grad(gate, tanh_ref)


def struct(shape, dtype):
    return jax.ShapeDtypeStruct(shape, dtype)


def call(
    name, kernel, out_shape, in_specs, scratch=(), out_specs=None, aliases=None, flops=1000, moved=1000
):
    return pl.pallas_call(
        kernel,
        out_shape=out_shape,
        in_specs=in_specs,
        out_specs=[VMEM] * len(out_shape) if out_specs is None else out_specs,
        scratch_shapes=scratch,
        input_output_aliases=aliases or {},
        compiler_params=pltpu.CompilerParams(vmem_limit_bytes=40 * 2**20),
        cost_estimate=pl.CostEstimate(flops=flops, bytes_accessed=moved, transcendentals=0),
        name=name,
    )


def on_device(queries, context, segment_start, memory, image_offset, cross_gate, out_grad):
    tok_rows, model = queries.shape[1:]
    width = context.shape[2]
    groups = width // 2 // HEAD_DIM
    heads = cross_gate.shape[0]
    repeat = heads // groups
    img = memory.shape[2]
    half = repeat * WINDOW
    seq, dp = lax.axis_size("seq"), lax.axis_size("dp")
    f32, bf16 = jnp.float32, jnp.bfloat16

    swaps = seq == 4 * GAP and dp == 2

    def send(value, where):
        return lax.ppermute(value, "seq", [(i, where(i)) for i in range(seq)])

    def send_all(value, where):
        pairs = [(s, d, *where(s, d)) for s in range(seq) for d in range(dp)]
        return lax.ppermute(value, ("seq", "dp"), [(s * dp + d, t * dp + e) for s, d, t, e in pairs])

    def send_near(value, step):
        if not swaps:
            return (send(value, lambda i: (i + step) % seq),)
        off_chip = lambda s, d: (s, d ^ 1) if s in (0, seq - 1) else (((s + 1) ^ 1) - 1, d)
        return send(value, lambda i: i ^ 1), send_all(value, off_chip)

    def merge(name, arrived, step, after):
        if len(arrived) == 1:
            return arrived[0][arrived[0].shape[0] - WINDOW :]
        return call(name, functools.partial(near_kernel, step=step), [window], [VMEM] * 2 + [ANY])(*arrived, after)[0]

    def send_z(value, step, straight=False):
        def where(i):
            wraps = not 0 <= i + step * GAP < seq
            return ((i if i % 2 == 0 or (straight and wraps) else i ^ 2) + step * GAP) % seq

        return send(value, where)

    q, ctx, grad = queries[0], context[0], out_grad[0]
    gate_tanh = jnp.tanh(cross_gate)
    gate_rows = jnp.broadcast_to(gate_tanh[:, None], (heads, LANES))
    image = struct((img, width), bf16)
    window = struct((WINDOW, width), bf16)
    own = memory[0, 0]
    is_owner = (image_offset < tok_rows).astype(bf16)
    own = jnp.concatenate([own, jnp.broadcast_to(is_owner, (img, MARKS))], axis=1)
    pair = send(own, lambda i: i ^ 1)
    tail = ctx[tok_rows - WINDOW - MORE :]
    halos = send_near(tail, 1)
    chip, marked, chip_half, owners = call(
        "chip_image",
        chip_kernel,
        [image, struct((img, width + LANES), bf16), struct((img, width // 2), bf16), struct((8, LANES), f32)],
        [VMEM] * 2,
    )(own, pair)
    off = jnp.broadcast_to(image_offset, (8, LANES))
    by_z = send_z(marked, 1, True)
    by_x = send(chip_half, lambda i: i ^ 2)
    self_out, kept = [None, None], [None, None]

    def self_forward(block, after):
        self_out[block], kept[block] = call(
            f"self_forward_{block}",
            functools.partial(self_kernel, block=block, groups=groups, repeat=repeat),
            [struct((groups, HEAD_DIM, half), bf16), struct((groups, 2 * WINDOW, half), f32)],
            [VMEM] * 4 + [ANY],
            flops=10**6,
            moved=10**5,
        )(q, ctx, tail if block else halo, segment_start, after)

    self_forward(1, chip)
    halo = merge("halo", halos, 1, self_out[1])
    cross_rows = call(
        "cross_rows",
        functools.partial(scale_kernel, groups=groups, repeat=repeat),
        [struct((groups, repeat * tok_rows, HEAD_DIM), bf16)],
        [VMEM] * 4 + [ANY],
    )(off, owners, gate_rows, grad, self_out[1])[0]
    arrived = call("arrived", join_kernel, [struct((img, width + LANES + width // 2), bf16)], [VMEM] * 2 + [ANY] * 2)(
        by_z, by_x, cross_rows, halo
    )[0]

    by_pair = send(arrived, lambda i: i ^ 1)
    self_forward(0, arrived)

    gate_shape = struct((heads * WINDOW // LANES, LANES), f32)
    scores, to_pair, to_x, in_chip, own_terms, masks, prev = call(
        "cross",
        functools.partial(cross_kernel, groups=groups, repeat=repeat),
        [
            struct((groups, 2 * img, repeat * tok_rows), bf16),
            struct((img, width + LANES), f32),
            struct((img, width + WIDE * LANES), bf16),
            struct((img, width), f32),
            struct((img, width), f32),
            struct((8, LANES), f32),
            image,
        ],
        [VMEM] * 10,
    )(off, owners, cross_rows, *self_out, grad, own, chip, arrived, by_pair)
    from_pair = send(to_pair, lambda i: i ^ 1)
    from_x = send(to_x, lambda i: i ^ 2)
    grad_self = call(
        "cross_query",
        functools.partial(cross_query_kernel, groups=groups, repeat=repeat),
        [struct((groups, repeat * tok_rows, HEAD_DIM), bf16)],
        [VMEM] * 4 + [ANY],
    )(scores, grad, own, prev, to_pair)[0]

    def self_backward(block, after, late=None):
        return call(
            f"self_backward_{block}",
            functools.partial(self_back_kernel, block=block, groups=groups, repeat=repeat),
            [
                struct((tok_rows, model), bf16),
                struct((WINDOW, width), f32) if block else struct((WINDOW + MORE, width), bf16),
                struct((WINDOW, width), f32),
            ],
            [VMEM] * 5 + [ANY] * (1 if late is None else 2),
            scratch=[pltpu.VMEM((WINDOW, model), bf16), pltpu.SemaphoreType.DMA((groups,))],
            out_specs=[ANY, VMEM, VMEM],
            aliases={5: 0} if block else None,
            flops=10**6,
            moved=10**5,
        )(q, ctx, tail if block else halo, kept[block], grad_self, after, *([] if late is None else [late]))

    to_z, gate = call(
        "outside",
        outside_kernel,
        [struct((img, width + LANES), bf16), gate_shape],
        [VMEM] * 3 + [ANY],
    )(to_pair, from_pair, masks, grad_self)
    from_z = send_z(to_z, -1)
    gates = []
    if swaps:
        gates = [send_z(gate, 1), send_z(gate, 2)]
    query_grad, halo_terms, low = self_backward(0, to_z)
    mine, gate, to_chip = call(
        "chip_sum",
        chip_sum_kernel,
        [struct((img, width), f32), gate_shape, struct((img, width + LANES), bf16)],
        [VMEM] * (4 + len(gates)) + [ANY],
    )(in_chip, from_x, from_z, gate, *gates, low)
    other = send(to_chip, lambda i: i ^ 1)
    halo_back = send_near(halo_terms, -1)
    query_grad, also, high = self_backward(1, query_grad, mine)
    halo_back = merge("halo_back", halo_back, -1, high)
    gate = call("gate_sum", gate_kernel, [gate_shape], [VMEM] * 2)(gate, other)[0]
    if swaps:
        far = [send_all(gate, lambda s, d: (s, d ^ 1))]
    else:
        gate = lax.psum(to_pair[: gate_shape.shape[0], width:], ("seq", "dp"))
        far = []
    memory_grad, context_grad, cross_gate_grad = call(
        "finish",
        functools.partial(finish_kernel, tok_rows=tok_rows),
        [image, struct((tok_rows, width), bf16), struct((1, heads), f32)],
        [VMEM] * (10 + len(far)),
    )(owners, own_terms, mine, other, low, also, high, halo_back, gate, *far, gate_rows)
    return (query_grad[None], context_grad[None], memory_grad[None, None], cross_gate_grad.reshape(heads))


def solution(mesh):
    placed = (
        P("dp", "seq", None),
        P("dp", "seq", None),
        P("dp", "seq"),
        P("dp", "seq", None, None),
        P("dp", "seq"),
        P(),
        P("dp", "seq", None),
    )
    return jax.shard_map(
        on_device,
        mesh=mesh,
        in_specs=placed,
        out_specs=(P("dp", "seq", None), P("dp", "seq", None), P("dp", "seq", None, None), P()),
        check_vma=False,
    )
```
